32 devices in a mesh: row: 4 (over z), col: 8 (over y, x, core).
Axes of the slice: x: 2, y: 2, z: 4, core: 2. Of those that a mesh axis runs over, the one named last changes fastest.
Arguments:
- three_index: float32 [32, 512, 1024], P('col', None, 'row'), may hold values from -1.2 to 1.2
- occ_energy: float32 [32], replicated, may hold values from -2 to -0.5
- vir_energy: float32 [512], replicated, may hold values from 0.5 to 3
- block_mask: int32 [32, 8, 16], replicated, may hold values from 0 to 1, as said below
- pair_list: int32 [32, 4], P('col'), may hold values from -1 to 3, as said below
Outputs:
- response_density: float32 [32, 512, 1024], P('col', None, 'row')
- virtual_density: float32 [512, 512], replicated
The draws below stay inside these ranges and needn't reach their ends.
Inputs may be any that keep to these rules, and one draw needn't show every extreme that they name: `block_mask`: each orbital keeps between 32 and 64 of its 128 blocks; some orbital keeps exactly 64. `pair_list`: in each row the live entries come first and are distinct, then -1; every orbital lists at least one partner class; some orbital lists 4.
All inputs are finite; a program needn't handle non-finite values.
Results may differ from the reference program's by a relative error of at most 0.0003.
Values sent between devices are 32-bit elements; how exact they have to be, the bound alone decides.
No kernel may reach another device: no remote copies, remote signals or barrier semaphores. Data moves between devices by JAX's collectives and lax.ppermute only.
A program may use at most 128 MiB of HBM per device.

```python
import jax
import jax.numpy as jnp
from jax import lax

NVIR = 512
NAUX = 1024
BLOCK = 64
PAIRS_DEV = 4
NOCC = 32
GROUP_ROWS = 4
NPANEL = 4
NVB = 8
NAB = 16
NBLK = 128
NNZ = 64


def shuffled_rows(base_key, count_rows, width):
    row_keys = jax.random.split(base_key, count_rows)

    def shuffle_one(row_key):
        return jax.random.permutation(row_key, width)
    return jax.vmap(shuffle_one)(row_keys)


def draw_block_mask(key, part):
    count_key = jax.random.fold_in(key, 11)
    order_key = jax.random.fold_in(key, 12)
    chosen_key = jax.random.fold_in(key, 13)
    counts = jax.random.randint(count_key, (NOCC,), NNZ // 2, NNZ + 1)
    chosen = jax.random.randint(chosen_key, (), 0, NOCC)
    counts = jnp.where(jnp.arange(NOCC) == chosen, NNZ, counts)
    shuffled = shuffled_rows(order_key, NOCC, NBLK)
    ranks = jnp.argsort(shuffled, axis=1)
    kept = (ranks < counts[:, None]).astype(jnp.int32)
    return kept.reshape(NOCC, NVB, NAB)


def draw_pair_list(key, part):
    count_key = jax.random.fold_in(key, 21)
    order_key = jax.random.fold_in(key, 22)
    chosen_key = jax.random.fold_in(key, 23)
    counts = jax.random.randint(count_key, (NOCC,), 1, PAIRS_DEV + 1)
    chosen = jax.random.randint(chosen_key, (), 0, NOCC)
    counts = jnp.where(jnp.arange(NOCC) == chosen, PAIRS_DEV, counts)
    shuffled = shuffled_rows(order_key, NOCC, NPANEL)[:, :PAIRS_DEV]
    slots = jnp.arange(PAIRS_DEV)[None, :]
    return jnp.where(slots < counts[:, None], shuffled, -1).astype(jnp.int32)


def steps_of(key, extent, cuts, low, largest):
    gain, own = 1.0, jax.random.fold_in(key, 6)
    for position, blocks in cuts:
        heights = jnp.exp(jax.random.uniform(jax.random.fold_in(own, position), (blocks,), jnp.float32, low / len(cuts), largest / len(cuts)))
        gain = gain * jnp.repeat(heights, extent[position] // blocks).reshape([-1 if axis == position else 1 for axis in range(len(extent))])
    return gain


def scatter_about(rng, extent, scale, bound, shards=(), kind=jnp.bfloat16):
    drawn = jax.random.normal(rng, extent, jnp.float32) * scale
    if len(shards) > 0:
        drawn = steps_of(rng, extent, shards, -0.22, 0.18) * drawn
    return jnp.clip(drawn, min=-bound, max=bound).astype(kind)


def setup_inputs(seed: int = 0) -> dict:
    key_list = jax.random.split(jax.random.key(seed), 6)
    three_index = scatter_about(key_list[0], (NOCC, NVIR, NAUX), 0.15, 1.2, ((0, 8), (2, 4)), jnp.float32)
    occ_energy = jnp.clip(jax.random.uniform(key_list[1], (NOCC,), jnp.float32, -2.0, -0.5), -2.0, -0.5)
    vir_energy = jnp.clip(jax.random.uniform(key_list[2], (NVIR,), jnp.float32, 0.5, 3.0), 0.5, 3.0)
    block_mask = draw_block_mask(jax.random.fold_in(key_list[5], 71), 0)
    pair_list = draw_pair_list(jax.random.fold_in(key_list[5], 71), 0)
    return {"three_index": three_index, "occ_energy": occ_energy, "vir_energy": vir_energy, "block_mask": block_mask, "pair_list": pair_list}


def expand_mask(block_rows):
    widened = jnp.repeat(block_rows.astype(jnp.float32), BLOCK, axis=-2)
    return jnp.repeat(widened, BLOCK, axis=-1)


def pair_terms(own_rows, partner, energy_own, energy_partner, virtual):
    cross_term = lax.dot_general(own_rows, partner, (((1,), (1,)), ((), ())), precision=lax.Precision.HIGHEST, preferred_element_type=jnp.float32)
    denominator = energy_own + energy_partner - virtual[:, None] - virtual[None, :]
    amplitude = cross_term / denominator
    weighted = 2.0 * amplitude - amplitude.T
    response = jnp.dot(weighted, partner, precision=lax.Precision.HIGHEST, preferred_element_type=jnp.float32)
    virt_density = lax.dot_general(weighted, amplitude, (((1,), (1,)), ((), ())), precision=lax.Precision.HIGHEST, preferred_element_type=jnp.float32)
    return response, virt_density


def reference(three_index, occ_energy, vir_energy, block_mask, pair_list):
    masked = three_index * expand_mask(block_mask)

    def one_orbital(density_sum, orbital):
        own_rows = masked[orbital]
        residue = orbital % GROUP_ROWS
        response_sum = jnp.zeros((NVIR, NAUX), jnp.float32)
        for slot_index in range(PAIRS_DEV):
            listed = pair_list[orbital, slot_index]
            live = (listed >= 0).astype(jnp.float32)
            partner_orbital = (jnp.maximum(listed, 0) * GROUP_ROWS + residue).astype(jnp.int32)
            response, virt_density = pair_terms(own_rows, masked[partner_orbital], occ_energy[orbital], occ_energy[partner_orbital], vir_energy)
            response_sum = response_sum + live * response
            density_sum = density_sum + live * virt_density
        return density_sum, response_sum

    density_sum, responses = lax.scan(one_orbital, jnp.zeros((NVIR, NVIR), jnp.float32), jnp.arange(NOCC, dtype=jnp.int32))
    return responses, density_sum / NOCC
```

```python
import functools

import jax
import jax.numpy as jnp
from jax import lax
from jax.experimental import pallas as pl
from jax.experimental.pallas import tpu as pltpu
from jax.sharding import PartitionSpec as P

BLOCK = 64
LANES = 128
NPANEL = 4
SLOTS = 64
CHUNKS = 2
VMEM_LIMIT = 48 * 1024 * 1024
SMEM = pl.BlockSpec(memory_space=pltpu.SMEM)
VMEM = pl.BlockSpec(memory_space=pltpu.VMEM)
NT = (((1,), (1,)), ((), ()))


def params():
    return pltpu.CompilerParams(vmem_limit_bytes=VMEM_LIMIT)


def cost(flops, size):
    return pl.CostEstimate(flops=flops, bytes_accessed=size, transcendentals=0)


def halves(value):
    high = value.astype(jnp.bfloat16)
    return high, (value - high.astype(jnp.float32)).astype(jnp.bfloat16)


def pack_kernel(naux_blocks, listed, own, *outs):
    width = own.shape[2]
    tiles = width // LANES
    per = outs[0].shape[0]
    lane = lax.broadcasted_iota(jnp.int32, (BLOCK, LANES), 1)

    def block(slot, half):
        index = listed[slot]
        vir = index // naux_blocks
        aux = index % naux_blocks
        pair = aux // 2
        value = own[
            pair // tiles,
            pl.ds(pl.multiple_of(vir * BLOCK, BLOCK), BLOCK),
            pl.ds(pl.multiple_of((pair % tiles) * LANES, LANES), LANES),
        ]
        return pltpu.roll(value, ((aux % 2) ^ half) * BLOCK, 1)

    for chunk, out in enumerate(outs):

        def step(at, carry, chunk=chunk, out=out):
            slot = 2 * (chunk * per + at)
            out[at] = jnp.where(lane < BLOCK, block(slot, 0), block(slot + 1, 1))
            return carry

        lax.fori_loop(0, per, step, 0, unroll=2)


def pack(own, listed, naux_blocks):
    per = SLOTS // 2 // CHUNKS
    shape = jax.ShapeDtypeStruct((per, BLOCK, LANES), jnp.float32)
    return pl.pallas_call(
        functools.partial(pack_kernel, naux_blocks),
        out_shape=[shape] * CHUNKS,
        in_specs=[SMEM, VMEM],
        out_specs=[VMEM] * CHUNKS,
        compiler_params=params(),
        cost_estimate=cost(0, 12 * 2**20),
        name="pack",
    )(listed, own)


def split_kernel(naux_blocks, place, own, high, low):
    width = own.shape[2]
    tiles = width // LANES
    pairs = naux_blocks // 2
    lane = lax.broadcasted_iota(jnp.int32, (BLOCK, LANES), 1)

    def step(tile, carry):
        vir = tile // pairs
        pair = tile % pairs
        rows = pl.ds(pl.multiple_of(vir * BLOCK, BLOCK), BLOCK)
        value = own[
            pair // tiles, rows, pl.ds(pl.multiple_of((pair % tiles) * LANES, LANES), LANES)
        ]
        kept = jnp.where(lane < BLOCK, place[2 * tile], place[2 * tile + 1]) >= 0
        value = jnp.where(kept, value, 0.0)
        columns = pl.ds(pl.multiple_of(pair * LANES, LANES), LANES)
        high[rows, columns], low[rows, columns] = halves(value)
        return carry

    lax.fori_loop(0, high.shape[0] // BLOCK * pairs, step, 0, unroll=2)


def split(own, place, naux_blocks):
    parts, nvir, width = own.shape
    shape = jax.ShapeDtypeStruct((nvir, parts * width), jnp.bfloat16)
    return pl.pallas_call(
        functools.partial(split_kernel, naux_blocks),
        out_shape=[shape] * 2,
        in_specs=[SMEM, VMEM],
        out_specs=[VMEM] * 2,
        compiler_params=params(),
        cost_estimate=cost(0, 4 * 2**20),
        name="split",
    )(place, own)


def dot(left, right):
    return jnp.dot(left, right, preferred_element_type=jnp.float32)


def dot_nt(left, right):
    return lax.dot_general(left, right, NT, preferred_element_type=jnp.float32)


def unpack(naux_blocks, place, chunks, m_high, m_low):
    pairs = naux_blocks // 2
    per = chunks[0].shape[0]
    lane = lax.broadcasted_iota(jnp.int32, (BLOCK, LANES), 1)

    def block(packed, slot, half):
        value = packed[slot // 2]
        return pltpu.roll(value, ((slot % 2) ^ half) * BLOCK, 1)

    def step(tile, carry):
        left = place[2 * tile]
        right = place[2 * tile + 1]
        at_left = jnp.maximum(left, 0)
        at_right = jnp.maximum(right, 0)
        value = jnp.where(lane < BLOCK, block(chunks, at_left, 0), block(chunks, at_right, 1))
        kept = jnp.where(lane < BLOCK, left, right) >= 0
        value = jnp.where(kept, value, 0.0)
        rows = pl.ds(pl.multiple_of((tile // pairs) * BLOCK, BLOCK), BLOCK)
        columns = pl.ds(pl.multiple_of((tile % pairs) * LANES, LANES), LANES)
        m_high[rows, columns], m_low[rows, columns] = halves(value)
        return carry

    lax.fori_loop(0, m_high.shape[0] // BLOCK * pairs, step, 0, unroll=2)


def density_into(total, previous, w_high, w_low, a_high, a_low, scale=None):
    nvir = w_high.shape[0]
    tile = 256
    for column in range(nvir // tile):
        cols = pl.ds(column * tile, tile)
        value = dot_nt(w_high[...], a_high[cols, :])
        value += dot_nt(w_high[...], a_low[cols, :])
        value += dot_nt(w_low[...], a_high[cols, :])
        if previous is not None:
            value += previous[:, cols]
        if scale is not None:
            value *= scale
        total[:, cols] = value


def panel_kernel(naux_blocks, first, last, *refs):
    refs = list(refs)
    place, scalars, vir_col, vir_row, own_high, own_low = refs[:6]
    refs = refs[6:]
    chunks = refs[:CHUNKS]
    refs = refs[CHUNKS:]
    response_in = density_in = None
    if not first:
        response_in, density_in = refs[:2]
        refs = refs[2:]
    response = refs[0]
    refs = refs[1:]
    if last:
        a_high, a_low, w_high, w_low = refs[:4]
        refs = refs[4:]
    else:
        density = refs[0]
        refs = refs[1:]
    m_high, m_low, amp, packed = refs[:4]
    if not last:
        a_high, a_low, w_high, w_low = refs[4:]

    per = chunks[0].shape[0]
    for chunk in range(CHUNKS):
        packed[chunk * per : (chunk + 1) * per] = chunks[chunk][...]
    unpack(naux_blocks, place, packed, m_high, m_low)

    energy = scalars[0]
    live = scalars[1]
    nvir = own_high.shape[0]
    tile = 256
    count = nvir // tile
    for column in range(count):
        cols = pl.ds(column * tile, tile)
        cross = dot_nt(own_high[...], m_high[cols, :])
        cross += dot_nt(own_high[...], m_low[cols, :])
        cross += dot_nt(own_low[...], m_high[cols, :])
        denominator = energy - vir_col[...] - vir_row[:, cols]
        value = cross / denominator * live
        amp[:, cols] = value
        a_high[:, cols], a_low[:, cols] = halves(value)
    for row in range(count):
        rows = pl.ds(row * tile, tile)
        for column in range(count):
            cols = pl.ds(column * tile, tile)
            weighted = 2.0 * amp[rows, cols] - amp[cols, rows].T
            w_high[rows, cols], w_low[rows, cols] = halves(weighted)
    parts, _, width = response.shape
    for part in range(parts):
        cols = pl.ds(part * width, width)
        value = dot(w_high[...], m_high[:, cols])
        value += dot(w_high[...], m_low[:, cols])
        value += dot(w_low[...], m_high[:, cols])
        if response_in is not None:
            value += response_in[part]
        response[part] = value
    if not last:
        density_into(density, density_in, w_high, w_low, a_high, a_low)


def panel(first, last, place, scalars, virtual, own_high, own_low, chunks, sums, parts):
    nvir, naux = own_high.shape
    width = naux // parts
    response = jax.ShapeDtypeStruct((parts, nvir, width), jnp.float32)
    square = jax.ShapeDtypeStruct((nvir, nvir), jnp.float32)
    half = jax.ShapeDtypeStruct((nvir, nvir), jnp.bfloat16)
    outs = [response] + ([half] * 4 if last else [square])
    scratch = [
        pltpu.VMEM((nvir, naux), jnp.bfloat16),
        pltpu.VMEM((nvir, naux), jnp.bfloat16),
        pltpu.VMEM((nvir, nvir), jnp.float32),
        pltpu.VMEM((SLOTS // 2, BLOCK, LANES), jnp.float32),
    ]
    if not last:
        scratch += [pltpu.VMEM((nvir, nvir), jnp.bfloat16)] * 4
    operands = [place, scalars, virtual[:, None], virtual[None, :], own_high, own_low, *chunks, *sums]
    return pl.pallas_call(
        functools.partial(panel_kernel, naux // BLOCK, first, last),
        out_shape=outs,
        in_specs=[SMEM] * 2 + [VMEM] * (len(operands) - 2),
        out_specs=[VMEM] * len(outs),
        scratch_shapes=scratch,
        compiler_params=params(),
        cost_estimate=cost(3 * 2 * nvir * nvir * (2 * naux + nvir), 8 * 2**20),
        name="panel",
    )(*operands)


def density_kernel(scale, previous, w_high, w_low, a_high, a_low, total):
    density_into(total, previous, w_high, w_low, a_high, a_low, scale)


def density_last(previous, w_high, w_low, a_high, a_low, scale):
    nvir = previous.shape[0]
    return pl.pallas_call(
        functools.partial(density_kernel, scale),
        out_shape=jax.ShapeDtypeStruct((nvir, nvir), jnp.float32),
        in_specs=[VMEM] * 5,
        out_specs=VMEM,
        compiler_params=params(),
        cost_estimate=cost(3 * 2 * nvir**3, 4 * 2**20),
        name="density",
    )(previous, w_high, w_low, a_high, a_low)


def exchange(value, axis, bit):
    size = lax.axis_size(axis)
    return lax.ppermute(value, axis, [(at, at ^ bit) for at in range(size)])


def sum_everywhere(value):
    steps = []
    for axis in ("col", "row"):
        bit = 1
        while bit < lax.axis_size(axis):
            steps.append((axis, bit))
            bit *= 2
    sides = []
    for axis, bit in steps:
        half = value.shape[0] // 2
        side = (lax.axis_index(axis) // bit) % 2
        kept = lax.dynamic_slice_in_dim(value, side * half, half, 0)
        sent = lax.dynamic_slice_in_dim(value, (1 - side) * half, half, 0)
        value = kept + exchange(sent, axis, bit)
        sides.append(side)
    for (axis, bit), side in zip(reversed(steps), reversed(sides)):
        other = exchange(value, axis, bit)
        value = jnp.where(
            side == 0, jnp.concatenate([value, other]), jnp.concatenate([other, value])
        )
    return value


def on_device(three_index, occ_energy, vir_energy, block_mask, pair_list):
    row = lax.axis_index("row")
    col = lax.axis_index("col")
    row_count = lax.axis_size("row")
    col_count = lax.axis_size("col")
    position = col % NPANEL
    group = col // NPANEL
    groups = col_count // NPANEL
    own_orbital = col * row_count + row
    naux_blocks = block_mask.shape[2]
    blocks = block_mask.shape[1] * naux_blocks

    panels = [position ^ turn for turn in range(NPANEL)]
    orbitals = jnp.stack([own_orbital] + [at * row_count + row for at in panels])
    masks = block_mask.reshape(-1, blocks)[orbitals]
    order = jnp.arange(blocks)
    counts = jnp.sum(
        jnp.where(order[None, :] <= order[:, None], masks[:, None, :], 0), axis=2
    )
    place = jnp.where(masks > 0, counts - 1, -1)
    listed = jnp.sum(
        (counts[0][None, :] <= jnp.arange(SLOTS)[:, None]).astype(jnp.int32), axis=1
    )
    listed = jnp.minimum(listed, blocks - 1)
    lists = pair_list[row]

    own = lax.all_to_all(three_index, "row", split_axis=0, concat_axis=0, tiled=True)
    packed = pack(own, listed, naux_blocks)
    own_high, own_low = split(own, place[0], naux_blocks)

    near = list(packed)
    reach = 1
    while reach < groups:
        links = [
            (at, at + reach * NPANEL)
            for at in range(min(reach, groups - reach) * NPANEL)
        ]
        new = (group >= reach) & (group < 2 * reach)
        for chunk in range(CHUNKS):
            got = lax.ppermute(near[chunk], "col", links)
            near[chunk] = jnp.where(new, got, near[chunk])
        reach *= 2
    far = [exchange(chunk, "col", 2) for chunk in near]
    near_twin = [exchange(chunk, "col", 1) for chunk in near]
    far_twin = [exchange(chunk, "col", 1) for chunk in far]

    sums = []
    arrived = [near, near_twin, far, far_twin]
    for turn in range(NPANEL):
        partner = orbitals[1 + turn]
        live = jnp.any(lists == panels[turn]).astype(jnp.float32)
        scalars = jnp.stack([occ_energy[own_orbital] + occ_energy[partner], live])
        sums = panel(
            turn == 0,
            turn == NPANEL - 1,
            place[1 + turn],
            scalars,
            vir_energy,
            own_high,
            own_low,
            arrived[turn],
            sums,
            row_count,
        )
        if turn == NPANEL - 2:
            density = sums[1]
    response, a_high, a_low, w_high, w_low = sums
    returned = lax.all_to_all(response, "row", split_axis=0, concat_axis=0, tiled=True)
    scale = 1.0 / (row_count * col_count)
    density = density_last(density, w_high, w_low, a_high, a_low, scale)
    return returned, sum_everywhere(density)


def solution(mesh):
    placed = (P("col", None, "row"), P(), P(), P(), P("col", None))
    return jax.shard_map(
        on_device,
        mesh=mesh,
        in_specs=placed,
        out_specs=(P("col", None, "row"), P()),
        check_vma=False,
    )
```

```python
import functools

import jax
import jax.numpy as jnp
from jax import lax
from jax.experimental import pallas as pl
from jax.experimental.pallas import tpu as pltpu
from jax.sharding import PartitionSpec as P

BLOCK = 64
NPANEL = 4
CHUNKS = 4
TILE = 256
VMEM_LIMIT = 48 * 1024 * 1024
SMEM = pl.BlockSpec(memory_space=pltpu.SMEM)
VMEM = pl.BlockSpec(memory_space=pltpu.VMEM)
NT = (((1,), (1,)), ((), ()))


def call(kernel, name, outs, operands, flops, scratch=(), scalars=0):
    size = sum(at.size * at.dtype.itemsize for at in [*outs, *operands])
    return pl.pallas_call(
        kernel,
        out_shape=outs,
        in_specs=[SMEM] * scalars + [VMEM] * (len(operands) - scalars),
        out_specs=[VMEM] * len(outs),
        scratch_shapes=list(scratch),
        compiler_params=pltpu.CompilerParams(vmem_limit_bytes=VMEM_LIMIT),
        cost_estimate=pl.CostEstimate(flops=flops, bytes_accessed=size, transcendentals=0),
        name=name,
    )(*operands)


def shape(*sizes, kind=jnp.float32):
    return jax.ShapeDtypeStruct(sizes, kind)


def halves(value):
    high = value.astype(jnp.bfloat16)
    return high, (value - high.astype(jnp.float32)).astype(jnp.bfloat16)


def dot(left, right):
    return jnp.dot(left, right, preferred_element_type=jnp.float32)


def dot_nt(left, right):
    return lax.dot_general(left, right, NT, preferred_element_type=jnp.float32)


def split_rows(chunks, mask, high, low):
    for chunk, rows in enumerate(chunks):
        parts, count, width = rows.shape
        for start in range(0, count, BLOCK):
            at = chunk * count + start
            for part in range(parts):
                cols = slice(part * width, (part + 1) * width)
                kept = mask[at // BLOCK : at // BLOCK + 1, cols]
                value = rows[part, start : start + BLOCK, :] * kept
                high[at : at + BLOCK, cols], low[at : at + BLOCK, cols] = halves(value)


def amplitudes(energy, live, vir_col, vir_row, own, panel, amp, a_parts, w_parts):
    nvir = amp.shape[0]
    for start in range(0, nvir, TILE):
        cols = slice(start, start + TILE)
        cross = dot_nt(own[0][...], panel[0][cols, :])
        cross += dot_nt(own[0][...], panel[1][cols, :])
        cross += dot_nt(own[1][...], panel[0][cols, :])
        value = cross / (energy - vir_col[...] - vir_row[:, cols]) * live
        amp[:, cols] = value
        a_parts[0][:, cols], a_parts[1][:, cols] = halves(value)
    for above in range(0, nvir, TILE):
        rows = slice(above, above + TILE)
        for start in range(0, nvir, TILE):
            cols = slice(start, start + TILE)
            value = 2.0 * amp[rows, cols] - amp[cols, rows].T
            w_parts[0][rows, cols], w_parts[1][rows, cols] = halves(value)


def respond(rows, w_parts, panel, cols):
    value = dot(w_parts[0][rows, :], panel[0][:, cols])
    value += dot(w_parts[0][rows, :], panel[1][:, cols])
    return value + dot(w_parts[1][rows, :], panel[0][:, cols])


def density_tile(cols, w_parts, a_parts):
    value = dot_nt(w_parts[0][...], a_parts[0][cols, :])
    value += dot_nt(w_parts[0][...], a_parts[1][cols, :])
    return value + dot_nt(w_parts[1][...], a_parts[0][cols, :])


def early_kernel(scalars, vir_col, vir_row, masks, *refs):
    own, near, twin = (refs[at * CHUNKS : (at + 1) * CHUNKS] for at in range(3))
    refs = refs[3 * CHUNKS :]
    own_high, own_low, response, density = refs[:4]
    m_high, m_low, amp, a_high, a_low, w_high, w_low = refs[4:]
    split_rows(own, masks.at[0], own_high, own_low)
    nvir = amp.shape[0]
    parts, _, width = response.shape
    panel, a_parts, w_parts = (m_high, m_low), (a_high, a_low), (w_high, w_low)
    for turn, chunks in enumerate((near, twin)):
        split_rows(chunks, masks.at[1 + turn], m_high, m_low)
        amplitudes(
            scalars[2 * turn], scalars[2 * turn + 1], vir_col, vir_row,
            (own_high, own_low), panel, amp, a_parts, w_parts,
        )
        for part in range(parts):
            cols = slice(part * width, (part + 1) * width)
            value = respond(slice(0, nvir), w_parts, panel, cols)
            response[part] = value if turn == 0 else response[part] + value
        for start in range(0, nvir, TILE):
            cols = slice(start, start + TILE)
            value = density_tile(cols, w_parts, a_parts)
            density[:, cols] = value if turn == 0 else density[:, cols] + value


def early(scalars, virtual, masks, own, near, twin):
    parts, rows, width = own[0].shape
    nvir, naux = rows * CHUNKS, parts * width
    half = jnp.bfloat16
    outs = [shape(nvir, naux, kind=half)] * 2 + [shape(parts, nvir, width), shape(nvir, nvir)]
    scratch = [pltpu.VMEM((nvir, naux), half)] * 2
    scratch += [pltpu.VMEM((nvir, nvir), jnp.float32)]
    scratch += [pltpu.VMEM((nvir, nvir), half)] * 4
    operands = [scalars, virtual[:, None], virtual[None, :], masks, *own, *near, *twin]
    flops = 2 * 3 * 2 * nvir * nvir * (2 * naux + nvir)
    return call(early_kernel, "early", outs, operands, flops, scratch, 1)


def late_kernel(scalars, vir_col, vir_row, masks, own_high, own_low, *refs):
    sources = refs[:CHUNKS], refs[CHUNKS : 2 * CHUNKS]
    refs = refs[2 * CHUNKS :]
    for turn, chunks in enumerate(sources):
        m_high, m_low, a_high, a_low, w_high, w_low = refs[6 * turn : 6 * turn + 6]
        split_rows(chunks, masks.at[turn], m_high, m_low)
        amplitudes(
            scalars[2 * turn], scalars[2 * turn + 1], vir_col, vir_row,
            (own_high, own_low), (m_high, m_low), refs[12], (a_high, a_low), (w_high, w_low),
        )


def late(scalars, virtual, masks, own, far, twin):
    nvir, naux = own[0].shape
    half = jnp.bfloat16
    outs = ([shape(nvir, naux, kind=half)] * 2 + [shape(nvir, nvir, kind=half)] * 4) * 2
    operands = [scalars, virtual[:, None], virtual[None, :], masks, *own, *far, *twin]
    flops = 2 * 3 * 2 * nvir * nvir * naux
    scratch = [pltpu.VMEM((nvir, nvir), jnp.float32)]
    outs = call(late_kernel, "late", outs, operands, flops, scratch, 1)
    return outs[:6], outs[6:]


def response_kernel(first, before, *refs):
    pieces = refs[8:]
    for piece in pieces:
        parts, count, width = piece.shape
        rows = slice(first, first + count)
        for part in range(parts):
            cols = slice(part * width, (part + 1) * width)
            value = before[part, rows, :]
            for at in (0, 4):
                value += respond(rows, refs[at + 2 : at + 4], refs[at : at + 2], cols)
            piece[part] = value
        first += count


def responses(first, counts, before, panels):
    parts, nvir, width = before.shape
    outs = [shape(parts, count, width) for count in counts]
    operands = [before]
    for m_high, m_low, _, _, w_high, w_low in panels:
        operands += [m_high, m_low, w_high, w_low]
    flops = 2 * 3 * 2 * sum(counts) * nvir * parts * width
    return call(functools.partial(response_kernel, first), "response", outs, operands, flops)


def density_kernel(scale, before, *refs):
    total = refs[8]
    for start in range(0, before.shape[0], TILE):
        cols = slice(start, start + TILE)
        value = before[:, cols]
        for at in (0, 4):
            value += density_tile(cols, refs[at + 2 : at + 4], refs[at : at + 2])
        total[:, cols] = value * scale


def densities(scale, before, panels):
    nvir = before.shape[0]
    operands = [before]
    for _, _, *squares in panels:
        operands += squares
    kernel = functools.partial(density_kernel, scale)
    return call(kernel, "density", [shape(nvir, nvir)], operands, 2 * 3 * 2 * nvir**3)[0]


def exchange(value, axis, bit):
    size = lax.axis_size(axis)
    return lax.ppermute(value, axis, [(at, at ^ bit) for at in range(size)])


def swap_parts(value):
    return lax.all_to_all(value, "row", split_axis=0, concat_axis=0, tiled=True)


def bits(axis):
    size = lax.axis_size(axis)
    return [1 << at for at in range(size.bit_length() - 1)]


def scatter_plane(value):
    for bit in bits("col"):
        half = value.shape[0] // 2
        side = (lax.axis_index("col") // bit) % 2
        kept = lax.dynamic_slice_in_dim(value, side * half, half, 0)
        sent = lax.dynamic_slice_in_dim(value, (1 - side) * half, half, 0)
        value = kept + exchange(sent, "col", bit)
    return value


def sum_row(value):
    terms = [value] + [exchange(value, "row", bit) for bit in range(1, lax.axis_size("row"))]
    while len(terms) > 1:
        terms = [terms[at] + terms[at + 1] for at in range(0, len(terms), 2)]
    return terms[0]


def gather_plane(value):
    for bit in reversed(bits("col")):
        side = (lax.axis_index("col") // bit) % 2
        other = exchange(value, "col", bit)
        value = jnp.where(
            side == 0, jnp.concatenate([value, other]), jnp.concatenate([other, value])
        )
    return value


def on_device(three_index, occ_energy, vir_energy, block_mask, pair_list):
    row = lax.axis_index("row")
    col = lax.axis_index("col")
    row_count = lax.axis_size("row")
    col_count = lax.axis_size("col")
    position = col % NPANEL
    group = col // NPANEL
    groups = col_count // NPANEL
    nvir = three_index.shape[1]
    step = nvir // CHUNKS

    own, near, far, near_twin, far_twin = [], [], [], [], []
    for chunk in range(CHUNKS):
        rows = swap_parts(three_index[:, chunk * step : (chunk + 1) * step, :])
        own.append(rows)
        reach = 1
        while reach < groups:
            count = min(reach, groups - reach) * NPANEL
            links = [(at, at + reach * NPANEL) for at in range(count)]
            got = lax.ppermute(rows, "col", links)
            rows = jnp.where((group >= reach) & (group < 2 * reach), got, rows)
            reach *= 2
        near.append(rows)
        far.append(exchange(rows, "col", 2))
        near_twin.append(exchange(rows, "col", 1))
        far_twin.append(exchange(far[-1], "col", 1))

    own_orbital = col * row_count + row
    panels = [position ^ turn for turn in range(NPANEL)]
    orbitals = jnp.stack([own_orbital] + [at * row_count + row for at in panels])
    masks = jnp.repeat(block_mask[orbitals].astype(jnp.float32), BLOCK, axis=-1)
    lists = pair_list[row]
    scalars = []
    for turn in range(NPANEL):
        live = jnp.any(lists == panels[turn]).astype(jnp.float32)
        scalars += [occ_energy[own_orbital] + occ_energy[orbitals[1 + turn]], live]
    first, second = jnp.stack(scalars[:4]), jnp.stack(scalars[4:])

    own_high, own_low, response, density = early(
        first, vir_energy, masks[:3], own, near, near_twin
    )
    last = late(second, vir_energy, masks[3:], (own_high, own_low), far, far_twin)
    half, quarter = nvir // 2, nvir // 4
    head = responses(0, [half], response, last)
    middle, tail = responses(half, [quarter, quarter], response, last)
    density = densities(1.0 / (row_count * col_count), density, last)

    returned = [swap_parts(head[0])]
    piece = scatter_plane(density)
    piece, middle = lax.optimization_barrier((piece, middle))
    returned.append(swap_parts(middle))
    piece = sum_row(piece)
    piece, tail = lax.optimization_barrier((piece, tail))
    returned.append(swap_parts(tail))
    return jnp.concatenate(returned, axis=1), gather_plane(piece)


def solution(mesh):
    placed = (P("col", None, "row"), P(), P(), P(), P("col", None))
    return jax.shard_map(
        on_device,
        mesh=mesh,
        in_specs=placed,
        out_specs=(P("col", None, "row"), P()),
        check_vma=False,
    )
```

```python
import functools

import jax
import jax.numpy as jnp
from jax import lax
from jax.experimental import pallas as pl
from jax.experimental.pallas import tpu as pltpu
from jax.sharding import PartitionSpec as P

BLOCK = 64
NPANEL = 4
TILE = 256
VMEM_LIMIT = 48 * 1024 * 1024
SMEM = pl.BlockSpec(memory_space=pltpu.SMEM)
VMEM = pl.BlockSpec(memory_space=pltpu.VMEM)
NT = (((1,), (1,)), ((), ()))


def call(kernel, name, outs, operands, flops, scratch=(), scalars=0):
    size = sum(at.size * at.dtype.itemsize for at in [*outs, *operands])
    return pl.pallas_call(
        kernel,
        out_shape=outs,
        in_specs=[SMEM] * scalars + [VMEM] * (len(operands) - scalars),
        out_specs=[VMEM] * len(outs),
        scratch_shapes=list(scratch),
        compiler_params=pltpu.CompilerParams(vmem_limit_bytes=VMEM_LIMIT),
        cost_estimate=pl.CostEstimate(flops=flops, bytes_accessed=size, transcendentals=0),
        name=name,
    )(*operands)


def shape(*sizes, kind=jnp.float32):
    return jax.ShapeDtypeStruct(sizes, kind)


def halves(value):
    high = value.astype(jnp.bfloat16)
    return high, (value - high.astype(jnp.float32)).astype(jnp.bfloat16)


def dot(left, right):
    return jnp.dot(left, right, preferred_element_type=jnp.float32)


def dot_nt(left, right):
    return lax.dot_general(left, right, NT, preferred_element_type=jnp.float32)


def split_rows(cuts, pieces, mask, high, low):
    for (part, first, count), piece in zip(cuts, pieces):
        width = piece.shape[1]
        cols = slice(part * width, (part + 1) * width)
        for start in range(0, count, BLOCK):
            at = first + start
            kept = mask[at // BLOCK : at // BLOCK + 1, cols]
            value = piece[start : start + BLOCK, :] * kept
            high[at : at + BLOCK, cols], low[at : at + BLOCK, cols] = halves(value)


def amplitudes(energy, live, vir_col, vir_row, own, panel, amp, a_parts, w_parts):
    nvir = amp.shape[0]
    for start in range(0, nvir, TILE):
        cols = slice(start, start + TILE)
        cross = dot_nt(own[0][...], panel[0][cols, :])
        cross += dot_nt(own[0][...], panel[1][cols, :])
        cross += dot_nt(own[1][...], panel[0][cols, :])
        value = cross / (energy - vir_col[...] - vir_row[:, cols]) * live
        amp[:, cols] = value
        a_parts[0][:, cols], a_parts[1][:, cols] = halves(value)
    for above in range(0, nvir, TILE):
        rows = slice(above, above + TILE)
        for start in range(0, nvir, TILE):
            cols = slice(start, start + TILE)
            value = 2.0 * amp[rows, cols] - amp[cols, rows].T
            w_parts[0][rows, cols], w_parts[1][rows, cols] = halves(value)


def respond(rows, w_parts, panel, cols):
    value = dot(w_parts[0][rows, :], panel[0][:, cols])
    value += dot(w_parts[0][rows, :], panel[1][:, cols])
    return value + dot(w_parts[1][rows, :], panel[0][:, cols])


def density_tile(cols, w_parts, a_parts):
    value = dot_nt(w_parts[0][...], a_parts[0][cols, :])
    value += dot_nt(w_parts[0][...], a_parts[1][cols, :])
    return value + dot_nt(w_parts[1][...], a_parts[0][cols, :])


def early_kernel(cuts, scalars, vir_col, vir_row, masks, *refs):
    count = len(cuts)
    own, near, twin = (refs[at * count : (at + 1) * count] for at in range(3))
    refs = refs[3 * count :]
    own_high, own_low, response, density = refs[:4]
    m_high, m_low, amp, a_high, a_low, w_high, w_low = refs[4:]
    split_rows(cuts, own, masks.at[0], own_high, own_low)
    nvir = amp.shape[0]
    parts, _, width = response.shape
    panel, a_parts, w_parts = (m_high, m_low), (a_high, a_low), (w_high, w_low)
    for turn, pieces in enumerate((near, twin)):
        split_rows(cuts, pieces, masks.at[1 + turn], m_high, m_low)
        amplitudes(
            scalars[2 * turn], scalars[2 * turn + 1], vir_col, vir_row,
            (own_high, own_low), panel, amp, a_parts, w_parts,
        )
        for part in range(parts):
            cols = slice(part * width, (part + 1) * width)
            value = respond(slice(0, nvir), w_parts, panel, cols)
            response[part] = value if turn == 0 else response[part] + value
        for start in range(0, nvir, TILE):
            cols = slice(start, start + TILE)
            value = density_tile(cols, w_parts, a_parts)
            density[:, cols] = value if turn == 0 else density[:, cols] + value


def early(cuts, scalars, virtual, masks, own, near, twin):
    nvir, width = own[0].shape
    naux = masks.shape[2]
    half = jnp.bfloat16
    outs = [shape(nvir, naux, kind=half)] * 2
    outs += [shape(naux // width, nvir, width), shape(nvir, nvir)]
    scratch = [pltpu.VMEM((nvir, naux), half)] * 2
    scratch += [pltpu.VMEM((nvir, nvir), jnp.float32)]
    scratch += [pltpu.VMEM((nvir, nvir), half)] * 4
    operands = [scalars, virtual[:, None], virtual[None, :], masks, *own, *near, *twin]
    flops = 2 * 3 * 2 * nvir * nvir * (2 * naux + nvir)
    kernel = functools.partial(early_kernel, cuts)
    return call(kernel, "early", outs, operands, flops, scratch, 1)


def late_kernel(cuts, scalars, vir_col, vir_row, masks, own_high, own_low, *refs):
    count = len(cuts)
    sources = refs[:count], refs[count : 2 * count]
    refs = refs[2 * count :]
    for turn, pieces in enumerate(sources):
        m_high, m_low, a_high, a_low, w_high, w_low = refs[6 * turn : 6 * turn + 6]
        split_rows(cuts, pieces, masks.at[turn], m_high, m_low)
        amplitudes(
            scalars[2 * turn], scalars[2 * turn + 1], vir_col, vir_row,
            (own_high, own_low), (m_high, m_low), refs[12], (a_high, a_low), (w_high, w_low),
        )


def late(cuts, scalars, virtual, masks, own, far, twin):
    nvir, naux = own[0].shape
    half = jnp.bfloat16
    outs = ([shape(nvir, naux, kind=half)] * 2 + [shape(nvir, nvir, kind=half)] * 4) * 2
    operands = [scalars, virtual[:, None], virtual[None, :], masks, *own, *far, *twin]
    flops = 2 * 3 * 2 * nvir * nvir * naux
    scratch = [pltpu.VMEM((nvir, nvir), jnp.float32)]
    kernel = functools.partial(late_kernel, cuts)
    outs = call(kernel, "late", outs, operands, flops, scratch, 1)
    return outs[:6], outs[6:]


def response_kernel(wanted, before, *refs):
    for (part, first, count), piece in zip(wanted, refs[8:]):
        rows = slice(first, first + count)
        width = piece.shape[1]
        cols = slice(part * width, (part + 1) * width)
        value = before[part, rows, :]
        for at in (0, 4):
            value += respond(rows, refs[at + 2 : at + 4], refs[at : at + 2], cols)
        piece[...] = value


def responses(wanted, before, panels):
    _, nvir, width = before.shape
    outs = [shape(count, width) for _, _, count in wanted]
    operands = [before]
    for m_high, m_low, _, _, w_high, w_low in panels:
        operands += [m_high, m_low, w_high, w_low]
    flops = 2 * 3 * 2 * sum(out.size for out in outs) * nvir
    return call(functools.partial(response_kernel, wanted), "response", outs, operands, flops)


def density_kernel(scale, before, *refs):
    total = refs[8]
    for start in range(0, before.shape[0], TILE):
        cols = slice(start, start + TILE)
        value = before[:, cols]
        for at in (0, 4):
            value += density_tile(cols, refs[at + 2 : at + 4], refs[at : at + 2])
        total[:, cols] = value * scale


def densities(scale, before, panels):
    nvir = before.shape[0]
    operands = [before]
    for _, _, *squares in panels:
        operands += squares
    kernel = functools.partial(density_kernel, scale)
    return call(kernel, "density", [shape(nvir, nvir)], operands, 2 * 3 * 2 * nvir**3)[0]


def exchange(value, axis, bit):
    size = lax.axis_size(axis)
    return lax.ppermute(value, axis, [(at, at ^ bit) for at in range(size)])


def after(value, *others):
    return lax.optimization_barrier((value, *others))[0]


def bits(axis):
    size = lax.axis_size(axis)
    return [1 << at for at in range(size.bit_length() - 1)]


def scatter_plane(value):
    for bit in bits("col"):
        half = value.shape[0] // 2
        side = (lax.axis_index("col") // bit) % 2
        kept = lax.dynamic_slice_in_dim(value, side * half, half, 0)
        sent = lax.dynamic_slice_in_dim(value, (1 - side) * half, half, 0)
        value = kept + exchange(sent, "col", bit)
    return value


def sum_row(value):
    for bit in bits("row"):
        value = value + exchange(value, "row", bit)
    return value


def gather_plane(value):
    for bit in reversed(bits("col")):
        side = (lax.axis_index("col") // bit) % 2
        other = exchange(value, "col", bit)
        value = jnp.where(
            side == 0, jnp.concatenate([value, other]), jnp.concatenate([other, value])
        )
    return value


def cut_list(nvir, row_count):
    cuts = [(part, 0, nvir) for part in range(row_count - 1)]
    return cuts + [(row_count - 1, at, nvir // 2) for at in (0, nvir // 2)]


def on_device(three_index, occ_energy, vir_energy, block_mask, pair_list):
    row = lax.axis_index("row")
    col = lax.axis_index("col")
    row_count = lax.axis_size("row")
    col_count = lax.axis_size("col")
    position = col % NPANEL
    group = col // NPANEL
    groups = col_count // NPANEL
    nvir = three_index.shape[1]
    cuts = cut_list(nvir, row_count)

    own, near, far, near_twin = [], [], [], []
    for at, (part, first, count) in enumerate(cuts):
        rows = lax.dynamic_index_in_dim(three_index, row ^ part, 0, keepdims=False)
        rows = rows[first : first + count]
        if part:
            if at > 2:
                rows = after(rows, own[at - 2])
            rows = exchange(rows, "row", part)
        own.append(rows)
        if at > 1:
            rows = after(rows, near[at - 2])
        reach = 1
        while reach < groups:
            span = min(reach, groups - reach) * NPANEL
            links = [(one, one + reach * NPANEL) for one in range(span)]
            got = lax.ppermute(rows, "col", links)
            rows = jnp.where((group >= reach) & (group < 2 * reach), got, rows)
            reach *= 2
        near.append(rows)
        sent = after(rows, far[at - 2]) if at > 1 else rows
        far.append(exchange(sent, "col", 2))
        near_twin.append(exchange(rows, "col", 1))

    own_orbital = col * row_count + row
    panels = [position ^ turn for turn in range(NPANEL)]
    orbitals = jnp.stack([own_orbital] + [at * row_count + row for at in panels])
    kept = block_mask[orbitals].reshape(NPANEL + 1, block_mask.shape[1], row_count, -1)
    kept = kept[:, :, row ^ jnp.arange(row_count), :].reshape(NPANEL + 1, kept.shape[1], -1)
    masks = jnp.repeat(kept.astype(jnp.float32), BLOCK, axis=-1)
    lists = pair_list[row]
    scalars = []
    for turn in range(NPANEL):
        live = jnp.any(lists == panels[turn]).astype(jnp.float32)
        scalars += [occ_energy[own_orbital] + occ_energy[orbitals[1 + turn]], live]
    first, second = jnp.stack(scalars[:4]), jnp.stack(scalars[4:])

    own_high, own_low, response, density = early(
        cuts, first, vir_energy, masks[:3], own, near, near_twin
    )
    far_twin = [exchange(piece, "col", 1) for piece in far[:-2]]
    far_twin += [exchange(after(piece, response), "col", 1) for piece in far[-2:]]
    last = late(cuts, second, vir_energy, masks[3:], (own_high, own_low), far, far_twin)

    middle = row_count // 2
    head = [(middle, 0, nvir)]
    rest = [(at, 0, nvir) for at in range(row_count) if at != middle]
    pieces = list(responses(head, response, last))
    density = after(density, pieces[0])
    density = densities(1.0 / (row_count * col_count), density, last)
    response = after(response, density)
    pieces += responses(rest, response, last)
    total = sum_row(scatter_plane(density))
    pieces[-1] = after(pieces[-1], total)

    returned = jnp.zeros_like(three_index)
    for (part, _, _), piece in zip(head + rest, pieces):
        if part:
            piece = exchange(piece, "row", part)
        returned = lax.dynamic_update_index_in_dim(returned, piece, row ^ part, 0)
    return returned, gather_plane(total)


def solution(mesh):
    placed = (P("col", None, "row"), P(), P(), P(), P("col", None))
    return jax.shard_map(
        on_device,
        mesh=mesh,
        in_specs=placed,
        out_specs=(P("col", None, "row"), P()),
        check_vma=False,
    )
```

```python
import functools

import jax
import jax.numpy as jnp
from jax import lax
from jax.experimental import pallas as pl
from jax.experimental.pallas import tpu as pltpu
from jax.sharding import PartitionSpec as P

BLOCK = 64
NPANEL = 4
TILE = 256
VMEM_LIMIT = 24 * 1024 * 1024
SMEM = pl.BlockSpec(memory_space=pltpu.SMEM)
VMEM = pl.BlockSpec(memory_space=pltpu.VMEM)
NT = (((1,), (1,)), ((), ()))


def call(kernel, name, outs, operands, flops, scratch=(), scalars=0):
    size = sum(at.size * at.dtype.itemsize for at in [*outs, *operands])
    return pl.pallas_call(
        kernel,
        out_shape=outs,
        in_specs=[SMEM] * scalars + [VMEM] * (len(operands) - scalars),
        out_specs=[VMEM] * len(outs),
        scratch_shapes=list(scratch),
        compiler_params=pltpu.CompilerParams(vmem_limit_bytes=VMEM_LIMIT),
        cost_estimate=pl.CostEstimate(flops=flops, bytes_accessed=size, transcendentals=0),
        name=name,
    )(*operands)


def shape(*sizes, kind=jnp.float32):
    return jax.ShapeDtypeStruct(sizes, kind)


def halves(value):
    high = value.astype(jnp.bfloat16)
    return high, (value - high.astype(jnp.float32)).astype(jnp.bfloat16)


def dot(left, right):
    return jnp.dot(left, right, preferred_element_type=jnp.float32)


def dot_nt(left, right):
    return lax.dot_general(left, right, NT, preferred_element_type=jnp.float32)


def split_rows(cuts, pieces, mask, high, low):
    for (part, first, count), piece in zip(cuts, pieces):
        width = piece.shape[1]
        cols = slice(part * width, (part + 1) * width)
        for start in range(0, count, BLOCK):
            at = first + start
            kept = mask[at // BLOCK : at // BLOCK + 1, cols]
            value = piece[start : start + BLOCK, :] * kept
            high[at : at + BLOCK, cols], low[at : at + BLOCK, cols] = halves(value)


def amplitudes(energy, live, vir_col, vir_row, own, panel, amp, a_parts, w_parts):
    nvir = amp.shape[0]
    for start in range(0, nvir, TILE):
        cols = slice(start, start + TILE)
        cross = dot_nt(own[0][...], panel[0][cols, :])
        cross += dot_nt(own[0][...], panel[1][cols, :])
        cross += dot_nt(own[1][...], panel[0][cols, :])
        value = cross / (energy - vir_col[...] - vir_row[:, cols]) * live
        amp[:, cols] = value
        a_parts[0][:, cols], a_parts[1][:, cols] = halves(value)
    for above in range(0, nvir, TILE):
        rows = slice(above, above + TILE)
        for start in range(0, nvir, TILE):
            cols = slice(start, start + TILE)
            value = 2.0 * amp[rows, cols] - amp[cols, rows].T
            w_parts[0][rows, cols], w_parts[1][rows, cols] = halves(value)


def respond(rows, w_parts, panel, cols):
    value = dot(w_parts[0][rows, :], panel[0][:, cols])
    value += dot(w_parts[0][rows, :], panel[1][:, cols])
    return value + dot(w_parts[1][rows, :], panel[0][:, cols])


def density_tile(cols, w_parts, a_parts):
    value = dot_nt(w_parts[0][...], a_parts[0][cols, :])
    value += dot_nt(w_parts[0][...], a_parts[1][cols, :])
    return value + dot_nt(w_parts[1][...], a_parts[0][cols, :])


def early_kernel(cuts, parts, scalars, vir_col, vir_row, masks, *refs):
    count = len(cuts)
    own, near, twin = (refs[at * count : (at + 1) * count] for at in range(3))
    refs = refs[3 * count :]
    own_high, own_low, density = refs[:3]
    slices = refs[3 : 3 + parts]
    m_high, m_low, amp, a_high, a_low, w_high, w_low = refs[3 + parts :]
    split_rows(cuts, own, masks.at[0], own_high, own_low)
    nvir = amp.shape[0]
    panel, a_parts, w_parts = (m_high, m_low), (a_high, a_low), (w_high, w_low)
    for turn, pieces in enumerate((near, twin)):
        split_rows(cuts, pieces, masks.at[1 + turn], m_high, m_low)
        amplitudes(
            scalars[2 * turn], scalars[2 * turn + 1], vir_col, vir_row,
            (own_high, own_low), panel, amp, a_parts, w_parts,
        )
        for part, piece in enumerate(slices):
            width = piece.shape[1]
            cols = slice(part * width, (part + 1) * width)
            value = respond(slice(0, nvir), w_parts, panel, cols)
            piece[...] = value if turn == 0 else piece[...] + value
        for start in range(0, nvir, TILE):
            cols = slice(start, start + TILE)
            value = density_tile(cols, w_parts, a_parts)
            density[:, cols] = value if turn == 0 else density[:, cols] + value


def early(cuts, scalars, virtual, masks, own, near, twin):
    nvir, width = own[0].shape
    naux = masks.shape[2]
    parts = naux // width
    half = jnp.bfloat16
    outs = [shape(nvir, naux, kind=half)] * 2 + [shape(nvir, nvir)]
    outs += [shape(nvir, width)] * parts
    scratch = [pltpu.VMEM((nvir, naux), half)] * 2
    scratch += [pltpu.VMEM((nvir, nvir), jnp.float32)]
    scratch += [pltpu.VMEM((nvir, nvir), half)] * 4
    operands = [scalars, virtual[:, None], virtual[None, :], masks, *own, *near, *twin]
    flops = 2 * 3 * 2 * nvir * nvir * (2 * naux + nvir)
    kernel = functools.partial(early_kernel, cuts, parts)
    outs = call(kernel, "early", outs, operands, flops, scratch, 1)
    return outs[0], outs[1], outs[2], list(outs[3:])


def late_kernel(cuts, head, scalars, vir_col, vir_row, masks, own_high, own_low, before, *refs):
    count = len(cuts)
    sources = refs[:count], refs[count : 2 * count]
    refs = refs[2 * count :]
    amp = refs[13]
    for turn, pieces in enumerate(sources):
        m_high, m_low, a_high, a_low, w_high, w_low = refs[6 * turn : 6 * turn + 6]
        split_rows(cuts, pieces, masks.at[turn], m_high, m_low)
        amplitudes(
            scalars[2 * turn], scalars[2 * turn + 1], vir_col, vir_row,
            (own_high, own_low), (m_high, m_low), amp, (a_high, a_low), (w_high, w_low),
        )
    respond_all([head], [before], [refs[12]], refs[:12])


def late(cuts, head, scalars, virtual, masks, own, before, far, twin):
    nvir, naux = own[0].shape
    width = before.shape[1]
    half = jnp.bfloat16
    outs = ([shape(nvir, naux, kind=half)] * 2 + [shape(nvir, nvir, kind=half)] * 4) * 2
    outs += [shape(head[2], width)]
    operands = [scalars, virtual[:, None], virtual[None, :], masks, *own, before, *far, *twin]
    flops = 2 * 3 * 2 * nvir * nvir * (naux + width)
    scratch = [pltpu.VMEM((nvir, nvir), jnp.float32)]
    kernel = functools.partial(late_kernel, cuts, head)
    outs = call(kernel, "late", outs, operands, flops, scratch, 1)
    return list(outs[:12]), outs[12]


def respond_all(wanted, before, pieces, panels):
    for (part, first, count), old, piece in zip(wanted, before, pieces):
        rows = slice(first, first + count)
        width = piece.shape[1]
        cols = slice(part * width, (part + 1) * width)
        value = old[rows, :]
        for at in (0, 6):
            m_high, m_low, _, _, w_high, w_low = panels[at : at + 6]
            value += respond(rows, (w_high, w_low), (m_high, m_low), cols)
        piece[...] = value


def density_kernel(scale, before, *refs):
    panels, total = refs[:8], refs[8]
    for start in range(0, before.shape[0], TILE):
        cols = slice(start, start + TILE)
        value = before[:, cols]
        for at in (0, 4):
            a_high, a_low, w_high, w_low = panels[at : at + 4]
            value += density_tile(cols, (w_high, w_low), (a_high, a_low))
        total[:, cols] = value * scale


def densities(scale, before, panels):
    kernel = functools.partial(density_kernel, scale)
    operands = [before, *panels[2:6], *panels[8:12]]
    return call(kernel, "density", [shape(*before.shape)], operands, 0)[0]


def rest_kernel(wanted, *refs):
    count = len(wanted)
    respond_all(wanted, refs[:count], refs[count + 12 :], refs[count : count + 12])


def rest(wanted, slices, panels):
    width = slices[0].shape[1]
    outs = [shape(count, width) for _, _, count in wanted]
    operands = [slices[part] for part, _, _ in wanted] + panels
    return list(call(functools.partial(rest_kernel, wanted), "rest", outs, operands, 0))


def exchange(value, axis, bit):
    size = lax.axis_size(axis)
    return lax.ppermute(value, axis, [(at, at ^ bit) for at in range(size)])


def after(value, *others):
    return lax.optimization_barrier((value, *others))[0]


def bits(axis):
    size = lax.axis_size(axis)
    return [1 << at for at in range(size.bit_length() - 1)]


def scatter_chip(value):
    half = value.shape[0] // 2
    side = lax.axis_index("col") % 2
    kept = lax.dynamic_slice_in_dim(value, side * half, half, 0)
    sent = lax.dynamic_slice_in_dim(value, (1 - side) * half, half, 0)
    return kept + exchange(sent, "col", 1)


def scatter_plane(value):
    place = lax.axis_index("col") // 2
    chips = lax.axis_size("col") // 2
    count = value.shape[0] // chips
    total = lax.dynamic_slice_in_dim(value, place * count, count, 0)
    for turn in range(1, chips):
        sent = lax.dynamic_slice_in_dim(value, (place ^ turn) * count, count, 0)
        total = total + exchange(sent, "col", 2 * turn)
    return total


def sum_row(value, head, others):
    steps = bits("row")
    value = after(value, head)
    for bit in steps:
        if bit == steps[-1]:
            value = after(value, *others)
        value = value + exchange(value, "row", bit)
    return value


def joined(terms, place):
    if len(terms) == 1:
        return terms[0]
    half = len(terms) // 2
    low, high = joined(terms[:half], place), joined(terms[half:], place)
    side = (place // half) % 2
    return jnp.where(side == 0, jnp.concatenate([low, high]), jnp.concatenate([high, low]))


def gather_plane(value):
    col = lax.axis_index("col")
    turns = range(1, lax.axis_size("col") // 2)
    terms = [value] + [exchange(value, "col", 2 * turn) for turn in turns]
    value = joined(terms, col // 2)
    return joined([value, exchange(value, "col", 1)], col)


def cut_list(nvir, row_count):
    cuts = [(part, 0, nvir) for part in range(row_count - 1)]
    return cuts + [(row_count - 1, at, nvir // 2) for at in (0, nvir // 2)]


def on_device(three_index, occ_energy, vir_energy, block_mask, pair_list):
    row = lax.axis_index("row")
    col = lax.axis_index("col")
    row_count = lax.axis_size("row")
    col_count = lax.axis_size("col")
    position = col % NPANEL
    group = col // NPANEL
    groups = col_count // NPANEL
    nvir = three_index.shape[1]
    cuts = cut_list(nvir, row_count)

    own_orbital = col * row_count + row
    panels = [position ^ turn for turn in range(NPANEL)]
    orbitals = jnp.stack([own_orbital] + [at * row_count + row for at in panels])
    kept = block_mask[orbitals].reshape(NPANEL + 1, block_mask.shape[1], row_count, -1)
    kept = kept[:, :, row ^ jnp.arange(row_count), :].reshape(NPANEL + 1, kept.shape[1], -1)
    masks = jnp.repeat(kept.astype(jnp.float32), BLOCK, axis=-1)
    lists = pair_list[row]
    scalars = []
    for turn in range(NPANEL):
        live = jnp.any(lists == panels[turn]).astype(jnp.float32)
        scalars += [occ_energy[own_orbital] + occ_energy[orbitals[1 + turn]], live]
    small = masks[:3], masks[3:], jnp.stack(scalars[:4]), jnp.stack(scalars[4:])

    own, came, near, far = [], [], [], []

    def receive(at):
        part, first, count = cuts[at]
        rows = lax.dynamic_index_in_dim(three_index, row ^ part, 0, keepdims=False)
        rows = rows[first : first + count]
        if part == row_count - 1:
            rows = after(rows, near[0 if first == 0 else 1])
        own.append(exchange(rows, "row", part) if part else rows)

    for at in range(len(cuts)):
        while len(own) < min(at + 2, len(cuts)) and (at or len(own) < row_count - 1):
            receive(len(own))
        rows = own[at]
        if at:
            rows = after(rows, came[-1])
        if at > 1:
            rows = after(rows, *own[at + 1 : at + 2])
        reach = 1
        while reach < groups:
            span = min(reach, groups - reach) * NPANEL
            links = [(one, one + reach * NPANEL) for one in range(span)]
            got = lax.ppermute(rows, "col", links)
            rows = jnp.where((group >= reach) & (group < 2 * reach), got, rows)
            reach *= 2
        came.append(got)
        near.append(rows)
        sent = after(rows, far[-1]) if at else after(rows, *small)
        far.append(exchange(sent, "col", 2))

    near_twin = [exchange(piece, "col", 1) for piece in near]
    own_high, own_low, density, slices = early(
        cuts, small[2], vir_energy, small[0], own, near, near_twin
    )
    far_twin = [exchange(piece, "col", 1) for piece in far[:-2]]
    far_twin += [exchange(after(piece, density), "col", 1) for piece in far[-2:]]

    middle = row_count // 2
    head = (middle, 0, nvir)
    others = [(at, 0, nvir) for at in range(1, row_count - 1) if at != middle]
    wanted = others + cuts[-2:] + cuts[:1]
    last, piece = late(
        cuts, head, small[3], vir_energy, small[1], (own_high, own_low), slices[middle],
        far, far_twin,
    )
    ends = {head: exchange(piece, "row", middle)}
    scale = 1.0 / (row_count * col_count)
    total = scatter_chip(densities(scale, after(density, piece), last))
    slices[0] = after(slices[0], total)
    pieces = rest(wanted, slices, last)
    for cut, piece in zip(others, pieces):
        ends[cut] = exchange(piece, "row", cut[0])
    total = scatter_plane(total)
    ends[wanted[-3]] = exchange(after(pieces[-3], total), "row", row_count - 1)
    total = sum_row(total, ends[head], [ends[cut] for cut in others])
    ends[wanted[-2]] = exchange(after(pieces[-2], total), "row", row_count - 1)
    ends[wanted[-1]] = pieces[-1]
    total = gather_plane(after(total, ends[wanted[-3]]))

    returned = jnp.zeros_like(three_index)
    for (part, first, _), piece in ends.items():
        returned = lax.dynamic_update_slice(returned, piece[None], (row ^ part, first, 0))
    return returned, total


def solution(mesh):
    placed = (P("col", None, "row"), P(), P(), P(), P("col", None))
    return jax.shard_map(
        on_device,
        mesh=mesh,
        in_specs=placed,
        out_specs=(P("col", None, "row"), P()),
        check_vma=False,
    )
```

```python
import functools

import jax
import jax.numpy as jnp
from jax import lax
from jax.experimental import pallas as pl
from jax.experimental.pallas import tpu as pltpu
from jax.sharding import PartitionSpec as P

BLOCK = 64
NPANEL = 4
TILE = 256
VMEM_LIMIT = 60 * 1024 * 1024
NT = (((1,), (1,)), ((), ()))


def staged(kernel, smalls, bigs, count, *refs):
    small, refs = refs[:smalls], refs[smalls:]
    sources, targets, scratch = refs[:bigs], refs[bigs : bigs + count], refs[bigs + count : -2]
    in_sem, out_sem = refs[-2:]
    held, made, own = scratch[:bigs], scratch[bigs : bigs + count], scratch[bigs + count :]
    loads = [
        pltpu.make_async_copy(source, target, in_sem.at[at])
        for at, (source, target) in enumerate(zip(sources, held))
    ]
    stores = [
        pltpu.make_async_copy(source, target, out_sem.at[at])
        for at, (source, target) in enumerate(zip(made, targets))
    ]
    for load in loads:
        load.start()
    kernel(small, held, made, own, [load.wait for load in loads], [store.start for store in stores])
    for store in stores:
        store.wait()


def call(kernel, name, outs, small, big, flops, scratch):
    size = sum(at.size * at.dtype.itemsize for at in [*outs, *big])
    any_space = pl.BlockSpec(memory_space=pl.ANY)
    specs = [pl.BlockSpec(memory_space=pltpu.SMEM)]
    specs += [pl.BlockSpec(memory_space=pltpu.VMEM)] * (len(small) - 1)
    buffers = [pltpu.VMEM(at.shape, at.dtype) for at in [*big, *outs]]
    sems = [pltpu.SemaphoreType.DMA((len(big),)), pltpu.SemaphoreType.DMA((len(outs),))]
    return pl.pallas_call(
        functools.partial(staged, kernel, len(small), len(big), len(outs)),
        out_shape=outs,
        in_specs=specs + [any_space] * len(big),
        out_specs=[any_space] * len(outs),
        scratch_shapes=[*buffers, *scratch, *sems],
        compiler_params=pltpu.CompilerParams(vmem_limit_bytes=VMEM_LIMIT),
        cost_estimate=pl.CostEstimate(flops=flops, bytes_accessed=size, transcendentals=0),
        name=name,
    )(*small, *big)


def shape(*sizes, kind=jnp.float32):
    return jax.ShapeDtypeStruct(sizes, kind)


def halves(value):
    high = value.astype(jnp.bfloat16)
    return high, (value - high.astype(jnp.float32)).astype(jnp.bfloat16)


def dot(left, right):
    return jnp.dot(left, right, preferred_element_type=jnp.float32)


def dot_nt(left, right):
    return lax.dot_general(left, right, NT, preferred_element_type=jnp.float32)


def split_rows(cuts, pieces, waits, mask, high, low):
    for (part, first, count), piece, wait in zip(cuts, pieces, waits):
        wait()
        width = piece.shape[1]
        cols = slice(part * width, (part + 1) * width)
        for start in range(0, count, BLOCK):
            at = first + start
            kept = mask[at // BLOCK : at // BLOCK + 1, cols]
            value = piece[start : start + BLOCK, :] * kept
            high[at : at + BLOCK, cols], low[at : at + BLOCK, cols] = halves(value)


def amplitudes(energy, live, vir_col, vir_row, own, panel, amp, a_parts, w_parts):
    nvir = amp.shape[0]
    for start in range(0, nvir, TILE):
        cols = slice(start, start + TILE)
        cross = dot_nt(own[0][...], panel[0][cols, :])
        cross += dot_nt(own[0][...], panel[1][cols, :])
        cross += dot_nt(own[1][...], panel[0][cols, :])
        value = cross / (energy - vir_col[...] - vir_row[:, cols]) * live
        amp[:, cols] = value
        a_parts[0][:, cols], a_parts[1][:, cols] = halves(value)
    for above in range(0, nvir, TILE):
        rows = slice(above, above + TILE)
        for start in range(0, nvir, TILE):
            cols = slice(start, start + TILE)
            value = 2.0 * amp[rows, cols] - amp[cols, rows].T
            w_parts[0][rows, cols], w_parts[1][rows, cols] = halves(value)


def respond(rows, w_parts, panel, cols):
    value = dot(w_parts[0][rows, :], panel[0][:, cols])
    value += dot(w_parts[0][rows, :], panel[1][:, cols])
    return value + dot(w_parts[1][rows, :], panel[0][:, cols])


def density_tile(cols, w_parts, a_parts):
    value = dot_nt(w_parts[0][...], a_parts[0][cols, :])
    value += dot_nt(w_parts[0][...], a_parts[1][cols, :])
    return value + dot_nt(w_parts[1][...], a_parts[0][cols, :])


def early_kernel(cuts, small, held, made, own_scratch, wait, give):
    scalars, vir_col, vir_row, masks = small
    count = len(cuts)
    own_high, own_low, density, *slices = made
    m_high, m_low, amp, a_high, a_low, w_high, w_low = own_scratch
    split_rows(cuts, held[:count], wait[:count], masks.at[0], own_high, own_low)
    give[0]()
    give[1]()
    nvir = amp.shape[0]
    panel, a_parts, w_parts = (m_high, m_low), (a_high, a_low), (w_high, w_low)
    for turn in range(2):
        where = slice((1 + turn) * count, (2 + turn) * count)
        split_rows(cuts, held[where], wait[where], masks.at[1 + turn], m_high, m_low)
        amplitudes(
            scalars[2 * turn], scalars[2 * turn + 1], vir_col, vir_row,
            (own_high, own_low), panel, amp, a_parts, w_parts,
        )
        for start in range(0, nvir, TILE):
            cols = slice(start, start + TILE)
            value = density_tile(cols, w_parts, a_parts)
            density[:, cols] = value if turn == 0 else density[:, cols] + value
        if turn:
            give[2]()
        for part, piece in enumerate(slices):
            width = piece.shape[1]
            cols = slice(part * width, (part + 1) * width)
            value = respond(slice(0, nvir), w_parts, panel, cols)
            piece[...] = value if turn == 0 else piece[...] + value
            if turn:
                give[3 + part]()


def squares(nvir, naux):
    half = jnp.bfloat16
    return [pltpu.VMEM((nvir, naux), half)] * 2, [pltpu.VMEM((nvir, nvir), half)] * 4


def early(cuts, scalars, virtual, masks, own, near, twin):
    nvir, width = own[0].shape
    naux = masks.shape[2]
    parts = naux // width
    outs = [shape(nvir, naux, kind=jnp.bfloat16)] * 2 + [shape(nvir, nvir)]
    outs += [shape(nvir, width)] * parts
    wide, square = squares(nvir, naux)
    small = [scalars, virtual[:, None], virtual[None, :], masks]
    flops = 2 * 3 * 2 * nvir * nvir * (2 * naux + nvir)
    kernel = functools.partial(early_kernel, cuts)
    scratch = [*wide, pltpu.VMEM((nvir, nvir), jnp.float32), *square]
    outs = call(kernel, "early", outs, small, [*own, *near, *twin], flops, scratch)
    return outs[:2], outs[2], list(outs[3:])


def late_kernel(cuts, wanted, scale, small, held, made, own_scratch, wait, give):
    scalars, vir_col, vir_row, masks = small
    count = len(cuts)
    amp, panels = own_scratch[0], (own_scratch[1:7], own_scratch[7:])
    wait[0]()
    wait[1]()
    for turn, (m_high, m_low, a_high, a_low, w_high, w_low) in enumerate(panels):
        where = slice(2 + turn * count, 2 + (1 + turn) * count)
        split_rows(cuts, held[where], wait[where], masks.at[turn], m_high, m_low)
        amplitudes(
            scalars[2 * turn], scalars[2 * turn + 1], vir_col, vir_row,
            held[:2], (m_high, m_low), amp, (a_high, a_low), (w_high, w_low),
        )
    density, *slices = held[2 + 2 * count :]
    total, *pieces = made
    for ready in wait[2 + 2 * count :]:
        ready()
    for start in range(0, density.shape[0], TILE):
        cols = slice(start, start + TILE)
        value = density[:, cols]
        for _, _, a_high, a_low, w_high, w_low in panels:
            value += density_tile(cols, (w_high, w_low), (a_high, a_low))
        total[:, cols] = value * scale
    give[0]()
    for at, ((part, first, height), piece) in enumerate(zip(wanted, pieces)):
        rows = slice(first, first + height)
        width = piece.shape[1]
        cols = slice(part * width, (part + 1) * width)
        value = slices[part][rows, :]
        for m_high, m_low, _, _, w_high, w_low in panels:
            value += respond(rows, (w_high, w_low), (m_high, m_low), cols)
        piece[...] = value
        give[1 + at]()


def late(cuts, wanted, scale, scalars, virtual, masks, own, far, twin, density, slices):
    nvir, naux = own[0].shape
    width = slices[0].shape[1]
    outs = [shape(nvir, nvir)] + [shape(height, width) for _, _, height in wanted]
    wide, square = squares(nvir, naux)
    small = [scalars, virtual[:, None], virtual[None, :], masks]
    flops = 2 * 3 * 2 * nvir * nvir * (2 * naux + nvir)
    kernel = functools.partial(late_kernel, cuts, wanted, scale)
    scratch = [pltpu.VMEM((nvir, nvir), jnp.float32), *wide, *square, *wide, *square]
    big = [*own, *far, *twin, density, *slices]
    outs = call(kernel, "late", outs, small, big, flops, scratch)
    return outs[0], list(outs[1:])


def exchange(value, axis, bit):
    size = lax.axis_size(axis)
    return lax.ppermute(value, axis, [(at, at ^ bit) for at in range(size)])


def after(value, *others):
    return lax.optimization_barrier((value, *others))[0]


def bits(axis):
    size = lax.axis_size(axis)
    return [1 << at for at in range(size.bit_length() - 1)]


def scatter_chip(value):
    half = value.shape[0] // 2
    side = lax.axis_index("col") % 2
    kept = lax.dynamic_slice_in_dim(value, side * half, half, 0)
    sent = lax.dynamic_slice_in_dim(value, (1 - side) * half, half, 0)
    return kept + exchange(sent, "col", 1)


def scatter_plane(value):
    place = lax.axis_index("col") // 2
    chips = lax.axis_size("col") // 2
    count = value.shape[0] // chips
    total = lax.dynamic_slice_in_dim(value, place * count, count, 0)
    for turn in range(1, chips):
        sent = lax.dynamic_slice_in_dim(value, (place ^ turn) * count, count, 0)
        total = total + exchange(sent, "col", 2 * turn)
    return total


def joined(terms, place):
    if len(terms) == 1:
        return terms[0]
    half = len(terms) // 2
    low, high = joined(terms[:half], place), joined(terms[half:], place)
    side = (place // half) % 2
    return jnp.where(side == 0, jnp.concatenate([low, high]), jnp.concatenate([high, low]))


def gather_plane(value, other):
    col = lax.axis_index("col")
    turns = range(1, lax.axis_size("col") // 2)
    terms = [value] + [exchange(value, "col", 2 * turn) for turn in turns]
    value = after(joined(terms, col // 2), other)
    return joined([value, exchange(value, "col", 1)], col)


def cut_list(nvir, row_count):
    cuts = [(part, 0, nvir) for part in range(row_count - 1)]
    return cuts + [(row_count - 1, at, nvir // 2) for at in (0, nvir // 2)]


def on_device(three_index, occ_energy, vir_energy, block_mask, pair_list):
    row = lax.axis_index("row")
    col = lax.axis_index("col")
    row_count = lax.axis_size("row")
    col_count = lax.axis_size("col")
    position = col % NPANEL
    group = col // NPANEL
    groups = col_count // NPANEL
    nvir = three_index.shape[1]
    cuts = cut_list(nvir, row_count)

    own_orbital = col * row_count + row
    panels = [position ^ turn for turn in range(NPANEL)]
    orbitals = jnp.stack([own_orbital] + [at * row_count + row for at in panels])
    kept = block_mask[orbitals].reshape(NPANEL + 1, block_mask.shape[1], row_count, -1)
    kept = kept[:, :, row ^ jnp.arange(row_count), :].reshape(NPANEL + 1, kept.shape[1], -1)
    masks = jnp.repeat(kept.astype(jnp.float32), BLOCK, axis=-1)
    lists = pair_list[row]
    scalars = []
    for turn in range(NPANEL):
        live = jnp.any(lists == panels[turn]).astype(jnp.float32)
        scalars += [occ_energy[own_orbital] + occ_energy[orbitals[1 + turn]], live]
    small = masks[:3], masks[3:], jnp.stack(scalars[:4]), jnp.stack(scalars[4:])

    own, came, near, far = [], [], [], []

    def receive(at):
        part, first, count = cuts[at]
        rows = lax.dynamic_index_in_dim(three_index, row ^ part, 0, keepdims=False)
        rows = rows[first : first + count]
        if part == row_count - 1:
            rows = after(rows, near[0 if first == 0 else 1])
        elif part > 1:
            rows = after(rows, *small[2:])
        own.append(exchange(rows, "row", part) if part else rows)

    for at in range(len(cuts)):
        while len(own) < min(at + 2, len(cuts)) and (at or len(own) < row_count - 1):
            receive(len(own))
        rows = own[at]
        if at:
            rows = after(rows, came[-1])
        if at > 1:
            rows = after(rows, *own[at + 1 : at + 2])
        reach = 1
        while reach < groups:
            span = min(reach, groups - reach) * NPANEL
            links = [(one, one + reach * NPANEL) for one in range(span)]
            got = lax.ppermute(rows, "col", links)
            rows = jnp.where((group >= reach) & (group < 2 * reach), got, rows)
            reach *= 2
        came.append(got)
        near.append(rows)
        sent = after(rows, far[-1]) if at else after(rows, *small)
        far.append(exchange(sent, "col", 2))

    near_twin = [exchange(piece, "col", 1) for piece in near]
    far_twin = [exchange(piece, "col", 1) for piece in far]
    halved, density, slices = early(
        cuts, after(small[2], far[-1]), vir_energy, small[0], own, near, near_twin
    )

    middle, edge, half = row_count // 2, row_count - 1, nvir // 2
    others = [(at, 0, nvir) for at in range(1, edge) if at != middle]
    wanted = [(middle, 0, half), (middle, half, half), *others]
    wanted += [(edge, 0, half), (edge, half, half), (0, 0, nvir)]
    scale = 1.0 / (row_count * col_count)
    total, pieces = late(
        cuts, wanted, scale, small[3], vir_energy, small[1], halved, far, far_twin,
        density, slices,
    )
    ends = [exchange(piece, "row", cut[0]) for cut, piece in zip(wanted[:-3], pieces)]
    total = after(scatter_plane(scatter_chip(total)), ends[0])
    for bit in bits("row")[:-1]:
        total = total + exchange(total, "row", bit)
    ends.append(exchange(after(pieces[-3], total), "row", edge))
    total = after(total, *ends[1:-1])
    total = total + exchange(total, "row", bits("row")[-1])
    ends.append(exchange(after(pieces[-2], total), "row", edge))
    total = gather_plane(total, ends[-2])
    ends.append(pieces[-1])

    returned = jnp.zeros_like(three_index)
    for (part, first, _), piece in zip(wanted, ends):
        returned = lax.dynamic_update_slice(returned, piece[None], (row ^ part, first, 0))
    return returned, total


def solution(mesh):
    placed = (P("col", None, "row"), P(), P(), P(), P("col", None))
    return jax.shard_map(
        on_device,
        mesh=mesh,
        in_specs=placed,
        out_specs=(P("col", None, "row"), P()),
        check_vma=False,
    )
```

```python
import functools

import jax
import jax.numpy as jnp
from jax import lax
from jax.experimental import pallas as pl
from jax.experimental.pallas import tpu as pltpu
from jax.sharding import PartitionSpec as P

BLOCK = 64
NPANEL = 4
TILE = 256
VMEM_LIMIT = 60 * 1024 * 1024
NT = (((1,), (1,)), ((), ()))


def staged(kernel, smalls, bigs, count, *refs):
    small, refs = refs[:smalls], refs[smalls:]
    sources, targets, scratch = refs[:bigs], refs[bigs : bigs + count], refs[bigs + count : -2]
    in_sem, out_sem = refs[-2:]
    held, made, own = scratch[:bigs], scratch[bigs : bigs + count], scratch[bigs + count :]
    loads = [
        pltpu.make_async_copy(source, target, in_sem.at[at])
        for at, (source, target) in enumerate(zip(sources, held))
    ]
    stores = [
        pltpu.make_async_copy(source, target, out_sem.at[at])
        for at, (source, target) in enumerate(zip(made, targets))
    ]
    for load in loads:
        load.start()
    kernel(small, held, made, own, [load.wait for load in loads], [store.start for store in stores])
    for store in stores:
        store.wait()


def call(kernel, name, outs, small, big, scratch):
    any_space = pl.BlockSpec(memory_space=pl.ANY)
    specs = [pl.BlockSpec(memory_space=pltpu.SMEM)]
    specs += [pl.BlockSpec(memory_space=pltpu.VMEM)] * (len(small) - 1)
    buffers = [pltpu.VMEM(at.shape, at.dtype) for at in [*big, *outs]]
    sems = [pltpu.SemaphoreType.DMA((len(big),)), pltpu.SemaphoreType.DMA((len(outs),))]
    return pl.pallas_call(
        functools.partial(staged, kernel, len(small), len(big), len(outs)),
        out_shape=outs,
        in_specs=specs + [any_space] * len(big),
        out_specs=[any_space] * len(outs),
        scratch_shapes=[*buffers, *scratch, *sems],
        compiler_params=pltpu.CompilerParams(vmem_limit_bytes=VMEM_LIMIT),
        cost_estimate=pl.CostEstimate(flops=0, bytes_accessed=0, transcendentals=0),
        name=name,
    )(*small, *big)


def shape(*sizes, kind=jnp.float32):
    return jax.ShapeDtypeStruct(sizes, kind)


def halves(value):
    high = value.astype(jnp.bfloat16)
    return high, (value - high.astype(jnp.float32)).astype(jnp.bfloat16)


def dot(left, right):
    return jnp.dot(left, right, preferred_element_type=jnp.float32)


def dot_nt(left, right):
    return lax.dot_general(left, right, NT, preferred_element_type=jnp.float32)


def split_rows(cuts, pieces, waits, mask, high, low):
    for (part, first, count), piece, wait in zip(cuts, pieces, waits):
        wait()
        width = piece.shape[1]
        cols = slice(part * width, (part + 1) * width)
        for start in range(0, count, BLOCK):
            at = first + start
            kept = mask[at // BLOCK : at // BLOCK + 1, cols]
            value = piece[start : start + BLOCK, :] * kept
            high[at : at + BLOCK, cols], low[at : at + BLOCK, cols] = halves(value)


def amplitudes(energy, live, vir_col, vir_row, own, panel, amp, a_parts, w_parts):
    nvir = amp.shape[0]
    for start in range(0, nvir, TILE):
        cols = slice(start, start + TILE)
        cross = dot_nt(own[0][...], panel[0][cols, :])
        cross += dot_nt(own[0][...], panel[1][cols, :])
        cross += dot_nt(own[1][...], panel[0][cols, :])
        value = cross / (energy - vir_col[...] - vir_row[:, cols]) * live
        amp[:, cols] = value
        a_parts[0][:, cols], a_parts[1][:, cols] = halves(value)
    for above in range(0, nvir, TILE):
        rows = slice(above, above + TILE)
        for start in range(0, nvir, TILE):
            cols = slice(start, start + TILE)
            value = 2.0 * amp[rows, cols] - amp[cols, rows].T
            w_parts[0][rows, cols], w_parts[1][rows, cols] = halves(value)


def respond(rows, w_parts, panel, cols):
    value = dot(w_parts[0][rows, :], panel[0][:, cols])
    value += dot(w_parts[0][rows, :], panel[1][:, cols])
    return value + dot(w_parts[1][rows, :], panel[0][:, cols])


def density_tile(cols, w_parts, a_parts):
    value = dot_nt(w_parts[0][...], a_parts[0][cols, :])
    value += dot_nt(w_parts[0][...], a_parts[1][cols, :])
    return value + dot_nt(w_parts[1][...], a_parts[0][cols, :])


def early_kernel(cuts, small, held, made, own_scratch, wait, give):
    scalars, vir_col, vir_row, masks = small
    count = len(cuts)
    own_high, own_low, density, *slices = made
    m_high, m_low, amp, a_high, a_low, w_high, w_low = own_scratch
    split_rows(cuts, held[:count], wait[:count], masks.at[0], own_high, own_low)
    give[0]()
    give[1]()
    nvir = amp.shape[0]
    panel, a_parts, w_parts = (m_high, m_low), (a_high, a_low), (w_high, w_low)
    for turn in range(2):
        where = slice((1 + turn) * count, (2 + turn) * count)
        split_rows(cuts, held[where], wait[where], masks.at[1 + turn], m_high, m_low)
        amplitudes(
            scalars[2 * turn], scalars[2 * turn + 1], vir_col, vir_row,
            (own_high, own_low), panel, amp, a_parts, w_parts,
        )
        for start in range(0, nvir, TILE):
            cols = slice(start, start + TILE)
            value = density_tile(cols, w_parts, a_parts)
            density[:, cols] = value if turn == 0 else density[:, cols] + value
        if turn:
            give[2]()
        for part, piece in enumerate(slices):
            width = piece.shape[1]
            cols = slice(part * width, (part + 1) * width)
            value = respond(slice(0, nvir), w_parts, panel, cols)
            piece[...] = value if turn == 0 else piece[...] + value
            if turn:
                give[3 + part]()


def squares(nvir, naux):
    half = jnp.bfloat16
    return [pltpu.VMEM((nvir, naux), half)] * 2, [pltpu.VMEM((nvir, nvir), half)] * 4


def early(cuts, scalars, virtual, masks, own, near, twin):
    nvir, width = own[0].shape
    naux = masks.shape[2]
    parts = naux // width
    outs = [shape(nvir, naux, kind=jnp.bfloat16)] * 2 + [shape(nvir, nvir)]
    outs += [shape(nvir, width)] * parts
    wide, square = squares(nvir, naux)
    small = [scalars, virtual[:, None], virtual[None, :], masks]
    kernel = functools.partial(early_kernel, cuts)
    scratch = [*wide, pltpu.VMEM((nvir, nvir), jnp.float32), *square]
    outs = call(kernel, "early", outs, small, [*own, *near, *twin], scratch)
    return outs[:2], outs[2], list(outs[3:])


def late_kernel(cuts, wanted, scale, small, held, made, own_scratch, wait, give):
    scalars, vir_col, vir_row, masks = small
    count = len(cuts)
    amp, panels = own_scratch[0], (own_scratch[1:7], own_scratch[7:])
    wait[0]()
    wait[1]()
    for turn, (m_high, m_low, a_high, a_low, w_high, w_low) in enumerate(panels):
        where = slice(2 + turn * count, 2 + (1 + turn) * count)
        split_rows(cuts, held[where], wait[where], masks.at[turn], m_high, m_low)
        amplitudes(
            scalars[2 * turn], scalars[2 * turn + 1], vir_col, vir_row,
            held[:2], (m_high, m_low), amp, (a_high, a_low), (w_high, w_low),
        )
    density, *slices = held[2 + 2 * count :]
    total, *pieces = made
    for ready in wait[2 + 2 * count :]:
        ready()
    for start in range(0, density.shape[0], TILE):
        cols = slice(start, start + TILE)
        value = density[:, cols]
        for _, _, a_high, a_low, w_high, w_low in panels:
            value += density_tile(cols, (w_high, w_low), (a_high, a_low))
        total[:, cols] = value * scale
    give[0]()
    for at, ((part, first, height), piece) in enumerate(zip(wanted, pieces)):
        rows = slice(first, first + height)
        width = piece.shape[1]
        cols = slice(part * width, (part + 1) * width)
        value = slices[part][rows, :]
        for m_high, m_low, _, _, w_high, w_low in panels:
            value += respond(rows, (w_high, w_low), (m_high, m_low), cols)
        piece[...] = value
        give[1 + at]()


def late(cuts, wanted, scale, scalars, virtual, masks, own, far, twin, density, slices):
    nvir, naux = own[0].shape
    width = slices[0].shape[1]
    outs = [shape(nvir, nvir)] + [shape(height, width) for _, _, height in wanted]
    wide, square = squares(nvir, naux)
    small = [scalars, virtual[:, None], virtual[None, :], masks]
    kernel = functools.partial(late_kernel, cuts, wanted, scale)
    scratch = [pltpu.VMEM((nvir, nvir), jnp.float32), *wide, *square, *wide, *square]
    big = [*own, *far, *twin, density, *slices]
    outs = call(kernel, "late", outs, small, big, scratch)
    return outs[0], list(outs[1:])


def exchange(value, axis, bit):
    size = lax.axis_size(axis)
    return lax.ppermute(value, axis, [(at, at ^ bit) for at in range(size)])


def after(value, *others):
    return lax.optimization_barrier((value, *others))[0]


def bits(axis):
    size = lax.axis_size(axis)
    return [1 << at for at in range(size.bit_length() - 1)]


def scatter_chip(value):
    half = value.shape[0] // 2
    side = lax.axis_index("col") % 2
    kept = lax.dynamic_slice_in_dim(value, side * half, half, 0)
    sent = lax.dynamic_slice_in_dim(value, (1 - side) * half, half, 0)
    return kept + exchange(sent, "col", 1)


def scatter_plane(value):
    place = lax.axis_index("col") // 2
    chips = lax.axis_size("col") // 2
    count = value.shape[0] // chips
    total = lax.dynamic_slice_in_dim(value, place * count, count, 0)
    for turn in range(1, chips):
        sent = lax.dynamic_slice_in_dim(value, (place ^ turn) * count, count, 0)
        total = total + exchange(sent, "col", 2 * turn)
    return total


def joined(terms, place):
    if len(terms) == 1:
        return terms[0]
    half = len(terms) // 2
    low, high = joined(terms[:half], place), joined(terms[half:], place)
    side = (place // half) % 2
    return jnp.where(side == 0, jnp.concatenate([low, high]), jnp.concatenate([high, low]))


def gather_plane(value):
    col = lax.axis_index("col")
    turns = range(1, lax.axis_size("col") // 2)
    terms = [value] + [exchange(value, "col", 2 * turn) for turn in turns]
    value = joined(terms, col // 2)
    return joined([value, exchange(value, "col", 1)], col)


def cut_list(nvir, row_count):
    cuts = [(part, 0, nvir) for part in range(row_count - 1)]
    return cuts + [(row_count - 1, at, nvir // 2) for at in (0, nvir // 2)]


def on_device(three_index, occ_energy, vir_energy, block_mask, pair_list):
    row = lax.axis_index("row")
    col = lax.axis_index("col")
    row_count = lax.axis_size("row")
    col_count = lax.axis_size("col")
    position = col % NPANEL
    group = col // NPANEL
    groups = col_count // NPANEL
    nvir = three_index.shape[1]
    cuts = cut_list(nvir, row_count)

    own_orbital = col * row_count + row
    panels = [position ^ turn for turn in range(NPANEL)]
    orbitals = jnp.stack([own_orbital] + [at * row_count + row for at in panels])
    kept = block_mask[orbitals].reshape(NPANEL + 1, block_mask.shape[1], row_count, -1)
    kept = kept[:, :, row ^ jnp.arange(row_count), :].reshape(NPANEL + 1, kept.shape[1], -1)
    masks = jnp.repeat(kept.astype(jnp.float32), BLOCK, axis=-1)
    lists = pair_list[row]
    scalars = []
    for turn in range(NPANEL):
        live = jnp.any(lists == panels[turn]).astype(jnp.float32)
        scalars += [occ_energy[own_orbital] + occ_energy[orbitals[1 + turn]], live]
    small = masks[:3], masks[3:], jnp.stack(scalars[:4]), jnp.stack(scalars[4:])

    own, came, near, far = [], [], [], []

    def receive(at):
        part, first, count = cuts[at]
        rows = lax.dynamic_index_in_dim(three_index, row ^ part, 0, keepdims=False)
        rows = rows[first : first + count]
        if part == row_count - 1:
            rows = after(rows, near[0 if first == 0 else 1])
        own.append(exchange(rows, "row", part) if part else rows)

    for at in range(len(cuts)):
        while len(own) < min(at + 2, len(cuts)) and (at or len(own) < row_count - 1):
            receive(len(own))
        rows = own[at]
        if at:
            rows = after(rows, came[-1])
        if at > 1:
            rows = after(rows, *own[at + 1 : at + 2])
        reach = 1
        while reach < groups:
            span = min(reach, groups - reach) * NPANEL
            links = [(one, one + reach * NPANEL) for one in range(span)]
            got = lax.ppermute(rows, "col", links)
            rows = jnp.where((group >= reach) & (group < 2 * reach), got, rows)
            reach *= 2
        came.append(got)
        near.append(rows)
        sent = after(rows, far[-1]) if at else after(rows, *small)
        far.append(exchange(sent, "col", 2))

    near_twin = [exchange(piece, "col", 1) for piece in near]
    halved, density, slices = early(
        cuts, small[2], vir_energy, small[0], own, near, near_twin
    )
    far_twin = [exchange(piece, "col", 1) for piece in far[:-2]]
    far_twin += [exchange(after(piece, density), "col", 1) for piece in far[-2:]]

    middle, edge, half = row_count // 2, row_count - 1, nvir // 2
    others = [(at, 0, nvir) for at in range(1, edge) if at != middle]
    wanted = [(middle, 0, nvir), *others]
    wanted += [(edge, 0, half), (edge, half, half), (0, 0, nvir)]
    scale = 1.0 / (row_count * col_count)
    total, pieces = late(
        cuts, wanted, scale, small[3], vir_energy, small[1], halved, far, far_twin,
        density, slices,
    )
    ends = [exchange(piece, "row", cut[0]) for cut, piece in zip(wanted[:-3], pieces)]
    total = scatter_plane(scatter_chip(total))
    for bit in bits("row")[:-1]:
        total = total + exchange(total, "row", bit)
    ends.append(exchange(after(pieces[-3], total), "row", edge))
    total = after(total, *ends[:-1])
    total = total + exchange(total, "row", bits("row")[-1])
    ends.append(exchange(after(pieces[-2], total), "row", edge))
    total = gather_plane(after(total, ends[-2]))
    ends.append(pieces[-1])

    returned = jnp.zeros_like(three_index)
    for (part, first, _), piece in zip(wanted, ends):
        returned = lax.dynamic_update_slice(returned, piece[None], (row ^ part, first, 0))
    return returned, total


def solution(mesh):
    placed = (P("col", None, "row"), P(), P(), P(), P("col", None))
    return jax.shard_map(
        on_device,
        mesh=mesh,
        in_specs=placed,
        out_specs=(P("col", None, "row"), P()),
        check_vma=False,
    )
```

```python
import functools

import jax
import jax.numpy as jnp
from jax import lax
from jax.experimental import pallas as pl
from jax.experimental.pallas import tpu as pltpu
from jax.sharding import PartitionSpec as P

BLOCK = 64
NPANEL = 4
TILE = 256
VMEM_LIMIT = 60 * 1024 * 1024
NT = (((1,), (1,)), ((), ()))


def staged(kernel, smalls, bigs, count, *refs):
    small, refs = refs[:smalls], refs[smalls:]
    sources, targets, scratch = refs[:bigs], refs[bigs : bigs + count], refs[bigs + count : -2]
    in_sem, out_sem = refs[-2:]
    held, made, own = scratch[:bigs], scratch[bigs : bigs + count], scratch[bigs + count :]
    loads = [
        pltpu.make_async_copy(source, target, in_sem.at[at])
        for at, (source, target) in enumerate(zip(sources, held))
    ]
    stores = [
        pltpu.make_async_copy(source, target, out_sem.at[at])
        for at, (source, target) in enumerate(zip(made, targets))
    ]
    for load in loads:
        load.start()
    kernel(small, held, made, own, [load.wait for load in loads], [store.start for store in stores])
    for store in stores:
        store.wait()


def call(kernel, name, outs, small, big, scratch):
    any_space = pl.BlockSpec(memory_space=pl.ANY)
    specs = [pl.BlockSpec(memory_space=pltpu.SMEM)]
    specs += [pl.BlockSpec(memory_space=pltpu.VMEM)] * (len(small) - 1)
    buffers = [pltpu.VMEM(at.shape, at.dtype) for at in [*big, *outs]]
    sems = [pltpu.SemaphoreType.DMA((len(big),)), pltpu.SemaphoreType.DMA((len(outs),))]
    return pl.pallas_call(
        functools.partial(staged, kernel, len(small), len(big), len(outs)),
        out_shape=outs,
        in_specs=specs + [any_space] * len(big),
        out_specs=[any_space] * len(outs),
        scratch_shapes=[*buffers, *scratch, *sems],
        compiler_params=pltpu.CompilerParams(vmem_limit_bytes=VMEM_LIMIT),
        cost_estimate=pl.CostEstimate(flops=0, bytes_accessed=0, transcendentals=0),
        name=name,
    )(*small, *big)


def shape(*sizes, kind=jnp.float32):
    return jax.ShapeDtypeStruct(sizes, kind)


def halves(value):
    high = value.astype(jnp.bfloat16)
    return high, (value - high.astype(jnp.float32)).astype(jnp.bfloat16)


def dot(left, right):
    return jnp.dot(left, right, preferred_element_type=jnp.float32)


def dot_nt(left, right):
    return lax.dot_general(left, right, NT, preferred_element_type=jnp.float32)


def split_rows(cuts, pieces, waits, mask, high, low):
    for (part, first, count), piece, wait in zip(cuts, pieces, waits):
        wait()
        width = piece.shape[1]
        cols = slice(part * width, (part + 1) * width)
        for start in range(0, count, BLOCK):
            at = first + start
            kept = mask[at // BLOCK : at // BLOCK + 1, cols]
            value = piece[start : start + BLOCK, :] * kept
            high[at : at + BLOCK, cols], low[at : at + BLOCK, cols] = halves(value)


def amplitudes(energy, live, vir_col, vir_row, own, panel, amp, a_parts, w_parts):
    nvir = amp.shape[0]
    for start in range(0, nvir, TILE):
        cols = slice(start, start + TILE)
        cross = dot_nt(own[0][...], panel[0][cols, :])
        cross += dot_nt(own[0][...], panel[1][cols, :])
        cross += dot_nt(own[1][...], panel[0][cols, :])
        value = cross / (energy - vir_col[...] - vir_row[:, cols]) * live
        amp[:, cols] = value
        a_parts[0][:, cols], a_parts[1][:, cols] = halves(value)
    for above in range(0, nvir, TILE):
        rows = slice(above, above + TILE)
        for start in range(0, nvir, TILE):
            cols = slice(start, start + TILE)
            value = 2.0 * amp[rows, cols] - amp[cols, rows].T
            w_parts[0][rows, cols], w_parts[1][rows, cols] = halves(value)


def respond(rows, w_parts, panel, cols):
    value = dot(w_parts[0][rows, :], panel[0][:, cols])
    value += dot(w_parts[0][rows, :], panel[1][:, cols])
    return value + dot(w_parts[1][rows, :], panel[0][:, cols])


def density_tile(cols, w_parts, a_parts):
    value = dot_nt(w_parts[0][...], a_parts[0][cols, :])
    value += dot_nt(w_parts[0][...], a_parts[1][cols, :])
    return value + dot_nt(w_parts[1][...], a_parts[0][cols, :])


def early_kernel(cuts, small, held, made, own_scratch, wait, give):
    scalars, vir_col, vir_row, masks = small
    count = len(cuts)
    own_high, own_low, density, *slices = made
    m_high, m_low, amp, a_high, a_low, w_high, w_low = own_scratch
    split_rows(cuts, held[:count], wait[:count], masks.at[0], own_high, own_low)
    give[0]()
    give[1]()
    nvir = amp.shape[0]
    panel, a_parts, w_parts = (m_high, m_low), (a_high, a_low), (w_high, w_low)
    for turn in range(2):
        where = slice((1 + turn) * count, (2 + turn) * count)
        split_rows(cuts, held[where], wait[where], masks.at[1 + turn], m_high, m_low)
        amplitudes(
            scalars[2 * turn], scalars[2 * turn + 1], vir_col, vir_row,
            (own_high, own_low), panel, amp, a_parts, w_parts,
        )
        for start in range(0, nvir, TILE):
            cols = slice(start, start + TILE)
            value = density_tile(cols, w_parts, a_parts)
            density[:, cols] = value if turn == 0 else density[:, cols] + value
        if turn:
            give[2]()
        for part, piece in enumerate(slices):
            width = piece.shape[1]
            cols = slice(part * width, (part + 1) * width)
            value = respond(slice(0, nvir), w_parts, panel, cols)
            piece[...] = value if turn == 0 else piece[...] + value
            if turn:
                give[3 + part]()


def squares(nvir, naux):
    half = jnp.bfloat16
    return [pltpu.VMEM((nvir, naux), half)] * 2, [pltpu.VMEM((nvir, nvir), half)] * 4


def early(cuts, scalars, virtual, masks, own, near, twin):
    nvir, width = own[0].shape
    naux = masks.shape[2]
    parts = naux // width
    outs = [shape(nvir, naux, kind=jnp.bfloat16)] * 2 + [shape(nvir, nvir)]
    outs += [shape(nvir, width)] * parts
    wide, square = squares(nvir, naux)
    small = [scalars, virtual[:, None], virtual[None, :], masks]
    kernel = functools.partial(early_kernel, cuts)
    scratch = [*wide, pltpu.VMEM((nvir, nvir), jnp.float32), *square]
    outs = call(kernel, "early", outs, small, [*own, *near, *twin], scratch)
    return outs[:2], outs[2], list(outs[3:])


def late_kernel(cuts, wanted, scale, small, held, made, own_scratch, wait, give):
    scalars, vir_col, vir_row, masks = small
    count = len(cuts)
    amp, panels = own_scratch[0], (own_scratch[1:7], own_scratch[7:])
    wait[0]()
    wait[1]()
    for turn, (m_high, m_low, a_high, a_low, w_high, w_low) in enumerate(panels):
        where = slice(2 + turn * count, 2 + (1 + turn) * count)
        split_rows(cuts, held[where], wait[where], masks.at[turn], m_high, m_low)
        amplitudes(
            scalars[2 * turn], scalars[2 * turn + 1], vir_col, vir_row,
            held[:2], (m_high, m_low), amp, (a_high, a_low), (w_high, w_low),
        )
    density, *slices = held[2 + 2 * count :]
    total, *pieces = made
    for ready in wait[2 + 2 * count :]:
        ready()
    for start in range(0, density.shape[0], TILE):
        cols = slice(start, start + TILE)
        value = density[:, cols]
        for _, _, a_high, a_low, w_high, w_low in panels:
            value += density_tile(cols, (w_high, w_low), (a_high, a_low))
        total[:, cols] = value * scale
    give[0]()
    for at, ((part, first, height), piece) in enumerate(zip(wanted, pieces)):
        rows = slice(first, first + height)
        width = piece.shape[1]
        cols = slice(part * width, (part + 1) * width)
        value = slices[part][rows, :]
        for m_high, m_low, _, _, w_high, w_low in panels:
            value += respond(rows, (w_high, w_low), (m_high, m_low), cols)
        piece[...] = value
        give[1 + at]()


def late(cuts, wanted, scale, scalars, virtual, masks, own, far, twin, density, slices):
    nvir, naux = own[0].shape
    width = slices[0].shape[1]
    outs = [shape(nvir, nvir)] + [shape(height, width) for _, _, height in wanted]
    wide, square = squares(nvir, naux)
    small = [scalars, virtual[:, None], virtual[None, :], masks]
    kernel = functools.partial(late_kernel, cuts, wanted, scale)
    scratch = [pltpu.VMEM((nvir, nvir), jnp.float32), *wide, *square, *wide, *square]
    big = [*own, *far, *twin, density, *slices]
    outs = call(kernel, "late", outs, small, big, scratch)
    return outs[0], list(outs[1:])


def exchange(value, axis, bit):
    size = lax.axis_size(axis)
    return lax.ppermute(value, axis, [(at, at ^ bit) for at in range(size)])


def after(value, *others):
    return lax.optimization_barrier((value, *others))[0]


def bits(axis):
    size = lax.axis_size(axis)
    return [1 << at for at in range(size.bit_length() - 1)]


def scatter_chip(value):
    half = value.shape[0] // 2
    side = lax.axis_index("col") % 2
    kept = lax.dynamic_slice_in_dim(value, side * half, half, 0)
    sent = lax.dynamic_slice_in_dim(value, (1 - side) * half, half, 0)
    return kept + exchange(sent, "col", 1)


def scatter_plane(value):
    place = lax.axis_index("col") // 2
    chips = lax.axis_size("col") // 2
    count = value.shape[0] // chips
    total = lax.dynamic_slice_in_dim(value, place * count, count, 0)
    for turn in range(1, chips):
        sent = lax.dynamic_slice_in_dim(value, (place ^ turn) * count, count, 0)
        total = total + exchange(sent, "col", 2 * turn)
    return total


def joined(terms, place):
    if len(terms) == 1:
        return terms[0]
    half = len(terms) // 2
    low, high = joined(terms[:half], place), joined(terms[half:], place)
    side = (place // half) % 2
    return jnp.where(side == 0, jnp.concatenate([low, high]), jnp.concatenate([high, low]))


def gather_plane(value):
    col = lax.axis_index("col")
    turns = range(1, lax.axis_size("col") // 2)
    terms = [value] + [exchange(value, "col", 2 * turn) for turn in turns]
    value = joined(terms, col // 2)
    return joined([value, exchange(value, "col", 1)], col)


def cut_list(nvir, row_count):
    cuts = [(part, 0, nvir) for part in range(row_count - 1)]
    return cuts + [(row_count - 1, at, nvir // 2) for at in (0, nvir // 2)]


def on_device(three_index, occ_energy, vir_energy, block_mask, pair_list):
    row = lax.axis_index("row")
    col = lax.axis_index("col")
    row_count = lax.axis_size("row")
    col_count = lax.axis_size("col")
    position = col % NPANEL
    group = col // NPANEL
    groups = col_count // NPANEL
    nvir = three_index.shape[1]
    cuts = cut_list(nvir, row_count)

    own_orbital = col * row_count + row
    panels = [position ^ turn for turn in range(NPANEL)]
    orbitals = jnp.stack([own_orbital] + [at * row_count + row for at in panels])
    kept = block_mask[orbitals].reshape(NPANEL + 1, block_mask.shape[1], row_count, -1)
    kept = kept[:, :, row ^ jnp.arange(row_count), :].reshape(NPANEL + 1, kept.shape[1], -1)
    masks = jnp.repeat(kept.astype(jnp.float32), BLOCK, axis=-1)
    lists = pair_list[row]
    scalars = []
    for turn in range(NPANEL):
        live = jnp.any(lists == panels[turn]).astype(jnp.float32)
        scalars += [occ_energy[own_orbital] + occ_energy[orbitals[1 + turn]], live]
    small = masks[:3], masks[3:], jnp.stack(scalars[:4]), jnp.stack(scalars[4:])

    own, came, near, far = [], [], [], []

    def receive(at):
        part, first, count = cuts[at]
        rows = lax.dynamic_index_in_dim(three_index, row ^ part, 0, keepdims=False)
        rows = rows[first : first + count]
        if part == row_count - 1:
            rows = after(rows, near[1])
        elif part > 1:
            rows = after(rows, *small[2:])
        own.append(exchange(rows, "row", part) if part else rows)

    for at in range(len(cuts)):
        while len(own) < min(at + 1 if at > 1 else row_count - 1, len(cuts)):
            receive(len(own))
        rows = own[at]
        if at:
            rows = after(rows, came[-1])
        reach = 1
        while reach < groups:
            span = min(reach, groups - reach) * NPANEL
            links = [(one, one + reach * NPANEL) for one in range(span)]
            got = lax.ppermute(rows, "col", links)
            rows = jnp.where((group >= reach) & (group < 2 * reach), got, rows)
            reach *= 2
        came.append(got)
        near.append(rows)
        sent = after(rows, far[-1]) if at else after(rows, *small)
        far.append(exchange(sent, "col", 2))

    near_twin = [exchange(piece, "col", 1) for piece in near]
    halved, density, slices = early(
        cuts, small[2], vir_energy, small[0], own, near, near_twin
    )
    far_twin = [exchange(piece, "col", 1) for piece in far[:-2]]
    far_twin += [exchange(after(piece, density), "col", 1) for piece in far[-2:]]

    middle, edge, half = row_count // 2, row_count - 1, nvir // 2
    others = [(at, 0, nvir) for at in range(1, edge) if at != middle]
    wanted = [(middle, 0, nvir), *others]
    wanted += [(edge, 0, half), (edge, half, half), (0, 0, nvir)]
    scale = 1.0 / (row_count * col_count)
    total, pieces = late(
        cuts, wanted, scale, small[3], vir_energy, small[1], halved, far, far_twin,
        density, slices,
    )
    ends = [exchange(piece, "row", cut[0]) for cut, piece in zip(wanted[:-3], pieces)]
    total = scatter_plane(scatter_chip(total))
    for bit in bits("row")[:-1]:
        total = total + exchange(total, "row", bit)
    ends.append(exchange(after(pieces[-3], total), "row", edge))
    total = after(total, *ends[:-1])
    total = total + exchange(total, "row", bits("row")[-1])
    ends.append(exchange(after(pieces[-2], total), "row", edge))
    total = gather_plane(after(total, ends[-2]))
    ends.append(pieces[-1])

    returned = jnp.zeros_like(three_index)
    for (part, first, _), piece in zip(wanted, ends):
        returned = lax.dynamic_update_slice(returned, piece[None], (row ^ part, first, 0))
    return returned, total


def solution(mesh):
    placed = (P("col", None, "row"), P(), P(), P(), P("col", None))
    return jax.shard_map(
        on_device,
        mesh=mesh,
        in_specs=placed,
        out_specs=(P("col", None, "row"), P()),
        check_vma=False,
    )
```

```python
import functools

import jax
import jax.numpy as jnp
from jax import lax
from jax.experimental import pallas as pl
from jax.experimental.pallas import tpu as pltpu
from jax.sharding import PartitionSpec as P

BLOCK = 64
NPANEL = 4
TILE = 256
VMEM_LIMIT = 60 * 1024 * 1024
NT = (((1,), (1,)), ((), ()))


def staged(kernel, smalls, bigs, count, *refs):
    small, refs = refs[:smalls], refs[smalls:]
    sources, targets, scratch = refs[:bigs], refs[bigs : bigs + count], refs[bigs + count : -2]
    in_sem, out_sem = refs[-2:]
    held, made, own = scratch[:bigs], scratch[bigs : bigs + count], scratch[bigs + count :]
    loads = [
        pltpu.make_async_copy(source, target, in_sem.at[at])
        for at, (source, target) in enumerate(zip(sources, held))
    ]
    stores = [
        pltpu.make_async_copy(source, target, out_sem.at[at])
        for at, (source, target) in enumerate(zip(made, targets))
    ]
    for load in loads:
        load.start()
    kernel(small, held, made, own, [load.wait for load in loads], [store.start for store in stores])
    for store in stores:
        store.wait()


def call(kernel, name, outs, small, big, scratch):
    any_space = pl.BlockSpec(memory_space=pl.ANY)
    specs = [pl.BlockSpec(memory_space=pltpu.SMEM)]
    specs += [pl.BlockSpec(memory_space=pltpu.VMEM)] * (len(small) - 1)
    buffers = [pltpu.VMEM(at.shape, at.dtype) for at in [*big, *outs]]
    sems = [pltpu.SemaphoreType.DMA((len(big),)), pltpu.SemaphoreType.DMA((len(outs),))]
    return pl.pallas_call(
        functools.partial(staged, kernel, len(small), len(big), len(outs)),
        out_shape=outs,
        in_specs=specs + [any_space] * len(big),
        out_specs=[any_space] * len(outs),
        scratch_shapes=[*buffers, *scratch, *sems],
        compiler_params=pltpu.CompilerParams(vmem_limit_bytes=VMEM_LIMIT),
        cost_estimate=pl.CostEstimate(flops=0, bytes_accessed=0, transcendentals=0),
        name=name,
    )(*small, *big)


def shape(*sizes, kind=jnp.float32):
    return jax.ShapeDtypeStruct(sizes, kind)


def halves(value):
    high = value.astype(jnp.bfloat16)
    return high, (value - high.astype(jnp.float32)).astype(jnp.bfloat16)


def dot(left, right):
    return jnp.dot(left, right, preferred_element_type=jnp.float32)


def dot_nt(left, right):
    return lax.dot_general(left, right, NT, preferred_element_type=jnp.float32)


def split_rows(cuts, pieces, waits, mask, high, low):
    for (part, first, count), piece, wait in zip(cuts, pieces, waits):
        wait()
        width = piece.shape[1]
        cols = slice(part * width, (part + 1) * width)
        for start in range(0, count, BLOCK):
            at = first + start
            kept = mask[at // BLOCK : at // BLOCK + 1, cols]
            value = piece[start : start + BLOCK, :] * kept
            high[at : at + BLOCK, cols], low[at : at + BLOCK, cols] = halves(value)


def amplitudes(energy, live, vir_col, vir_row, own, panel, amp, a_parts, w_parts):
    nvir = amp.shape[0]
    for start in range(0, nvir, TILE):
        cols = slice(start, start + TILE)
        cross = dot_nt(own[0][...], panel[0][cols, :])
        cross += dot_nt(own[0][...], panel[1][cols, :])
        cross += dot_nt(own[1][...], panel[0][cols, :])
        value = cross / (energy - vir_col[...] - vir_row[:, cols]) * live
        amp[:, cols] = value
        a_parts[0][:, cols], a_parts[1][:, cols] = halves(value)
    for above in range(0, nvir, TILE):
        rows = slice(above, above + TILE)
        for start in range(0, nvir, TILE):
            cols = slice(start, start + TILE)
            value = 2.0 * amp[rows, cols] - amp[cols, rows].T
            w_parts[0][rows, cols], w_parts[1][rows, cols] = halves(value)


def respond(rows, w_parts, panel, cols):
    value = dot(w_parts[0][rows, :], panel[0][:, cols])
    value += dot(w_parts[0][rows, :], panel[1][:, cols])
    return value + dot(w_parts[1][rows, :], panel[0][:, cols])


def density_tile(cols, w_parts, a_parts):
    value = dot_nt(w_parts[0][...], a_parts[0][cols, :])
    value += dot_nt(w_parts[0][...], a_parts[1][cols, :])
    return value + dot_nt(w_parts[1][...], a_parts[0][cols, :])


def early_kernel(cuts, small, held, made, own_scratch, wait, give):
    scalars, vir_col, vir_row, masks = small
    count = len(cuts)
    own_high, own_low, density, *slices = made
    m_high, m_low, amp, a_high, a_low, w_high, w_low = own_scratch
    split_rows(cuts, held[:count], wait[:count], masks.at[0], own_high, own_low)
    give[0]()
    give[1]()
    nvir = amp.shape[0]
    panel, a_parts, w_parts = (m_high, m_low), (a_high, a_low), (w_high, w_low)
    for turn in range(2):
        where = slice((1 + turn) * count, (2 + turn) * count)
        split_rows(cuts, held[where], wait[where], masks.at[1 + turn], m_high, m_low)
        amplitudes(
            scalars[2 * turn], scalars[2 * turn + 1], vir_col, vir_row,
            (own_high, own_low), panel, amp, a_parts, w_parts,
        )
        for start in range(0, nvir, TILE):
            cols = slice(start, start + TILE)
            value = density_tile(cols, w_parts, a_parts)
            density[:, cols] = value if turn == 0 else density[:, cols] + value
        if turn:
            give[2]()
        for part, piece in enumerate(slices):
            width = piece.shape[1]
            cols = slice(part * width, (part + 1) * width)
            value = respond(slice(0, nvir), w_parts, panel, cols)
            piece[...] = value if turn == 0 else piece[...] + value
            if turn:
                give[3 + part]()


def squares(nvir, naux):
    half = jnp.bfloat16
    return [pltpu.VMEM((nvir, naux), half)] * 2, [pltpu.VMEM((nvir, nvir), half)] * 4


def early(cuts, scalars, virtual, masks, own, near, twin):
    nvir, width = own[0].shape
    naux = masks.shape[2]
    parts = naux // width
    outs = [shape(nvir, naux, kind=jnp.bfloat16)] * 2 + [shape(nvir, nvir)]
    outs += [shape(nvir, width)] * parts
    wide, square = squares(nvir, naux)
    small = [scalars, virtual[:, None], virtual[None, :], masks]
    kernel = functools.partial(early_kernel, cuts)
    scratch = [*wide, pltpu.VMEM((nvir, nvir), jnp.float32), *square]
    outs = call(kernel, "early", outs, small, [*own, *near, *twin], scratch)
    return outs[:2], outs[2], list(outs[3:])


def late_kernel(cuts, wanted, scale, small, held, made, own_scratch, wait, give):
    scalars, vir_col, vir_row, masks = small
    count = len(cuts)
    amp, panels = own_scratch[0], (own_scratch[1:7], own_scratch[7:])
    wait[0]()
    wait[1]()
    for turn, (m_high, m_low, a_high, a_low, w_high, w_low) in enumerate(panels):
        where = slice(2 + turn * count, 2 + (1 + turn) * count)
        split_rows(cuts, held[where], wait[where], masks.at[turn], m_high, m_low)
        amplitudes(
            scalars[2 * turn], scalars[2 * turn + 1], vir_col, vir_row,
            held[:2], (m_high, m_low), amp, (a_high, a_low), (w_high, w_low),
        )
    density, *slices = held[2 + 2 * count :]
    total, *pieces = made
    for ready in wait[2 + 2 * count :]:
        ready()
    for start in range(0, density.shape[0], TILE):
        cols = slice(start, start + TILE)
        value = density[:, cols]
        for _, _, a_high, a_low, w_high, w_low in panels:
            value += density_tile(cols, (w_high, w_low), (a_high, a_low))
        total[:, cols] = value * scale
    give[0]()
    for at, ((part, first, height), piece) in enumerate(zip(wanted, pieces)):
        rows = slice(first, first + height)
        width = piece.shape[1]
        cols = slice(part * width, (part + 1) * width)
        value = slices[part][rows, :]
        for m_high, m_low, _, _, w_high, w_low in panels:
            value += respond(rows, (w_high, w_low), (m_high, m_low), cols)
        piece[...] = value
        give[1 + at]()


def late(cuts, wanted, scale, scalars, virtual, masks, own, far, twin, density, slices):
    nvir, naux = own[0].shape
    width = slices[0].shape[1]
    outs = [shape(nvir, nvir)] + [shape(height, width) for _, _, height in wanted]
    wide, square = squares(nvir, naux)
    small = [scalars, virtual[:, None], virtual[None, :], masks]
    kernel = functools.partial(late_kernel, cuts, wanted, scale)
    scratch = [pltpu.VMEM((nvir, nvir), jnp.float32), *wide, *square, *wide, *square]
    big = [*own, *far, *twin, density, *slices]
    outs = call(kernel, "late", outs, small, big, scratch)
    return outs[0], list(outs[1:])


def exchange(value, axis, bit):
    size = lax.axis_size(axis)
    return lax.ppermute(value, axis, [(at, at ^ bit) for at in range(size)])


def after(value, *others):
    return lax.optimization_barrier((value, *others))[0]


def bits(axis):
    size = lax.axis_size(axis)
    return [1 << at for at in range(size.bit_length() - 1)]


def scatter_chip(value):
    half = value.shape[0] // 2
    side = lax.axis_index("col") % 2
    kept = lax.dynamic_slice_in_dim(value, side * half, half, 0)
    sent = lax.dynamic_slice_in_dim(value, (1 - side) * half, half, 0)
    return kept + exchange(sent, "col", 1)


def scatter_plane(value):
    place = lax.axis_index("col") // 2
    chips = lax.axis_size("col") // 2
    count = value.shape[0] // chips
    total = lax.dynamic_slice_in_dim(value, place * count, count, 0)
    for turn in range(1, chips):
        sent = lax.dynamic_slice_in_dim(value, (place ^ turn) * count, count, 0)
        total = total + exchange(sent, "col", 2 * turn)
    return total


def joined(terms, place):
    if len(terms) == 1:
        return terms[0]
    half = len(terms) // 2
    low, high = joined(terms[:half], place), joined(terms[half:], place)
    side = (place // half) % 2
    return jnp.where(side == 0, jnp.concatenate([low, high]), jnp.concatenate([high, low]))


def gather_plane(value):
    col = lax.axis_index("col")
    turns = range(1, lax.axis_size("col") // 2)
    terms = [value] + [exchange(value, "col", 2 * turn) for turn in turns]
    value = joined(terms, col // 2)
    return joined([value, exchange(value, "col", 1)], col)


def cut_list(nvir, row_count):
    return [(part, 0, nvir) for part in range(row_count)]


def on_device(three_index, occ_energy, vir_energy, block_mask, pair_list):
    row = lax.axis_index("row")
    col = lax.axis_index("col")
    row_count = lax.axis_size("row")
    col_count = lax.axis_size("col")
    position = col % NPANEL
    group = col // NPANEL
    groups = col_count // NPANEL
    nvir = three_index.shape[1]
    cuts = cut_list(nvir, row_count)

    own_orbital = col * row_count + row
    panels = [position ^ turn for turn in range(NPANEL)]
    orbitals = jnp.stack([own_orbital] + [at * row_count + row for at in panels])
    kept = block_mask[orbitals].reshape(NPANEL + 1, block_mask.shape[1], row_count, -1)
    kept = kept[:, :, row ^ jnp.arange(row_count), :].reshape(NPANEL + 1, kept.shape[1], -1)
    masks = jnp.repeat(kept.astype(jnp.float32), BLOCK, axis=-1)
    lists = pair_list[row]
    scalars = []
    for turn in range(NPANEL):
        live = jnp.any(lists == panels[turn]).astype(jnp.float32)
        scalars += [occ_energy[own_orbital] + occ_energy[orbitals[1 + turn]], live]
    small = masks[:3], masks[3:], jnp.stack(scalars[:4]), jnp.stack(scalars[4:])

    own, came, near, far = [], [], [], []

    def receive(at):
        part, first, count = cuts[at]
        rows = lax.dynamic_index_in_dim(three_index, row ^ part, 0, keepdims=False)
        rows = rows[first : first + count]
        if part == row_count - 1:
            rows = after(rows, near[0])
        elif part > 1:
            rows = after(rows, scalars[1])
        own.append(exchange(rows, "row", part) if part else rows)

    for at in range(len(cuts)):
        while len(own) < min(at + 1 if at > 1 else row_count - 1, len(cuts)):
            receive(len(own))
        rows = own[at]
        if at:
            rows = after(rows, came[-1])
        reach = 1
        while reach < groups:
            span = min(reach, groups - reach) * NPANEL
            links = [(one, one + reach * NPANEL) for one in range(span)]
            got = lax.ppermute(rows, "col", links)
            rows = jnp.where((group >= reach) & (group < 2 * reach), got, rows)
            reach *= 2
        came.append(got)
        near.append(rows)
        sent = after(rows, far[-1]) if at else after(rows, *small)
        far.append(exchange(sent, "col", 2))

    near_twin = [exchange(piece, "col", 1) for piece in near]
    halved, density, slices = early(
        cuts, small[2], vir_energy, small[0], own, near, near_twin
    )
    far_twin = [exchange(piece, "col", 1) for piece in far[:-1]]
    far_twin.append(exchange(after(far[-1], density), "col", 1))

    middle, edge, most = row_count // 2, row_count - 1, nvir // 4 * 3
    wanted = [(middle, 0, most), (middle, most, nvir - most)]
    wanted += [(at, 0, nvir) for at in range(row_count) if at != middle]
    scale = 1.0 / (row_count * col_count)
    total, pieces = late(
        cuts, wanted, scale, small[3], vir_energy, small[1], halved, far, far_twin,
        density, slices,
    )

    def leave(at, *others):
        return exchange(after(pieces[at], *others), "row", wanted[at][0])

    ends = [leave(0)]
    total = scatter_plane(scatter_chip(total))
    ends.append(leave(1, total))
    total = after(total, ends[0])
    for bit in bits("row")[:-1]:
        total = total + exchange(total, "row", bit)
    total = after(total, ends[1])
    ends.append(pieces[2])
    ends += [leave(at, total) for at in range(3, len(wanted) - 1)]
    total = total + exchange(total, "row", bits("row")[-1])
    ends.append(leave(len(wanted) - 1, total))
    total = gather_plane(total)

    returned = jnp.zeros_like(three_index)
    for (part, first, _), piece in zip(wanted, ends):
        returned = lax.dynamic_update_slice(returned, piece[None], (row ^ part, first, 0))
    return returned, total


def solution(mesh):
    placed = (P("col", None, "row"), P(), P(), P(), P("col", None))
    return jax.shard_map(
        on_device,
        mesh=mesh,
        in_specs=placed,
        out_specs=(P("col", None, "row"), P()),
        check_vma=False,
    )
```

```python
import functools

import jax
import jax.numpy as jnp
from jax import lax
from jax.experimental import pallas as pl
from jax.experimental.pallas import tpu as pltpu
from jax.sharding import PartitionSpec as P

BLOCK = 64
NPANEL = 4
TILE = 256
VMEM_LIMIT = 60 * 1024 * 1024
NT = (((1,), (1,)), ((), ()))


def staged(kernel, smalls, bigs, count, *refs):
    small, refs = refs[:smalls], refs[smalls:]
    sources, targets, scratch = refs[:bigs], refs[bigs : bigs + count], refs[bigs + count : -2]
    in_sem, out_sem = refs[-2:]
    held, made, own = scratch[:bigs], scratch[bigs : bigs + count], scratch[bigs + count :]
    loads = [
        pltpu.make_async_copy(source, target, in_sem.at[at])
        for at, (source, target) in enumerate(zip(sources, held))
    ]
    stores = [
        pltpu.make_async_copy(source, target, out_sem.at[at])
        for at, (source, target) in enumerate(zip(made, targets))
    ]
    kernel(small, held, made, own, loads, [store.start for store in stores])
    for store in stores:
        store.wait()


def call(kernel, name, outs, small, big, scratch):
    any_space = pl.BlockSpec(memory_space=pl.ANY)
    specs = [pl.BlockSpec(memory_space=pltpu.SMEM)]
    specs += [pl.BlockSpec(memory_space=pltpu.VMEM)] * (len(small) - 1)
    buffers = [pltpu.VMEM(at.shape, at.dtype) for at in [*big, *outs]]
    sems = [pltpu.SemaphoreType.DMA((len(big),)), pltpu.SemaphoreType.DMA((len(outs),))]
    return pl.pallas_call(
        functools.partial(staged, kernel, len(small), len(big), len(outs)),
        out_shape=outs,
        in_specs=specs + [any_space] * len(big),
        out_specs=[any_space] * len(outs),
        scratch_shapes=[*buffers, *scratch, *sems],
        compiler_params=pltpu.CompilerParams(vmem_limit_bytes=VMEM_LIMIT),
        cost_estimate=pl.CostEstimate(flops=0, bytes_accessed=0, transcendentals=0),
        name=name,
    )(*small, *big)


def shape(*sizes, kind=jnp.float32):
    return jax.ShapeDtypeStruct(sizes, kind)


def halves(value):
    high = value.astype(jnp.bfloat16)
    return high, (value - high.astype(jnp.float32)).astype(jnp.bfloat16)


def dot(left, right):
    return jnp.dot(left, right, preferred_element_type=jnp.float32)


def dot_nt(left, right):
    return lax.dot_general(left, right, NT, preferred_element_type=jnp.float32)


def begin(loads):
    for load in loads:
        load.start()


def split_rows(cuts, pieces, loads, mask, high, low):
    for (part, first, count), piece, load in zip(cuts, pieces, loads):
        load.wait()
        width = piece.shape[1]
        cols = slice(part * width, (part + 1) * width)
        for start in range(0, count, BLOCK):
            at = first + start
            kept = mask[at // BLOCK : at // BLOCK + 1, cols]
            value = piece[start : start + BLOCK, :] * kept
            high[at : at + BLOCK, cols], low[at : at + BLOCK, cols] = halves(value)


def amplitudes(energy, live, vir_col, vir_row, own, panel, amp, a_parts, w_parts):
    nvir = amp.shape[0]
    for start in range(0, nvir, TILE):
        cols = slice(start, start + TILE)
        cross = dot_nt(own[0][...], panel[0][cols, :])
        cross += dot_nt(own[0][...], panel[1][cols, :])
        cross += dot_nt(own[1][...], panel[0][cols, :])
        value = cross / (energy - vir_col[...] - vir_row[:, cols]) * live
        amp[:, cols] = value
        a_parts[0][:, cols], a_parts[1][:, cols] = halves(value)
    for above in range(0, nvir, TILE):
        rows = slice(above, above + TILE)
        for start in range(0, nvir, TILE):
            cols = slice(start, start + TILE)
            value = 2.0 * amp[rows, cols] - amp[cols, rows].T
            w_parts[0][rows, cols], w_parts[1][rows, cols] = halves(value)


def respond(rows, w_parts, panel, cols):
    value = dot(w_parts[0][rows, :], panel[0][:, cols])
    value += dot(w_parts[0][rows, :], panel[1][:, cols])
    return value + dot(w_parts[1][rows, :], panel[0][:, cols])


def density_tile(cols, w_parts, a_parts):
    value = dot_nt(w_parts[0][...], a_parts[0][cols, :])
    value += dot_nt(w_parts[0][...], a_parts[1][cols, :])
    return value + dot_nt(w_parts[1][...], a_parts[0][cols, :])


def early_kernel(cuts, small, held, made, own_scratch, loads, give):
    scalars, vir_col, vir_row, masks = small
    count = len(cuts)
    own_high, own_low, density, *slices = made
    m_high, m_low, amp, a_high, a_low, w_high, w_low = own_scratch
    begin(loads[: 2 * count])
    split_rows(cuts, held[:count], loads[:count], masks.at[0], own_high, own_low)
    begin(loads[2 * count :])
    give[0]()
    give[1]()
    nvir = amp.shape[0]
    panel, a_parts, w_parts = (m_high, m_low), (a_high, a_low), (w_high, w_low)
    for turn in range(2):
        where = slice((1 + turn) * count, (2 + turn) * count)
        split_rows(cuts, held[where], loads[where], masks.at[1 + turn], m_high, m_low)
        amplitudes(
            scalars[2 * turn], scalars[2 * turn + 1], vir_col, vir_row,
            (own_high, own_low), panel, amp, a_parts, w_parts,
        )
        for start in range(0, nvir, TILE):
            cols = slice(start, start + TILE)
            value = density_tile(cols, w_parts, a_parts)
            density[:, cols] = value if turn == 0 else density[:, cols] + value
        if turn:
            give[2]()
        for part, piece in enumerate(slices):
            width = piece.shape[1]
            cols = slice(part * width, (part + 1) * width)
            value = respond(slice(0, nvir), w_parts, panel, cols)
            piece[...] = value if turn == 0 else piece[...] + value
            if turn:
                give[3 + part]()


def squares(nvir, naux):
    half = jnp.bfloat16
    return [pltpu.VMEM((nvir, naux), half)] * 2, [pltpu.VMEM((nvir, nvir), half)] * 4


def early(cuts, scalars, virtual, masks, own, near, twin):
    nvir, width = own[0].shape
    naux = masks.shape[2]
    parts = naux // width
    outs = [shape(nvir, naux, kind=jnp.bfloat16)] * 2 + [shape(nvir, nvir)]
    outs += [shape(nvir, width)] * parts
    wide, square = squares(nvir, naux)
    small = [scalars, virtual[:, None], virtual[None, :], masks]
    kernel = functools.partial(early_kernel, cuts)
    scratch = [*wide, pltpu.VMEM((nvir, nvir), jnp.float32), *square]
    outs = call(kernel, "early", outs, small, [*own, *near, *twin], scratch)
    return outs[:2], outs[2], list(outs[3:])


def late_kernel(cuts, wanted, scale, small, held, made, own_scratch, loads, give):
    scalars, vir_col, vir_row, masks = small
    count = len(cuts)
    amp, panels = own_scratch[0], (own_scratch[1:7], own_scratch[7:])
    begin(loads[: 2 + count])
    for turn, (m_high, m_low, a_high, a_low, w_high, w_low) in enumerate(panels):
        where = slice(2 + turn * count, 2 + (1 + turn) * count)
        split_rows(cuts, held[where], loads[where], masks.at[turn], m_high, m_low)
        if turn == 0:
            loads[0].wait()
            loads[1].wait()
            begin(loads[2 + count :])
        amplitudes(
            scalars[2 * turn], scalars[2 * turn + 1], vir_col, vir_row,
            held[:2], (m_high, m_low), amp, (a_high, a_low), (w_high, w_low),
        )
    density, *slices = held[2 + 2 * count :]
    total, *pieces = made
    for load in loads[2 + 2 * count :]:
        load.wait()
    for start in range(0, density.shape[0], TILE):
        cols = slice(start, start + TILE)
        value = density[:, cols]
        for _, _, a_high, a_low, w_high, w_low in panels:
            value += density_tile(cols, (w_high, w_low), (a_high, a_low))
        total[:, cols] = value * scale
    give[0]()
    for at, ((part, first, height), piece) in enumerate(zip(wanted, pieces)):
        rows = slice(first, first + height)
        width = piece.shape[1]
        cols = slice(part * width, (part + 1) * width)
        value = slices[part][rows, :]
        for m_high, m_low, _, _, w_high, w_low in panels:
            value += respond(rows, (w_high, w_low), (m_high, m_low), cols)
        piece[...] = value
        give[1 + at]()


def late(cuts, wanted, scale, scalars, virtual, masks, own, far, twin, density, slices):
    nvir, naux = own[0].shape
    width = slices[0].shape[1]
    outs = [shape(nvir, nvir)] + [shape(height, width) for _, _, height in wanted]
    wide, square = squares(nvir, naux)
    small = [scalars, virtual[:, None], virtual[None, :], masks]
    kernel = functools.partial(late_kernel, cuts, wanted, scale)
    scratch = [pltpu.VMEM((nvir, nvir), jnp.float32), *wide, *square, *wide, *square]
    big = [*own, *far, *twin, density, *slices]
    outs = call(kernel, "late", outs, small, big, scratch)
    return outs[0], list(outs[1:])


def exchange(value, axis, bit):
    size = lax.axis_size(axis)
    return lax.ppermute(value, axis, [(at, at ^ bit) for at in range(size)])


def after(value, *others):
    return lax.optimization_barrier((value, *others))[0]


def bits(axis):
    size = lax.axis_size(axis)
    return [1 << at for at in range(size.bit_length() - 1)]


def scatter_chip(value):
    half = value.shape[0] // 2
    side = lax.axis_index("col") % 2
    kept = lax.dynamic_slice_in_dim(value, side * half, half, 0)
    sent = lax.dynamic_slice_in_dim(value, (1 - side) * half, half, 0)
    return kept + exchange(sent, "col", 1)


def scatter_plane(value):
    place = lax.axis_index("col") // 2
    chips = lax.axis_size("col") // 2
    count = value.shape[0] // chips
    total = lax.dynamic_slice_in_dim(value, place * count, count, 0)
    for turn in range(1, chips):
        sent = lax.dynamic_slice_in_dim(value, (place ^ turn) * count, count, 0)
        total = total + exchange(sent, "col", 2 * turn)
    return total


def joined(terms, place):
    if len(terms) == 1:
        return terms[0]
    half = len(terms) // 2
    low, high = joined(terms[:half], place), joined(terms[half:], place)
    side = (place // half) % 2
    return jnp.where(side == 0, jnp.concatenate([low, high]), jnp.concatenate([high, low]))


def gather_plane(value):
    col = lax.axis_index("col")
    turns = range(1, lax.axis_size("col") // 2)
    terms = [value] + [exchange(value, "col", 2 * turn) for turn in turns]
    value = joined(terms, col // 2)
    return joined([value, exchange(value, "col", 1)], col)


def cut_list(nvir, row_count):
    return [(part, 0, nvir) for part in range(row_count)]


def on_device(three_index, occ_energy, vir_energy, block_mask, pair_list):
    row = lax.axis_index("row")
    col = lax.axis_index("col")
    row_count = lax.axis_size("row")
    col_count = lax.axis_size("col")
    position = col % NPANEL
    group = col // NPANEL
    groups = col_count // NPANEL
    nvir = three_index.shape[1]
    cuts = cut_list(nvir, row_count)

    own_orbital = col * row_count + row
    panels = [position ^ turn for turn in range(NPANEL)]
    orbitals = jnp.stack([own_orbital] + [at * row_count + row for at in panels])
    kept = block_mask[orbitals].reshape(NPANEL + 1, block_mask.shape[1], row_count, -1)
    kept = kept[:, :, row ^ jnp.arange(row_count), :].reshape(NPANEL + 1, kept.shape[1], -1)
    masks = jnp.repeat(kept.astype(jnp.float32), BLOCK, axis=-1)
    lists = pair_list[row]
    scalars = []
    for turn in range(NPANEL):
        live = jnp.any(lists == panels[turn]).astype(jnp.float32)
        scalars += [occ_energy[own_orbital] + occ_energy[orbitals[1 + turn]], live]
    small = masks[:3], masks[3:], jnp.stack(scalars[:4]), jnp.stack(scalars[4:])

    own, came, near, far = [], [], [], []

    def receive(at):
        part, first, count = cuts[at]
        rows = lax.dynamic_index_in_dim(three_index, row ^ part, 0, keepdims=False)
        rows = rows[first : first + count]
        if part == row_count - 1:
            rows = after(rows, near[0])
        elif part > 1:
            rows = after(rows, scalars[1])
        own.append(exchange(rows, "row", part) if part else rows)

    for at in range(len(cuts)):
        while len(own) < min(at + 1 if at > 1 else row_count - 1, len(cuts)):
            receive(len(own))
        rows = own[at]
        if at:
            rows = after(rows, came[-1])
        reach = 1
        while reach < groups:
            span = min(reach, groups - reach) * NPANEL
            links = [(one, one + reach * NPANEL) for one in range(span)]
            got = lax.ppermute(rows, "col", links)
            rows = jnp.where((group >= reach) & (group < 2 * reach), got, rows)
            reach *= 2
        came.append(got)
        near.append(rows)
        sent = after(rows, far[-1]) if at else after(rows, *small)
        far.append(exchange(sent, "col", 2))

    near_twin = [exchange(piece, "col", 1) for piece in near]
    halved, density, slices = early(
        cuts, small[2], vir_energy, small[0], own, near, near_twin
    )
    far_twin = [exchange(piece, "col", 1) for piece in far[:-1]]
    far_twin.append(exchange(after(far[-1], density), "col", 1))

    middle, edge, most = row_count // 2, row_count - 1, nvir // 4 * 3
    wanted = [(middle, 0, most), (middle, most, nvir - most)]
    wanted += [(edge, at, nvir // 2) for at in (0, nvir // 2)]
    wanted += [(at, 0, nvir) for at in range(edge) if at != middle]
    scale = 1.0 / (row_count * col_count)
    total, pieces = late(
        cuts, wanted, scale, small[3], vir_energy, small[1], halved, far, far_twin,
        density, slices,
    )

    def leave(at, *others):
        return exchange(after(pieces[at], *others), "row", wanted[at][0])

    ends = [leave(0)]
    total = scatter_plane(scatter_chip(total))
    ends += [leave(1, total), leave(2, total)]
    total = after(total, ends[0])
    for bit in bits("row")[:-1]:
        total = total + exchange(total, "row", bit)
    total = after(total, ends[1])
    others = [leave(at, total) for at in range(5, len(wanted))]
    total = total + exchange(total, "row", bits("row")[-1])
    ends += [leave(3, total), pieces[4], *others]
    total = gather_plane(after(total, ends[2]))

    returned = jnp.zeros_like(three_index)
    for (part, first, _), piece in zip(wanted, ends):
        returned = lax.dynamic_update_slice(returned, piece[None], (row ^ part, first, 0))
    return returned, total


def solution(mesh):
    placed = (P("col", None, "row"), P(), P(), P(), P("col", None))
    return jax.shard_map(
        on_device,
        mesh=mesh,
        in_specs=placed,
        out_specs=(P("col", None, "row"), P()),
        check_vma=False,
    )
```

```python
import functools

import jax
import jax.numpy as jnp
from jax import lax
from jax.experimental import pallas as pl
from jax.experimental.pallas import tpu as pltpu
from jax.sharding import PartitionSpec as P

BLOCK = 64
NPANEL = 4
TILE = 256
VMEM_LIMIT = 60 * 1024 * 1024
NT = (((1,), (1,)), ((), ()))


def staged(kernel, smalls, bigs, count, *refs):
    small, refs = refs[:smalls], refs[smalls:]
    sources, targets, scratch = refs[:bigs], refs[bigs : bigs + count], refs[bigs + count : -2]
    in_sem, out_sem = refs[-2:]
    held, made, own = scratch[:bigs], scratch[bigs : bigs + count], scratch[bigs + count :]
    loads = [
        pltpu.make_async_copy(source, target, in_sem.at[at])
        for at, (source, target) in enumerate(zip(sources, held))
    ]
    stores = [
        pltpu.make_async_copy(source, target, out_sem.at[at])
        for at, (source, target) in enumerate(zip(made, targets))
    ]
    kernel(small, held, made, own, loads, [store.start for store in stores])
    for store in stores:
        store.wait()


def call(kernel, name, outs, small, big, scratch):
    any_space = pl.BlockSpec(memory_space=pl.ANY)
    specs = [pl.BlockSpec(memory_space=pltpu.SMEM)]
    specs += [pl.BlockSpec(memory_space=pltpu.VMEM)] * (len(small) - 1)
    buffers = [pltpu.VMEM(at.shape, at.dtype) for at in [*big, *outs]]
    sems = [pltpu.SemaphoreType.DMA((len(big),)), pltpu.SemaphoreType.DMA((len(outs),))]
    return pl.pallas_call(
        functools.partial(staged, kernel, len(small), len(big), len(outs)),
        out_shape=outs,
        in_specs=specs + [any_space] * len(big),
        out_specs=[any_space] * len(outs),
        scratch_shapes=[*buffers, *scratch, *sems],
        compiler_params=pltpu.CompilerParams(vmem_limit_bytes=VMEM_LIMIT),
        cost_estimate=pl.CostEstimate(flops=0, bytes_accessed=0, transcendentals=0),
        name=name,
    )(*small, *big)


def shape(*sizes, kind=jnp.float32):
    return jax.ShapeDtypeStruct(sizes, kind)


def halves(value):
    high = value.astype(jnp.bfloat16)
    return high, (value - high.astype(jnp.float32)).astype(jnp.bfloat16)


def dot(left, right):
    return jnp.dot(left, right, preferred_element_type=jnp.float32)


def dot_nt(left, right):
    return lax.dot_general(left, right, NT, preferred_element_type=jnp.float32)


def begin(loads):
    for load in loads:
        load.start()


def split_rows(cuts, pieces, loads, mask, high, low):
    for (part, first, count), piece, load in zip(cuts, pieces, loads):
        load.wait()
        width = piece.shape[1]
        cols = slice(part * width, (part + 1) * width)
        for start in range(0, count, BLOCK):
            at = first + start
            kept = mask[at // BLOCK : at // BLOCK + 1, cols]
            value = piece[start : start + BLOCK, :] * kept
            high[at : at + BLOCK, cols], low[at : at + BLOCK, cols] = halves(value)


def amplitudes(energy, live, vir_col, vir_row, own, panel, amp, a_parts, w_parts):
    nvir = amp.shape[0]
    for start in range(0, nvir, TILE):
        cols = slice(start, start + TILE)
        cross = dot_nt(own[0][...], panel[0][cols, :])
        cross += dot_nt(own[0][...], panel[1][cols, :])
        cross += dot_nt(own[1][...], panel[0][cols, :])
        value = cross / (energy - vir_col[...] - vir_row[:, cols]) * live
        amp[:, cols] = value
        a_parts[0][:, cols], a_parts[1][:, cols] = halves(value)
    for above in range(0, nvir, TILE):
        rows = slice(above, above + TILE)
        for start in range(0, nvir, TILE):
            cols = slice(start, start + TILE)
            value = 2.0 * amp[rows, cols] - amp[cols, rows].T
            w_parts[0][rows, cols], w_parts[1][rows, cols] = halves(value)


def respond(rows, w_parts, panel, cols):
    value = dot(w_parts[0][rows, :], panel[0][:, cols])
    value += dot(w_parts[0][rows, :], panel[1][:, cols])
    return value + dot(w_parts[1][rows, :], panel[0][:, cols])


def density_tile(cols, w_parts, a_parts):
    value = dot_nt(w_parts[0][...], a_parts[0][cols, :])
    value += dot_nt(w_parts[0][...], a_parts[1][cols, :])
    return value + dot_nt(w_parts[1][...], a_parts[0][cols, :])


def early_kernel(cuts, small, held, made, own_scratch, loads, give):
    scalars, vir_col, vir_row, masks = small
    count = len(cuts)
    own_high, own_low, density, *slices = made
    m_high, m_low, amp, a_high, a_low, w_high, w_low = own_scratch
    begin(loads[: 2 * count])
    split_rows(cuts, held[:count], loads[:count], masks.at[0], own_high, own_low)
    begin(loads[2 * count :])
    give[0]()
    give[1]()
    nvir = amp.shape[0]
    panel, a_parts, w_parts = (m_high, m_low), (a_high, a_low), (w_high, w_low)
    for turn in range(2):
        where = slice((1 + turn) * count, (2 + turn) * count)
        split_rows(cuts, held[where], loads[where], masks.at[1 + turn], m_high, m_low)
        amplitudes(
            scalars[2 * turn], scalars[2 * turn + 1], vir_col, vir_row,
            (own_high, own_low), panel, amp, a_parts, w_parts,
        )
        for start in range(0, nvir, TILE):
            cols = slice(start, start + TILE)
            value = density_tile(cols, w_parts, a_parts)
            density[:, cols] = value if turn == 0 else density[:, cols] + value
        if turn:
            give[2]()
        for part, piece in enumerate(slices):
            width = piece.shape[1]
            cols = slice(part * width, (part + 1) * width)
            value = respond(slice(0, nvir), w_parts, panel, cols)
            piece[...] = value if turn == 0 else piece[...] + value
            if turn:
                give[3 + part]()


def squares(nvir, naux):
    half = jnp.bfloat16
    return [pltpu.VMEM((nvir, naux), half)] * 2, [pltpu.VMEM((nvir, nvir), half)] * 4


def early(cuts, scalars, virtual, masks, own, near, twin):
    nvir, width = own[0].shape
    naux = masks.shape[2]
    parts = naux // width
    outs = [shape(nvir, naux, kind=jnp.bfloat16)] * 2 + [shape(nvir, nvir)]
    outs += [shape(nvir, width)] * parts
    wide, square = squares(nvir, naux)
    small = [scalars, virtual[:, None], virtual[None, :], masks]
    kernel = functools.partial(early_kernel, cuts)
    scratch = [*wide, pltpu.VMEM((nvir, nvir), jnp.float32), *square]
    outs = call(kernel, "early", outs, small, [*own, *near, *twin], scratch)
    return outs[:2], outs[2], list(outs[3:])


def late_kernel(cuts, wanted, scale, small, held, made, own_scratch, loads, give):
    scalars, vir_col, vir_row, masks = small
    count = len(cuts)
    amp, panels = own_scratch[0], (own_scratch[1:7], own_scratch[7:])
    begin(loads[: 2 + count])
    for turn, (m_high, m_low, a_high, a_low, w_high, w_low) in enumerate(panels):
        where = slice(2 + turn * count, 2 + (1 + turn) * count)
        split_rows(cuts, held[where], loads[where], masks.at[turn], m_high, m_low)
        if turn == 0:
            loads[0].wait()
            loads[1].wait()
            begin(loads[2 + count :])
        amplitudes(
            scalars[2 * turn], scalars[2 * turn + 1], vir_col, vir_row,
            held[:2], (m_high, m_low), amp, (a_high, a_low), (w_high, w_low),
        )
    density, *slices = held[2 + 2 * count :]
    total, *pieces = made
    for load in loads[2 + 2 * count :]:
        load.wait()
    for start in range(0, density.shape[0], TILE):
        cols = slice(start, start + TILE)
        value = density[:, cols]
        for _, _, a_high, a_low, w_high, w_low in panels:
            value += density_tile(cols, (w_high, w_low), (a_high, a_low))
        total[:, cols] = value * scale
    give[0]()
    for at, ((part, first, height), piece) in enumerate(zip(wanted, pieces)):
        rows = slice(first, first + height)
        width = piece.shape[1]
        cols = slice(part * width, (part + 1) * width)
        value = slices[part][rows, :]
        for m_high, m_low, _, _, w_high, w_low in panels:
            value += respond(rows, (w_high, w_low), (m_high, m_low), cols)
        piece[...] = value
        give[1 + at]()


def late(cuts, wanted, scale, scalars, virtual, masks, own, far, twin, density, slices):
    nvir, naux = own[0].shape
    width = slices[0].shape[1]
    outs = [shape(nvir, nvir)] + [shape(height, width) for _, _, height in wanted]
    wide, square = squares(nvir, naux)
    small = [scalars, virtual[:, None], virtual[None, :], masks]
    kernel = functools.partial(late_kernel, cuts, wanted, scale)
    scratch = [pltpu.VMEM((nvir, nvir), jnp.float32), *wide, *square, *wide, *square]
    big = [*own, *far, *twin, density, *slices]
    outs = call(kernel, "late", outs, small, big, scratch)
    return outs[0], list(outs[1:])


def exchange(value, axis, bit):
    size = lax.axis_size(axis)
    return lax.ppermute(value, axis, [(at, at ^ bit) for at in range(size)])


def after(value, *others):
    return lax.optimization_barrier((value, *others))[0]


def across(value, inner):
    edge = lax.axis_size("row") - 1
    pairs = [(at, edge - at) for at in range(edge + 1)]
    return lax.ppermute(value, "row", [at for at in pairs if (abs(at[0] - at[1]) == 1) == inner])


def bits(axis):
    size = lax.axis_size(axis)
    return [1 << at for at in range(size.bit_length() - 1)]


def scatter_chip(value):
    half = value.shape[0] // 2
    side = lax.axis_index("col") % 2
    kept = lax.dynamic_slice_in_dim(value, side * half, half, 0)
    sent = lax.dynamic_slice_in_dim(value, (1 - side) * half, half, 0)
    return kept + exchange(sent, "col", 1)


def scatter_plane(value):
    place = lax.axis_index("col") // 2
    chips = lax.axis_size("col") // 2
    count = value.shape[0] // chips
    total = lax.dynamic_slice_in_dim(value, place * count, count, 0)
    for turn in range(1, chips):
        sent = lax.dynamic_slice_in_dim(value, (place ^ turn) * count, count, 0)
        total = total + exchange(sent, "col", 2 * turn)
    return total


def joined(terms, place):
    if len(terms) == 1:
        return terms[0]
    half = len(terms) // 2
    low, high = joined(terms[:half], place), joined(terms[half:], place)
    side = (place // half) % 2
    return jnp.where(side == 0, jnp.concatenate([low, high]), jnp.concatenate([high, low]))


def gather_plane(value):
    col = lax.axis_index("col")
    turns = range(1, lax.axis_size("col") // 2)
    terms = [value] + [exchange(value, "col", 2 * turn) for turn in turns]
    value = joined(terms, col // 2)
    return joined([value, exchange(value, "col", 1)], col)


def cut_list(nvir, row_count):
    return [(part, 0, nvir) for part in (0, 1, row_count - 1, *range(2, row_count - 1))]


def on_device(three_index, occ_energy, vir_energy, block_mask, pair_list):
    row = lax.axis_index("row")
    col = lax.axis_index("col")
    row_count = lax.axis_size("row")
    col_count = lax.axis_size("col")
    position = col % NPANEL
    group = col // NPANEL
    groups = col_count // NPANEL
    nvir = three_index.shape[1]
    cuts = cut_list(nvir, row_count)

    own_orbital = col * row_count + row
    panels = [position ^ turn for turn in range(NPANEL)]
    orbitals = jnp.stack([own_orbital] + [at * row_count + row for at in panels])
    kept = block_mask[orbitals].reshape(NPANEL + 1, block_mask.shape[1], row_count, -1)
    kept = kept[:, :, row ^ jnp.arange(row_count), :].reshape(NPANEL + 1, kept.shape[1], -1)
    masks = jnp.repeat(kept.astype(jnp.float32), BLOCK, axis=-1)
    lists = pair_list[row]
    scalars = []
    for turn in range(NPANEL):
        live = jnp.any(lists == panels[turn]).astype(jnp.float32)
        scalars += [occ_energy[own_orbital] + occ_energy[orbitals[1 + turn]], live]
    small = masks[:3], masks[3:], jnp.stack(scalars[:4]), jnp.stack(scalars[4:])

    own, came, near, far = [], [], [], []

    def receive(at):
        part = cuts[at][0]
        rows = lax.dynamic_index_in_dim(three_index, row ^ part, 0, keepdims=False)
        if part == row_count - 1:
            rows = across(rows, True) + across(after(rows, scalars[1]), False)
        elif part:
            rows = exchange(after(rows, *near[:1]), "row", part)
        own.append(rows)

    for at in range(len(cuts)):
        while len(own) < (len(cuts) if at else 3):
            receive(len(own))
        rows = own[at]
        if at:
            rows = after(rows, came[-1])
        reach = 1
        while reach < groups:
            span = min(reach, groups - reach) * NPANEL
            links = [(one, one + reach * NPANEL) for one in range(span)]
            got = lax.ppermute(rows, "col", links)
            rows = jnp.where((group >= reach) & (group < 2 * reach), got, rows)
            reach *= 2
        came.append(got)
        near.append(rows)
        sent = after(rows, far[-1]) if at else after(rows, *small)
        far.append(exchange(sent, "col", 2))

    near_twin = [exchange(piece, "col", 1) for piece in near]
    halved, density, slices = early(
        cuts, small[2], vir_energy, small[0], own, near, near_twin
    )
    far_twin = [exchange(piece, "col", 1) for piece in far[:-1]]
    far_twin.append(exchange(after(far[-1], density), "col", 1))

    wanted = [cuts[at] for at in (2, 1, *range(3, len(cuts)), 0)]
    scale = 1.0 / (row_count * col_count)
    total, pieces = late(
        cuts, wanted, scale, small[3], vir_energy, small[1], halved, far, far_twin,
        density, slices,
    )

    inner, first = across(pieces[0], True), exchange(pieces[1], "row", 1)
    total = scatter_plane(scatter_chip(total))
    outer = across(after(pieces[0], total), False)
    total = after(total, inner, first)
    for bit in bits("row")[:-1]:
        total = total + exchange(total, "row", bit)
    others = [
        exchange(after(piece, total), "row", cut[0])
        for cut, piece in zip(wanted[2:-1], pieces[2:-1])
    ]
    total = total + exchange(total, "row", bits("row")[-1])
    total = gather_plane(after(total, outer))
    ends = [inner + outer, first, *others, pieces[-1]]

    returned = jnp.zeros_like(three_index)
    for (part, first, _), piece in zip(wanted, ends):
        returned = lax.dynamic_update_slice(returned, piece[None], (row ^ part, first, 0))
    return returned, total


def solution(mesh):
    placed = (P("col", None, "row"), P(), P(), P(), P("col", None))
    return jax.shard_map(
        on_device,
        mesh=mesh,
        in_specs=placed,
        out_specs=(P("col", None, "row"), P()),
        check_vma=False,
    )
```

```python
import functools

import jax
import jax.numpy as jnp
from jax import lax
from jax.experimental import pallas as pl
from jax.experimental.pallas import tpu as pltpu
from jax.sharding import PartitionSpec as P

BLOCK = 64
NPANEL = 4
TILE = 256
VMEM_LIMIT = 60 * 1024 * 1024
NT = (((1,), (1,)), ((), ()))


def staged(kernel, smalls, bigs, count, *refs):
    small, refs = refs[:smalls], refs[smalls:]
    sources, targets, scratch = refs[:bigs], refs[bigs : bigs + count], refs[bigs + count : -2]
    in_sem, out_sem = refs[-2:]
    held, made, own = scratch[:bigs], scratch[bigs : bigs + count], scratch[bigs + count :]
    loads = [
        pltpu.make_async_copy(source, target, in_sem.at[at])
        for at, (source, target) in enumerate(zip(sources, held))
    ]
    stores = [
        pltpu.make_async_copy(source, target, out_sem.at[at])
        for at, (source, target) in enumerate(zip(made, targets))
    ]
    kernel(small, held, made, own, loads, [store.start for store in stores])
    for store in stores:
        store.wait()


def call(kernel, name, outs, small, big, scratch):
    any_space = pl.BlockSpec(memory_space=pl.ANY)
    specs = [pl.BlockSpec(memory_space=pltpu.SMEM)]
    specs += [pl.BlockSpec(memory_space=pltpu.VMEM)] * (len(small) - 1)
    buffers = [pltpu.VMEM(at.shape, at.dtype) for at in [*big, *outs]]
    sems = [pltpu.SemaphoreType.DMA((len(big),)), pltpu.SemaphoreType.DMA((len(outs),))]
    return pl.pallas_call(
        functools.partial(staged, kernel, len(small), len(big), len(outs)),
        out_shape=outs,
        in_specs=specs + [any_space] * len(big),
        out_specs=[any_space] * len(outs),
        scratch_shapes=[*buffers, *scratch, *sems],
        compiler_params=pltpu.CompilerParams(vmem_limit_bytes=VMEM_LIMIT),
        cost_estimate=pl.CostEstimate(flops=0, bytes_accessed=0, transcendentals=0),
        name=name,
    )(*small, *big)


def shape(*sizes, kind=jnp.float32):
    return jax.ShapeDtypeStruct(sizes, kind)


def halves(value):
    high = value.astype(jnp.bfloat16)
    return high, (value - high.astype(jnp.float32)).astype(jnp.bfloat16)


def dot(left, right):
    return jnp.dot(left, right, preferred_element_type=jnp.float32)


def dot_nt(left, right):
    return lax.dot_general(left, right, NT, preferred_element_type=jnp.float32)


def begin(loads):
    for load in loads:
        load.start()


def split_rows(cuts, pieces, loads, mask, high, low):
    for (part, first, count), piece, load in zip(cuts, pieces, loads):
        load.wait()
        width = piece.shape[1]
        cols = slice(part * width, (part + 1) * width)
        for start in range(0, count, BLOCK):
            at = first + start
            kept = mask[at // BLOCK : at // BLOCK + 1, cols]
            value = piece[start : start + BLOCK, :] * kept
            high[at : at + BLOCK, cols], low[at : at + BLOCK, cols] = halves(value)


def amplitudes(energy, live, vir_col, vir_row, own, panel, amp, a_parts, w_parts):
    nvir = amp.shape[0]
    for start in range(0, nvir, TILE):
        cols = slice(start, start + TILE)
        cross = dot_nt(own[0][...], panel[0][cols, :])
        cross += dot_nt(own[0][...], panel[1][cols, :])
        cross += dot_nt(own[1][...], panel[0][cols, :])
        value = cross / (energy - vir_col[...] - vir_row[:, cols]) * live
        amp[:, cols] = value
        a_parts[0][:, cols], a_parts[1][:, cols] = halves(value)
    for above in range(0, nvir, TILE):
        rows = slice(above, above + TILE)
        for start in range(0, nvir, TILE):
            cols = slice(start, start + TILE)
            value = 2.0 * amp[rows, cols] - amp[cols, rows].T
            w_parts[0][rows, cols], w_parts[1][rows, cols] = halves(value)


def respond(rows, w_parts, panel, cols):
    value = dot(w_parts[0][rows, :], panel[0][:, cols])
    value += dot(w_parts[0][rows, :], panel[1][:, cols])
    return value + dot(w_parts[1][rows, :], panel[0][:, cols])


def density_tile(cols, w_parts, a_parts):
    value = dot_nt(w_parts[0][...], a_parts[0][cols, :])
    value += dot_nt(w_parts[0][...], a_parts[1][cols, :])
    return value + dot_nt(w_parts[1][...], a_parts[0][cols, :])


def early_kernel(cuts, small, held, made, own_scratch, loads, give):
    scalars, vir_col, vir_row, masks = small
    count = len(cuts)
    own_high, own_low, density, *slices = made
    m_high, m_low, amp, a_high, a_low, w_high, w_low = own_scratch
    begin(loads[: 2 * count])
    split_rows(cuts, held[:count], loads[:count], masks.at[0], own_high, own_low)
    begin(loads[2 * count :])
    give[0]()
    give[1]()
    nvir = amp.shape[0]
    panel, a_parts, w_parts = (m_high, m_low), (a_high, a_low), (w_high, w_low)
    for turn in range(2):
        where = slice((1 + turn) * count, (2 + turn) * count)
        split_rows(cuts, held[where], loads[where], masks.at[1 + turn], m_high, m_low)
        amplitudes(
            scalars[2 * turn], scalars[2 * turn + 1], vir_col, vir_row,
            (own_high, own_low), panel, amp, a_parts, w_parts,
        )
        for start in range(0, nvir, TILE):
            cols = slice(start, start + TILE)
            value = density_tile(cols, w_parts, a_parts)
            density[:, cols] = value if turn == 0 else density[:, cols] + value
        if turn:
            give[2]()
        for part, piece in enumerate(slices):
            width = piece.shape[1]
            cols = slice(part * width, (part + 1) * width)
            value = respond(slice(0, nvir), w_parts, panel, cols)
            piece[...] = value if turn == 0 else piece[...] + value
            if turn:
                give[3 + part]()


def squares(nvir, naux):
    half = jnp.bfloat16
    return [pltpu.VMEM((nvir, naux), half)] * 2, [pltpu.VMEM((nvir, nvir), half)] * 4


def early(cuts, scalars, virtual, masks, own, near, twin):
    nvir, width = own[0].shape
    naux = masks.shape[2]
    parts = naux // width
    outs = [shape(nvir, naux, kind=jnp.bfloat16)] * 2 + [shape(nvir, nvir)]
    outs += [shape(nvir, width)] * parts
    wide, square = squares(nvir, naux)
    small = [scalars, *virtual, masks]
    kernel = functools.partial(early_kernel, cuts)
    scratch = [*wide, pltpu.VMEM((nvir, nvir), jnp.float32), *square]
    outs = call(kernel, "early", outs, small, [*own, *near, *twin], scratch)
    return outs[:2], outs[2], list(outs[3:])


def late_kernel(cuts, wanted, scale, small, held, made, own_scratch, loads, give):
    scalars, vir_col, vir_row, masks = small
    count = len(cuts)
    amp, panels = own_scratch[0], (own_scratch[1:7], own_scratch[7:])
    begin(loads[: 2 + count])
    for turn, (m_high, m_low, a_high, a_low, w_high, w_low) in enumerate(panels):
        where = slice(2 + turn * count, 2 + (1 + turn) * count)
        split_rows(cuts, held[where], loads[where], masks.at[turn], m_high, m_low)
        if turn == 0:
            loads[0].wait()
            loads[1].wait()
            begin(loads[2 + count :])
        amplitudes(
            scalars[2 * turn], scalars[2 * turn + 1], vir_col, vir_row,
            held[:2], (m_high, m_low), amp, (a_high, a_low), (w_high, w_low),
        )
    density, *slices = held[2 + 2 * count :]
    total, *pieces = made
    for load in loads[2 + 2 * count :]:
        load.wait()
    for start in range(0, density.shape[0], TILE):
        cols = slice(start, start + TILE)
        value = density[:, cols]
        for _, _, a_high, a_low, w_high, w_low in panels:
            value += density_tile(cols, (w_high, w_low), (a_high, a_low))
        total[:, cols] = value * scale
    give[0]()
    for at, ((part, first, height), piece) in enumerate(zip(wanted, pieces)):
        rows = slice(first, first + height)
        width = piece.shape[1]
        cols = slice(part * width, (part + 1) * width)
        value = slices[part][rows, :]
        for m_high, m_low, _, _, w_high, w_low in panels:
            value += respond(rows, (w_high, w_low), (m_high, m_low), cols)
        piece[...] = value
        give[1 + at]()


def late(cuts, wanted, scale, scalars, virtual, masks, own, far, twin, density, slices):
    nvir, naux = own[0].shape
    width = slices[0].shape[1]
    outs = [shape(nvir, nvir)] + [shape(height, width) for _, _, height in wanted]
    wide, square = squares(nvir, naux)
    small = [scalars, *virtual, masks]
    kernel = functools.partial(late_kernel, cuts, wanted, scale)
    scratch = [pltpu.VMEM((nvir, nvir), jnp.float32), *wide, *square, *wide, *square]
    big = [*own, *far, *twin, density, *slices]
    outs = call(kernel, "late", outs, small, big, scratch)
    return outs[0], list(outs[1:])


def exchange(value, axis, bit):
    size = lax.axis_size(axis)
    return lax.ppermute(value, axis, [(at, at ^ bit) for at in range(size)])


def after(value, *others):
    return lax.optimization_barrier((value, *others))[0]


def bits(axis):
    size = lax.axis_size(axis)
    return [1 << at for at in range(size.bit_length() - 1)]


def scatter_chip(value):
    half = value.shape[0] // 2
    side = lax.axis_index("col") % 2
    kept = lax.dynamic_slice_in_dim(value, side * half, half, 0)
    sent = lax.dynamic_slice_in_dim(value, (1 - side) * half, half, 0)
    return kept + exchange(sent, "col", 1)


def scatter_plane(value):
    place = lax.axis_index("col") // 2
    chips = lax.axis_size("col") // 2
    count = value.shape[0] // chips
    total = lax.dynamic_slice_in_dim(value, place * count, count, 0)
    for turn in range(1, chips):
        sent = lax.dynamic_slice_in_dim(value, (place ^ turn) * count, count, 0)
        total = total + exchange(sent, "col", 2 * turn)
    return total


def joined(terms, place):
    if len(terms) == 1:
        return terms[0]
    half = len(terms) // 2
    low, high = joined(terms[:half], place), joined(terms[half:], place)
    side = (place // half) % 2
    return jnp.where(side == 0, jnp.concatenate([low, high]), jnp.concatenate([high, low]))


def gather_plane(value):
    col = lax.axis_index("col")
    turns = range(1, lax.axis_size("col") // 2)
    terms = [value] + [exchange(value, "col", 2 * turn) for turn in turns]
    value = joined(terms, col // 2)
    return joined([value, exchange(value, "col", 1)], col)


def cut_list(nvir, row_count):
    return [(part, 0, nvir) for part in range(row_count)]


def on_device(three_index, occ_energy, vir_energy, block_mask, pair_list):
    row = lax.axis_index("row")
    col = lax.axis_index("col")
    row_count = lax.axis_size("row")
    col_count = lax.axis_size("col")
    position = col % NPANEL
    group = col // NPANEL
    groups = col_count // NPANEL
    nvir = three_index.shape[1]
    cuts = cut_list(nvir, row_count)

    own_orbital = col * row_count + row
    panels = [position ^ turn for turn in range(NPANEL)]
    orbitals = jnp.stack([own_orbital] + [at * row_count + row for at in panels])
    kept = block_mask[orbitals].reshape(NPANEL + 1, block_mask.shape[1], row_count, -1)
    kept = kept[:, :, row ^ jnp.arange(row_count), :].reshape(NPANEL + 1, kept.shape[1], -1)
    masks = jnp.repeat(kept.astype(jnp.float32), BLOCK, axis=-1)
    lists = pair_list[row]
    scalars = []
    for turn in range(NPANEL):
        live = jnp.any(lists == panels[turn]).astype(jnp.float32)
        scalars += [occ_energy[own_orbital] + occ_energy[orbitals[1 + turn]], live]
    small = masks[:3], masks[3:], jnp.stack(scalars[:4]), jnp.stack(scalars[4:])
    virtual = lax.optimization_barrier((vir_energy[:, None], vir_energy[None, :]))

    own, came, near, far = [], [], [], []

    def receive(at):
        part, first, count = cuts[at]
        rows = lax.dynamic_index_in_dim(three_index, row ^ part, 0, keepdims=False)
        rows = rows[first : first + count]
        if part == row_count - 1:
            rows = after(rows, near[0])
        elif part > 1:
            rows = after(rows, scalars[1])
        own.append(exchange(rows, "row", part) if part else rows)

    for at in range(len(cuts)):
        while len(own) < min(at + 1 if at > 1 else row_count - 1, len(cuts)):
            receive(len(own))
        rows = own[at]
        if at:
            rows = after(rows, came[-1])
        reach = 1
        while reach < groups:
            span = min(reach, groups - reach) * NPANEL
            links = [(one, one + reach * NPANEL) for one in range(span)]
            got = lax.ppermute(rows, "col", links)
            rows = jnp.where((group >= reach) & (group < 2 * reach), got, rows)
            reach *= 2
        came.append(got)
        near.append(rows)
        sent = after(rows, far[-1]) if at else after(rows, *small, *virtual)
        far.append(exchange(sent, "col", 2))

    near_twin = [exchange(piece, "col", 1) for piece in near]
    halved, density, slices = early(
        cuts, small[2], virtual, small[0], own, near, near_twin
    )
    far_twin = [exchange(piece, "col", 1) for piece in far[:-1]]
    far_twin.append(exchange(after(far[-1], density), "col", 1))

    middle, edge, most = row_count // 2, row_count - 1, nvir // 4 * 3
    wanted = [(middle, 0, most), (middle, most, nvir - most), (edge, 0, nvir)]
    wanted += [(at, 0, nvir) for at in range(edge) if at != middle]
    scale = 1.0 / (row_count * col_count)
    total, pieces = late(
        cuts, wanted, scale, small[3], virtual, small[1], halved, far, far_twin,
        density, slices,
    )

    def leave(at, *others):
        return exchange(after(pieces[at], *others), "row", wanted[at][0])

    ends = [leave(0)]
    total = scatter_plane(scatter_chip(total))
    ends.append(leave(1, total))
    total = after(total, ends[0])
    for bit in bits("row")[:-1]:
        total = total + exchange(total, "row", bit)
    total = after(total, ends[1])
    ends += [leave(2, total), pieces[3]]
    ends += [leave(at, total) for at in range(4, len(wanted))]
    total = total + exchange(total, "row", bits("row")[-1])
    total = gather_plane(total)

    returned = jnp.zeros_like(three_index)
    for (part, first, _), piece in zip(wanted, ends):
        returned = lax.dynamic_update_slice(returned, piece[None], (row ^ part, first, 0))
    return returned, total


def solution(mesh):
    placed = (P("col", None, "row"), P(), P(), P(), P("col", None))
    return jax.shard_map(
        on_device,
        mesh=mesh,
        in_specs=placed,
        out_specs=(P("col", None, "row"), P()),
        check_vma=False,
    )
```

```python
import functools

import jax
import jax.numpy as jnp
from jax import lax
from jax.experimental import pallas as pl
from jax.experimental.pallas import tpu as pltpu
from jax.sharding import PartitionSpec as P

BLOCK = 64
NPANEL = 4
TILE = 256
VMEM_LIMIT = 60 * 1024 * 1024
NT = (((1,), (1,)), ((), ()))


def staged(kernel, smalls, bigs, count, *refs):
    small, refs = refs[:smalls], refs[smalls:]
    sources, targets, scratch = refs[:bigs], refs[bigs : bigs + count], refs[bigs + count : -2]
    in_sem, out_sem = refs[-2:]
    held, made, own = scratch[:bigs], scratch[bigs : bigs + count], scratch[bigs + count :]
    loads = [
        pltpu.make_async_copy(source, target, in_sem.at[at])
        for at, (source, target) in enumerate(zip(sources, held))
    ]
    stores = [
        pltpu.make_async_copy(source, target, out_sem.at[at])
        for at, (source, target) in enumerate(zip(made, targets))
    ]
    kernel(small, held, made, own, loads, [store.start for store in stores])
    for store in stores:
        store.wait()


def call(kernel, name, outs, small, big, scratch):
    any_space = pl.BlockSpec(memory_space=pl.ANY)
    specs = [pl.BlockSpec(memory_space=pltpu.SMEM)]
    specs += [pl.BlockSpec(memory_space=pltpu.VMEM)] * (len(small) - 1)
    buffers = [pltpu.VMEM(at.shape, at.dtype) for at in [*big, *outs]]
    sems = [pltpu.SemaphoreType.DMA((len(big),)), pltpu.SemaphoreType.DMA((len(outs),))]
    return pl.pallas_call(
        functools.partial(staged, kernel, len(small), len(big), len(outs)),
        out_shape=outs,
        in_specs=specs + [any_space] * len(big),
        out_specs=[any_space] * len(outs),
        scratch_shapes=[*buffers, *scratch, *sems],
        compiler_params=pltpu.CompilerParams(vmem_limit_bytes=VMEM_LIMIT),
        cost_estimate=pl.CostEstimate(flops=0, bytes_accessed=0, transcendentals=0),
        name=name,
    )(*small, *big)


def shape(*sizes, kind=jnp.float32):
    return jax.ShapeDtypeStruct(sizes, kind)


def halves(value):
    high = value.astype(jnp.bfloat16)
    return high, (value - high.astype(jnp.float32)).astype(jnp.bfloat16)


def dot(left, right):
    return jnp.dot(left, right, preferred_element_type=jnp.float32)


def dot_nt(left, right):
    return lax.dot_general(left, right, NT, preferred_element_type=jnp.float32)


def begin(loads):
    for load in loads:
        load.start()


def split_rows(cuts, pieces, loads, mask, high, low):
    for (part, first, count), piece, load in zip(cuts, pieces, loads):
        load.wait()
        width = piece.shape[1]
        cols = slice(part * width, (part + 1) * width)
        for start in range(0, count, BLOCK):
            at = first + start
            kept = mask[at // BLOCK : at // BLOCK + 1, cols]
            value = piece[start : start + BLOCK, :] * kept
            high[at : at + BLOCK, cols], low[at : at + BLOCK, cols] = halves(value)


def amplitudes(energy, live, vir_col, vir_row, own, panel, amp, a_parts, w_parts):
    nvir = amp.shape[0]
    for start in range(0, nvir, TILE):
        cols = slice(start, start + TILE)
        cross = dot_nt(own[0][...], panel[0][cols, :])
        cross += dot_nt(own[0][...], panel[1][cols, :])
        cross += dot_nt(own[1][...], panel[0][cols, :])
        value = cross / (energy - vir_col[...] - vir_row[:, cols]) * live
        amp[:, cols] = value
        a_parts[0][:, cols], a_parts[1][:, cols] = halves(value)
    for above in range(0, nvir, TILE):
        rows = slice(above, above + TILE)
        for start in range(0, nvir, TILE):
            cols = slice(start, start + TILE)
            value = 2.0 * amp[rows, cols] - amp[cols, rows].T
            w_parts[0][rows, cols], w_parts[1][rows, cols] = halves(value)


def respond(rows, w_parts, panel, cols):
    value = dot(w_parts[0][rows, :], panel[0][:, cols])
    value += dot(w_parts[0][rows, :], panel[1][:, cols])
    return value + dot(w_parts[1][rows, :], panel[0][:, cols])


def density_tile(cols, w_parts, a_parts):
    value = dot_nt(w_parts[0][...], a_parts[0][cols, :])
    value += dot_nt(w_parts[0][...], a_parts[1][cols, :])
    return value + dot_nt(w_parts[1][...], a_parts[0][cols, :])


def early_kernel(cuts, small, held, made, own_scratch, loads, give):
    scalars, vir_col, vir_row, masks = small
    count = len(cuts)
    own_high, own_low, density, *slices = made
    m_high, m_low, amp, a_high, a_low, w_high, w_low = own_scratch
    begin(loads[: 2 * count])
    split_rows(cuts, held[:count], loads[:count], masks.at[0], own_high, own_low)
    begin(loads[2 * count :])
    give[0]()
    give[1]()
    nvir = amp.shape[0]
    panel, a_parts, w_parts = (m_high, m_low), (a_high, a_low), (w_high, w_low)
    for turn in range(2):
        where = slice((1 + turn) * count, (2 + turn) * count)
        split_rows(cuts, held[where], loads[where], masks.at[1 + turn], m_high, m_low)
        amplitudes(
            scalars[2 * turn], scalars[2 * turn + 1], vir_col, vir_row,
            (own_high, own_low), panel, amp, a_parts, w_parts,
        )
        for start in range(0, nvir, TILE):
            cols = slice(start, start + TILE)
            value = density_tile(cols, w_parts, a_parts)
            density[:, cols] = value if turn == 0 else density[:, cols] + value
        if turn:
            give[2]()
        for part, piece in enumerate(slices):
            width = piece.shape[1]
            cols = slice(part * width, (part + 1) * width)
            value = respond(slice(0, nvir), w_parts, panel, cols)
            piece[...] = value if turn == 0 else piece[...] + value
            if turn:
                give[3 + part]()


def squares(nvir, naux):
    half = jnp.bfloat16
    return [pltpu.VMEM((nvir, naux), half)] * 2, [pltpu.VMEM((nvir, nvir), half)] * 4


def early(cuts, scalars, virtual, masks, own, near, twin):
    nvir, width = own[0].shape
    naux = masks.shape[2]
    parts = naux // width
    outs = [shape(nvir, naux, kind=jnp.bfloat16)] * 2 + [shape(nvir, nvir)]
    outs += [shape(nvir, width)] * parts
    wide, square = squares(nvir, naux)
    small = [scalars, *virtual, masks]
    kernel = functools.partial(early_kernel, cuts)
    scratch = [*wide, pltpu.VMEM((nvir, nvir), jnp.float32), *square]
    outs = call(kernel, "early", outs, small, [*own, *near, *twin], scratch)
    return outs[:2], outs[2], list(outs[3:])


def late_kernel(cuts, wanted, scale, small, held, made, own_scratch, loads, give):
    scalars, vir_col, vir_row, masks = small
    count = len(cuts)
    amp, panels = own_scratch[0], (own_scratch[1:7], own_scratch[7:])
    begin(loads[: 2 + count])
    for turn, (m_high, m_low, a_high, a_low, w_high, w_low) in enumerate(panels):
        where = slice(2 + turn * count, 2 + (1 + turn) * count)
        split_rows(cuts, held[where], loads[where], masks.at[turn], m_high, m_low)
        if turn == 0:
            loads[0].wait()
            loads[1].wait()
            begin(loads[2 + count :])
        amplitudes(
            scalars[2 * turn], scalars[2 * turn + 1], vir_col, vir_row,
            held[:2], (m_high, m_low), amp, (a_high, a_low), (w_high, w_low),
        )
    density, *slices = held[2 + 2 * count :]
    total, *pieces = made
    for load in loads[2 + 2 * count :]:
        load.wait()
    for start in range(0, density.shape[0], TILE):
        cols = slice(start, start + TILE)
        value = density[:, cols]
        for _, _, a_high, a_low, w_high, w_low in panels:
            value += density_tile(cols, (w_high, w_low), (a_high, a_low))
        total[:, cols] = value * scale
    give[0]()
    for at, ((part, first, height), piece) in enumerate(zip(wanted, pieces)):
        rows = slice(first, first + height)
        width = piece.shape[1]
        cols = slice(part * width, (part + 1) * width)
        value = slices[part][rows, :]
        for m_high, m_low, _, _, w_high, w_low in panels:
            value += respond(rows, (w_high, w_low), (m_high, m_low), cols)
        piece[...] = value
        give[1 + at]()


def late(cuts, wanted, scale, scalars, virtual, masks, own, far, twin, density, slices):
    nvir, naux = own[0].shape
    width = slices[0].shape[1]
    outs = [shape(nvir, nvir)] + [shape(height, width) for _, _, height in wanted]
    wide, square = squares(nvir, naux)
    small = [scalars, *virtual, masks]
    kernel = functools.partial(late_kernel, cuts, wanted, scale)
    scratch = [pltpu.VMEM((nvir, nvir), jnp.float32), *wide, *square, *wide, *square]
    big = [*own, *far, *twin, density, *slices]
    outs = call(kernel, "late", outs, small, big, scratch)
    return outs[0], list(outs[1:])


def exchange(value, axis, bit):
    size = lax.axis_size(axis)
    return lax.ppermute(value, axis, [(at, at ^ bit) for at in range(size)])


def after(value, *others):
    return lax.optimization_barrier((value, *others))[0]


def bits(axis):
    size = lax.axis_size(axis)
    return [1 << at for at in range(size.bit_length() - 1)]


def scatter_chip(value):
    half = value.shape[0] // 2
    side = lax.axis_index("col") % 2
    kept = lax.dynamic_slice_in_dim(value, side * half, half, 0)
    sent = lax.dynamic_slice_in_dim(value, (1 - side) * half, half, 0)
    return kept + exchange(sent, "col", 1)


def scatter_plane(value):
    place = lax.axis_index("col") // 2
    chips = lax.axis_size("col") // 2
    count = value.shape[0] // chips
    total = lax.dynamic_slice_in_dim(value, place * count, count, 0)
    for turn in range(1, chips):
        sent = lax.dynamic_slice_in_dim(value, (place ^ turn) * count, count, 0)
        total = total + exchange(sent, "col", 2 * turn)
    return total


def joined(terms, place):
    if len(terms) == 1:
        return terms[0]
    half = len(terms) // 2
    low, high = joined(terms[:half], place), joined(terms[half:], place)
    side = (place // half) % 2
    return jnp.where(side == 0, jnp.concatenate([low, high]), jnp.concatenate([high, low]))


def gather_plane(value):
    col = lax.axis_index("col")
    turns = range(1, lax.axis_size("col") // 2)
    terms = [value] + [exchange(value, "col", 2 * turn) for turn in turns]
    value = joined(terms, col // 2)
    return joined([value, exchange(value, "col", 1)], col)


def cut_list(nvir, row_count):
    return [(part, 0, nvir) for part in range(row_count)]


def on_device(three_index, occ_energy, vir_energy, block_mask, pair_list):
    row = lax.axis_index("row")
    col = lax.axis_index("col")
    row_count = lax.axis_size("row")
    col_count = lax.axis_size("col")
    position = col % NPANEL
    group = col // NPANEL
    groups = col_count // NPANEL
    nvir = three_index.shape[1]
    cuts = cut_list(nvir, row_count)

    own_orbital = col * row_count + row
    panels = [position ^ turn for turn in range(NPANEL)]
    orbitals = jnp.stack([own_orbital] + [at * row_count + row for at in panels])
    kept = block_mask[orbitals].reshape(NPANEL + 1, block_mask.shape[1], row_count, -1)
    kept = kept[:, :, row ^ jnp.arange(row_count), :].reshape(NPANEL + 1, kept.shape[1], -1)
    masks = jnp.repeat(kept.astype(jnp.float32), BLOCK, axis=-1)
    lists = pair_list[row]
    scalars = []
    for turn in range(NPANEL):
        live = jnp.any(lists == panels[turn]).astype(jnp.float32)
        scalars += [occ_energy[own_orbital] + occ_energy[orbitals[1 + turn]], live]
    small = masks[:3], masks[3:], jnp.stack(scalars[:4]), jnp.stack(scalars[4:])
    virtual = vir_energy[:, None], vir_energy[None, :]

    own, came, near, far = [], [], [], []

    def receive(at):
        part, first, count = cuts[at]
        rows = lax.dynamic_index_in_dim(three_index, row ^ part, 0, keepdims=False)
        rows = rows[first : first + count]
        if part == row_count - 1:
            rows = after(rows, near[0])
        elif part > 1:
            rows = after(rows, scalars[1])
        own.append(exchange(rows, "row", part) if part else rows)

    for at in range(len(cuts)):
        while len(own) < min(at + 1 if at > 1 else row_count - 1, len(cuts)):
            receive(len(own))
        rows = own[at]
        if at:
            rows = after(rows, came[-1])
        reach = 1
        while reach < groups:
            span = min(reach, groups - reach) * NPANEL
            links = [(one, one + reach * NPANEL) for one in range(span)]
            got = lax.ppermute(rows, "col", links)
            rows = jnp.where((group >= reach) & (group < 2 * reach), got, rows)
            reach *= 2
        came.append(got)
        near.append(rows)
        sent = after(rows, far[-1]) if at else after(rows, *small)
        far.append(exchange(sent, "col", 2))

    near_twin = [exchange(piece, "col", 1) for piece in near]
    halved, density, slices = early(
        cuts, small[2], virtual, small[0], own, near, near_twin
    )
    far_twin = [exchange(piece, "col", 1) for piece in far[:-1]]
    far_twin.append(exchange(after(far[-1], density), "col", 1))

    middle, edge, most = row_count // 2, row_count - 1, nvir // 4 * 3
    wanted = [(middle, 0, most), (middle, most, nvir - most), (edge, 0, nvir)]
    wanted += [(at, 0, nvir) for at in range(edge) if at != middle]
    scale = 1.0 / (row_count * col_count)
    total, pieces = late(
        cuts, wanted, scale, small[3], virtual, small[1], halved, far, far_twin,
        density, slices,
    )

    def leave(at, *others):
        return exchange(after(pieces[at], *others), "row", wanted[at][0])

    ends, others = [leave(0)], [leave(at) for at in range(4, len(wanted))]
    total = scatter_plane(scatter_chip(total))
    ends.append(leave(1, total))
    total = after(total, ends[0], *others)
    for bit in bits("row")[:-1]:
        total = total + exchange(total, "row", bit)
    total = after(total, ends[1])
    ends += [leave(2, total), pieces[3], *others]
    total = total + exchange(total, "row", bits("row")[-1])
    total = gather_plane(total)

    returned = jnp.zeros_like(three_index)
    for (part, first, _), piece in zip(wanted, ends):
        returned = lax.dynamic_update_slice(returned, piece[None], (row ^ part, first, 0))
    return returned, total


def solution(mesh):
    placed = (P("col", None, "row"), P(), P(), P(), P("col", None))
    return jax.shard_map(
        on_device,
        mesh=mesh,
        in_specs=placed,
        out_specs=(P("col", None, "row"), P()),
        check_vma=False,
    )
```

```python
import functools

import jax
import jax.numpy as jnp
from jax import lax
from jax.experimental import pallas as pl
from jax.experimental.pallas import tpu as pltpu
from jax.sharding import PartitionSpec as P

BLOCK = 64
NPANEL = 4
TILE = 256
VMEM_LIMIT = 60 * 1024 * 1024
NT = (((1,), (1,)), ((), ()))


def staged(kernel, smalls, bigs, count, *refs):
    small, refs = refs[:smalls], refs[smalls:]
    sources, targets, scratch = refs[:bigs], refs[bigs : bigs + count], refs[bigs + count : -2]
    in_sem, out_sem = refs[-2:]
    held, made, own = scratch[:bigs], scratch[bigs : bigs + count], scratch[bigs + count :]
    loads = [
        pltpu.make_async_copy(source, target, in_sem.at[at])
        for at, (source, target) in enumerate(zip(sources, held))
    ]
    stores = [
        pltpu.make_async_copy(source, target, out_sem.at[at])
        for at, (source, target) in enumerate(zip(made, targets))
    ]
    kernel(small, held, made, own, loads, [store.start for store in stores])
    for store in stores:
        store.wait()


def call(kernel, name, outs, small, big, scratch):
    any_space = pl.BlockSpec(memory_space=pl.ANY)
    specs = [pl.BlockSpec(memory_space=pltpu.SMEM)]
    specs += [pl.BlockSpec(memory_space=pltpu.VMEM)] * (len(small) - 1)
    buffers = [pltpu.VMEM(at.shape, at.dtype) for at in [*big, *outs]]
    sems = [pltpu.SemaphoreType.DMA((len(big),)), pltpu.SemaphoreType.DMA((len(outs),))]
    return pl.pallas_call(
        functools.partial(staged, kernel, len(small), len(big), len(outs)),
        out_shape=outs,
        in_specs=specs + [any_space] * len(big),
        out_specs=[any_space] * len(outs),
        scratch_shapes=[*buffers, *scratch, *sems],
        compiler_params=pltpu.CompilerParams(vmem_limit_bytes=VMEM_LIMIT),
        cost_estimate=pl.CostEstimate(flops=0, bytes_accessed=0, transcendentals=0),
        name=name,
    )(*small, *big)


def shape(*sizes, kind=jnp.float32):
    return jax.ShapeDtypeStruct(sizes, kind)


def halves(value):
    high = value.astype(jnp.bfloat16)
    return high, (value - high.astype(jnp.float32)).astype(jnp.bfloat16)


def dot(left, right):
    return jnp.dot(left, right, preferred_element_type=jnp.float32)


def dot_nt(left, right):
    return lax.dot_general(left, right, NT, preferred_element_type=jnp.float32)


def begin(loads):
    for load in loads:
        load.start()


def split_rows(cuts, pieces, loads, mask, high, low):
    for (part, first, count), piece, load in zip(cuts, pieces, loads):
        load.wait()
        width = piece.shape[1]
        cols = slice(part * width, (part + 1) * width)
        for start in range(0, count, BLOCK):
            at = first + start
            kept = mask[at // BLOCK : at // BLOCK + 1, cols]
            value = piece[start : start + BLOCK, :] * kept
            high[at : at + BLOCK, cols], low[at : at + BLOCK, cols] = halves(value)


def amplitudes(energy, live, vir_col, vir_row, own, panel, amp, a_parts, w_parts):
    nvir = amp.shape[0]
    for start in range(0, nvir, TILE):
        cols = slice(start, start + TILE)
        cross = dot_nt(own[0][...], panel[0][cols, :])
        cross += dot_nt(own[0][...], panel[1][cols, :])
        cross += dot_nt(own[1][...], panel[0][cols, :])
        value = cross / (energy - vir_col[...] - vir_row[:, cols]) * live
        amp[:, cols] = value
        a_parts[0][:, cols], a_parts[1][:, cols] = halves(value)
    for above in range(0, nvir, TILE):
        rows = slice(above, above + TILE)
        for start in range(0, nvir, TILE):
            cols = slice(start, start + TILE)
            value = 2.0 * amp[rows, cols] - amp[cols, rows].T
            w_parts[0][rows, cols], w_parts[1][rows, cols] = halves(value)


def respond(rows, w_parts, panel, cols):
    value = dot(w_parts[0][rows, :], panel[0][:, cols])
    value += dot(w_parts[0][rows, :], panel[1][:, cols])
    return value + dot(w_parts[1][rows, :], panel[0][:, cols])


def density_tile(cols, w_parts, a_parts):
    value = dot_nt(w_parts[0][...], a_parts[0][cols, :])
    value += dot_nt(w_parts[0][...], a_parts[1][cols, :])
    return value + dot_nt(w_parts[1][...], a_parts[0][cols, :])


def early_kernel(cuts, small, held, made, own_scratch, loads, give):
    scalars, vir_col, vir_row, masks = small
    count = len(cuts)
    own_high, own_low, density, *slices = made
    m_high, m_low, amp, a_high, a_low, w_high, w_low = own_scratch
    begin(loads[: 2 * count])
    split_rows(cuts, held[:count], loads[:count], masks.at[0], own_high, own_low)
    begin(loads[2 * count :])
    give[0]()
    give[1]()
    nvir = amp.shape[0]
    panel, a_parts, w_parts = (m_high, m_low), (a_high, a_low), (w_high, w_low)
    for turn in range(2):
        where = slice((1 + turn) * count, (2 + turn) * count)
        split_rows(cuts, held[where], loads[where], masks.at[1 + turn], m_high, m_low)
        amplitudes(
            scalars[2 * turn], scalars[2 * turn + 1], vir_col, vir_row,
            (own_high, own_low), panel, amp, a_parts, w_parts,
        )
        for start in range(0, nvir, TILE):
            cols = slice(start, start + TILE)
            value = density_tile(cols, w_parts, a_parts)
            density[:, cols] = value if turn == 0 else density[:, cols] + value
        if turn:
            give[2]()
        for part, piece in enumerate(slices):
            width = piece.shape[1]
            cols = slice(part * width, (part + 1) * width)
            value = respond(slice(0, nvir), w_parts, panel, cols)
            piece[...] = value if turn == 0 else piece[...] + value
            if turn:
                give[3 + part]()


def squares(nvir, naux):
    half = jnp.bfloat16
    return [pltpu.VMEM((nvir, naux), half)] * 2, [pltpu.VMEM((nvir, nvir), half)] * 4


def early(cuts, scalars, virtual, masks, own, near, twin):
    nvir, width = own[0].shape
    naux = masks.shape[2]
    parts = naux // width
    outs = [shape(nvir, naux, kind=jnp.bfloat16)] * 2 + [shape(nvir, nvir)]
    outs += [shape(nvir, width)] * parts
    wide, square = squares(nvir, naux)
    small = [scalars, *virtual, masks]
    kernel = functools.partial(early_kernel, cuts)
    scratch = [*wide, pltpu.VMEM((nvir, nvir), jnp.float32), *square]
    outs = call(kernel, "early", outs, small, [*own, *near, *twin], scratch)
    return outs[:2], outs[2], list(outs[3:])


def late_kernel(cuts, wanted, scale, small, held, made, own_scratch, loads, give):
    scalars, vir_col, vir_row, masks = small
    count = len(cuts)
    amp, panels = own_scratch[0], (own_scratch[1:7], own_scratch[7:])
    begin(loads[: 2 + count])
    for turn, (m_high, m_low, a_high, a_low, w_high, w_low) in enumerate(panels):
        where = slice(2 + turn * count, 2 + (1 + turn) * count)
        split_rows(cuts, held[where], loads[where], masks.at[turn], m_high, m_low)
        if turn == 0:
            loads[0].wait()
            loads[1].wait()
            begin(loads[2 + count :])
        amplitudes(
            scalars[2 * turn], scalars[2 * turn + 1], vir_col, vir_row,
            held[:2], (m_high, m_low), amp, (a_high, a_low), (w_high, w_low),
        )
    density, *slices = held[2 + 2 * count :]
    total, *pieces = made
    for load in loads[2 + 2 * count :]:
        load.wait()
    for start in range(0, density.shape[0], TILE):
        cols = slice(start, start + TILE)
        value = density[:, cols]
        for _, _, a_high, a_low, w_high, w_low in panels:
            value += density_tile(cols, (w_high, w_low), (a_high, a_low))
        total[:, cols] = value * scale
    give[0]()
    for at, ((part, first, height), piece) in enumerate(zip(wanted, pieces)):
        rows = slice(first, first + height)
        width = piece.shape[1]
        cols = slice(part * width, (part + 1) * width)
        value = slices[part][rows, :]
        for m_high, m_low, _, _, w_high, w_low in panels:
            value += respond(rows, (w_high, w_low), (m_high, m_low), cols)
        piece[...] = value
        give[1 + at]()


def late(cuts, wanted, scale, scalars, virtual, masks, own, far, twin, density, slices):
    nvir, naux = own[0].shape
    width = slices[0].shape[1]
    outs = [shape(nvir, nvir)] + [shape(height, width) for _, _, height in wanted]
    wide, square = squares(nvir, naux)
    small = [scalars, *virtual, masks]
    kernel = functools.partial(late_kernel, cuts, wanted, scale)
    scratch = [pltpu.VMEM((nvir, nvir), jnp.float32), *wide, *square, *wide, *square]
    big = [*own, *far, *twin, density, *slices]
    outs = call(kernel, "late", outs, small, big, scratch)
    return outs[0], list(outs[1:])


def exchange(value, axis, bit):
    size = lax.axis_size(axis)
    return lax.ppermute(value, axis, [(at, at ^ bit) for at in range(size)])


def after(value, *others):
    return lax.optimization_barrier((value, *others))[0]


def bits(axis):
    size = lax.axis_size(axis)
    return [1 << at for at in range(size.bit_length() - 1)]


def scatter_chip(value):
    half = value.shape[0] // 2
    side = lax.axis_index("col") % 2
    kept = lax.dynamic_slice_in_dim(value, side * half, half, 0)
    sent = lax.dynamic_slice_in_dim(value, (1 - side) * half, half, 0)
    return kept + exchange(sent, "col", 1)


def scatter_plane(value):
    place = lax.axis_index("col") // 2
    chips = lax.axis_size("col") // 2
    count = value.shape[0] // chips
    total = lax.dynamic_slice_in_dim(value, place * count, count, 0)
    for turn in range(1, chips):
        sent = lax.dynamic_slice_in_dim(value, (place ^ turn) * count, count, 0)
        total = total + exchange(sent, "col", 2 * turn)
    return total


def joined(terms, place):
    if len(terms) == 1:
        return terms[0]
    half = len(terms) // 2
    low, high = joined(terms[:half], place), joined(terms[half:], place)
    side = (place // half) % 2
    return jnp.where(side == 0, jnp.concatenate([low, high]), jnp.concatenate([high, low]))


def gather_plane(value):
    col = lax.axis_index("col")
    turns = range(1, lax.axis_size("col") // 2)
    terms = [value] + [exchange(value, "col", 2 * turn) for turn in turns]
    value = joined(terms, col // 2)
    return joined([value, exchange(value, "col", 1)], col)


def cut_list(nvir, row_count):
    return [(part, 0, nvir) for part in range(row_count)]


def on_device(three_index, occ_energy, vir_energy, block_mask, pair_list):
    row = lax.axis_index("row")
    col = lax.axis_index("col")
    row_count = lax.axis_size("row")
    col_count = lax.axis_size("col")
    position = col % NPANEL
    group = col // NPANEL
    groups = col_count // NPANEL
    nvir = three_index.shape[1]
    cuts = cut_list(nvir, row_count)

    own_orbital = col * row_count + row
    panels = [position ^ turn for turn in range(NPANEL)]
    orbitals = jnp.stack([own_orbital] + [at * row_count + row for at in panels])
    kept = block_mask[orbitals].reshape(NPANEL + 1, block_mask.shape[1], row_count, -1)
    kept = kept[:, :, row ^ jnp.arange(row_count), :].reshape(NPANEL + 1, kept.shape[1], -1)
    masks = jnp.repeat(kept.astype(jnp.float32), BLOCK, axis=-1)
    lists = pair_list[row]
    scalars = []
    for turn in range(NPANEL):
        live = jnp.any(lists == panels[turn]).astype(jnp.float32)
        scalars += [occ_energy[own_orbital] + occ_energy[orbitals[1 + turn]], live]
    small = masks[:3], masks[3:], jnp.stack(scalars[:4]), jnp.stack(scalars[4:])
    virtual = lax.optimization_barrier((vir_energy[:, None], vir_energy[None, :]))

    own, came, near, far = [], [], [], []

    def receive(at):
        part, first, count = cuts[at]
        rows = lax.dynamic_index_in_dim(three_index, row ^ part, 0, keepdims=False)
        rows = rows[first : first + count]
        if part == row_count - 1:
            rows = after(rows, near[0])
        own.append(exchange(rows, "row", part) if part else rows)

    for at in range(len(cuts)):
        while len(own) < min(at + 1 if at > 1 else row_count - 1, len(cuts)):
            receive(len(own))
        rows = own[at]
        if at:
            rows = after(rows, came[-1])
        reach = 1
        while reach < groups:
            span = min(reach, groups - reach) * NPANEL
            links = [(one, one + reach * NPANEL) for one in range(span)]
            got = lax.ppermute(rows, "col", links)
            rows = jnp.where((group >= reach) & (group < 2 * reach), got, rows)
            reach *= 2
        came.append(got)
        near.append(rows)
        sent = after(rows, far[-1]) if at else after(rows, *small, *virtual)
        far.append(exchange(sent, "col", 2))

    near_twin = [exchange(piece, "col", 1) for piece in near]
    halved, density, slices = early(
        cuts, small[2], virtual, small[0], own, near, near_twin
    )
    far_twin = [exchange(piece, "col", 1) for piece in far[:-1]]
    far_twin.append(exchange(after(far[-1], density), "col", 1))

    middle, edge, most = row_count // 2, row_count - 1, nvir // 4 * 3
    wanted = [(middle, 0, most), (middle, most, nvir - most), (edge, 0, nvir)]
    wanted += [(at, 0, nvir) for at in range(edge) if at != middle]
    scale = 1.0 / (row_count * col_count)
    total, pieces = late(
        cuts, wanted, scale, small[3], virtual, small[1], halved, far, far_twin,
        density, slices,
    )

    def leave(at, *others):
        return exchange(after(pieces[at], *others), "row", wanted[at][0])

    ends = [leave(0)]
    total = scatter_plane(scatter_chip(total))
    ends.append(leave(1, total))
    total = after(total, ends[0])
    for bit in bits("row")[:-1]:
        total = total + exchange(total, "row", bit)
    total = after(total, ends[1])
    ends += [leave(2, total), pieces[3]]
    ends += [leave(at, total) for at in range(4, len(wanted))]
    total = total + exchange(total, "row", bits("row")[-1])
    total = gather_plane(total)

    returned = jnp.zeros_like(three_index)
    for (part, first, _), piece in zip(wanted, ends):
        returned = lax.dynamic_update_slice(returned, piece[None], (row ^ part, first, 0))
    return returned, total


def solution(mesh):
    placed = (P("col", None, "row"), P(), P(), P(), P("col", None))
    return jax.shard_map(
        on_device,
        mesh=mesh,
        in_specs=placed,
        out_specs=(P("col", None, "row"), P()),
        check_vma=False,
    )
```

```python
import functools

import jax
import jax.numpy as jnp
from jax import lax
from jax.experimental import pallas as pl
from jax.experimental.pallas import tpu as pltpu
from jax.sharding import PartitionSpec as P

BLOCK = 64
LANES = 128
NPANEL = 4
TILE = 256
VMEM_LIMIT = 60 * 1024 * 1024
NT = (((1,), (1,)), ((), ()))


def staged(kernel, smalls, bigs, count, *refs):
    small, refs = refs[:smalls], refs[smalls:]
    sources, targets, scratch = refs[:bigs], refs[bigs : bigs + count], refs[bigs + count : -2]
    in_sem, out_sem = refs[-2:]
    held, made, own = scratch[:bigs], scratch[bigs : bigs + count], scratch[bigs + count :]
    loads = [
        pltpu.make_async_copy(source, target, in_sem.at[at])
        for at, (source, target) in enumerate(zip(sources, held))
    ]
    stores = [
        pltpu.make_async_copy(source, target, out_sem.at[at])
        for at, (source, target) in enumerate(zip(made, targets))
    ]
    kernel(small, held, made, own, loads, [store.start for store in stores])
    for store in stores:
        store.wait()


def call(kernel, name, outs, small, big, scratch):
    any_space = pl.BlockSpec(memory_space=pl.ANY)
    specs = [pl.BlockSpec(memory_space=pltpu.SMEM)]
    specs += [pl.BlockSpec(memory_space=pltpu.VMEM)] * (len(small) - 1)
    buffers = [pltpu.VMEM(at.shape, at.dtype) for at in [*big, *outs]]
    sems = [pltpu.SemaphoreType.DMA((len(big),)), pltpu.SemaphoreType.DMA((len(outs),))]
    return pl.pallas_call(
        functools.partial(staged, kernel, len(small), len(big), len(outs)),
        out_shape=outs,
        in_specs=specs + [any_space] * len(big),
        out_specs=[any_space] * len(outs),
        scratch_shapes=[*buffers, *scratch, *sems],
        compiler_params=pltpu.CompilerParams(vmem_limit_bytes=VMEM_LIMIT),
        cost_estimate=pl.CostEstimate(flops=0, bytes_accessed=0, transcendentals=0),
        name=name,
    )(*small, *big)


def shape(*sizes, kind=jnp.float32):
    return jax.ShapeDtypeStruct(sizes, kind)


def halves(value):
    high = value.astype(jnp.bfloat16)
    return high, (value - high.astype(jnp.float32)).astype(jnp.bfloat16)


def dot(left, right):
    return jnp.dot(left, right, preferred_element_type=jnp.float32)


def dot_nt(left, right):
    return lax.dot_general(left, right, NT, preferred_element_type=jnp.float32)


def begin(loads):
    for load in loads:
        load.start()


def split_rows(cuts, pieces, loads, mask, high, low):
    for (part, first, count), piece, load in zip(cuts, pieces, loads):
        load.wait()
        width = piece.shape[1]
        cols = slice(part * width, (part + 1) * width)
        for start in range(0, count, BLOCK):
            at = first + start
            kept = mask[at // BLOCK : at // BLOCK + 1, cols]
            value = piece[start : start + BLOCK, :] * kept
            high[at : at + BLOCK, cols], low[at : at + BLOCK, cols] = halves(value)


def amplitudes(energy, live, vir_col, vir_row, own, panel, amp, a_parts, w_parts):
    nvir = amp.shape[0]
    for start in range(0, nvir, TILE):
        cols = slice(start, start + TILE)
        cross = dot_nt(own[0][...], panel[0][cols, :])
        cross += dot_nt(own[0][...], panel[1][cols, :])
        cross += dot_nt(own[1][...], panel[0][cols, :])
        value = cross / (energy - vir_col[:, :1] - vir_row[:, cols]) * live
        amp[:, cols] = value
        a_parts[0][:, cols], a_parts[1][:, cols] = halves(value)
    for above in range(0, nvir, TILE):
        rows = slice(above, above + TILE)
        for start in range(0, nvir, TILE):
            cols = slice(start, start + TILE)
            value = 2.0 * amp[rows, cols] - amp[cols, rows].T
            w_parts[0][rows, cols], w_parts[1][rows, cols] = halves(value)


def respond(rows, w_parts, panel, cols):
    value = dot(w_parts[0][rows, :], panel[0][:, cols])
    value += dot(w_parts[0][rows, :], panel[1][:, cols])
    return value + dot(w_parts[1][rows, :], panel[0][:, cols])


def density_tile(cols, w_parts, a_parts):
    value = dot_nt(w_parts[0][...], a_parts[0][cols, :])
    value += dot_nt(w_parts[0][...], a_parts[1][cols, :])
    return value + dot_nt(w_parts[1][...], a_parts[0][cols, :])


def early_kernel(cuts, small, held, made, own_scratch, loads, give):
    scalars, vir_col, vir_row, masks = small
    count = len(cuts)
    own_high, own_low, density, *slices = made
    m_high, m_low, amp, a_high, a_low, w_high, w_low = own_scratch
    begin(loads[: 2 * count])
    split_rows(cuts, held[:count], loads[:count], masks.at[0], own_high, own_low)
    begin(loads[2 * count :])
    give[0]()
    give[1]()
    nvir = amp.shape[0]
    panel, a_parts, w_parts = (m_high, m_low), (a_high, a_low), (w_high, w_low)
    for turn in range(2):
        where = slice((1 + turn) * count, (2 + turn) * count)
        split_rows(cuts, held[where], loads[where], masks.at[1 + turn], m_high, m_low)
        amplitudes(
            scalars[2 * turn], scalars[2 * turn + 1], vir_col, vir_row,
            (own_high, own_low), panel, amp, a_parts, w_parts,
        )
        for start in range(0, nvir, TILE):
            cols = slice(start, start + TILE)
            value = density_tile(cols, w_parts, a_parts)
            density[:, cols] = value if turn == 0 else density[:, cols] + value
        if turn:
            give[2]()
        for part, piece in enumerate(slices):
            width = piece.shape[1]
            cols = slice(part * width, (part + 1) * width)
            value = respond(slice(0, nvir), w_parts, panel, cols)
            piece[...] = value if turn == 0 else piece[...] + value
            if turn:
                give[3 + part]()


def squares(nvir, naux):
    half = jnp.bfloat16
    return [pltpu.VMEM((nvir, naux), half)] * 2, [pltpu.VMEM((nvir, nvir), half)] * 4


def early(cuts, scalars, virtual, masks, own, near, twin):
    nvir, width = own[0].shape
    naux = masks.shape[2]
    parts = naux // width
    outs = [shape(nvir, naux, kind=jnp.bfloat16)] * 2 + [shape(nvir, nvir)]
    outs += [shape(nvir, width)] * parts
    wide, square = squares(nvir, naux)
    small = [scalars, *virtual, masks]
    kernel = functools.partial(early_kernel, cuts)
    scratch = [*wide, pltpu.VMEM((nvir, nvir), jnp.float32), *square]
    outs = call(kernel, "early", outs, small, [*own, *near, *twin], scratch)
    return outs[:2], outs[2], list(outs[3:])


def late_kernel(cuts, wanted, scale, small, held, made, own_scratch, loads, give):
    scalars, vir_col, vir_row, masks = small
    count = len(cuts)
    amp, panels = own_scratch[0], (own_scratch[1:7], own_scratch[7:])
    begin(loads[: 2 + count])
    for turn, (m_high, m_low, a_high, a_low, w_high, w_low) in enumerate(panels):
        where = slice(2 + turn * count, 2 + (1 + turn) * count)
        split_rows(cuts, held[where], loads[where], masks.at[turn], m_high, m_low)
        if turn == 0:
            loads[0].wait()
            loads[1].wait()
            begin(loads[2 + count :])
        amplitudes(
            scalars[2 * turn], scalars[2 * turn + 1], vir_col, vir_row,
            held[:2], (m_high, m_low), amp, (a_high, a_low), (w_high, w_low),
        )
    density, *slices = held[2 + 2 * count :]
    total, *pieces = made
    for load in loads[2 + 2 * count :]:
        load.wait()
    for start in range(0, density.shape[0], TILE):
        cols = slice(start, start + TILE)
        value = density[:, cols]
        for _, _, a_high, a_low, w_high, w_low in panels:
            value += density_tile(cols, (w_high, w_low), (a_high, a_low))
        total[:, cols] = value * scale
    give[0]()
    for at, ((part, first, height), piece) in enumerate(zip(wanted, pieces)):
        rows = slice(first, first + height)
        width = piece.shape[1]
        cols = slice(part * width, (part + 1) * width)
        value = slices[part][rows, :]
        for m_high, m_low, _, _, w_high, w_low in panels:
            value += respond(rows, (w_high, w_low), (m_high, m_low), cols)
        piece[...] = value
        give[1 + at]()


def late(cuts, wanted, scale, scalars, virtual, masks, own, far, twin, density, slices):
    nvir, naux = own[0].shape
    width = slices[0].shape[1]
    outs = [shape(nvir, nvir)] + [shape(height, width) for _, _, height in wanted]
    wide, square = squares(nvir, naux)
    small = [scalars, *virtual, masks]
    kernel = functools.partial(late_kernel, cuts, wanted, scale)
    scratch = [pltpu.VMEM((nvir, nvir), jnp.float32), *wide, *square, *wide, *square]
    big = [*own, *far, *twin, density, *slices]
    outs = call(kernel, "late", outs, small, big, scratch)
    return outs[0], list(outs[1:])


def exchange(value, axis, bit):
    size = lax.axis_size(axis)
    return lax.ppermute(value, axis, [(at, at ^ bit) for at in range(size)])


def after(value, *others):
    return lax.optimization_barrier((value, *others))[0]


def bits(axis):
    size = lax.axis_size(axis)
    return [1 << at for at in range(size.bit_length() - 1)]


def scatter_chip(value):
    half = value.shape[0] // 2
    side = lax.axis_index("col") % 2
    kept = lax.dynamic_slice_in_dim(value, side * half, half, 0)
    sent = lax.dynamic_slice_in_dim(value, (1 - side) * half, half, 0)
    return kept + exchange(sent, "col", 1)


def scatter_plane(value):
    place = lax.axis_index("col") // 2
    chips = lax.axis_size("col") // 2
    count = value.shape[0] // chips
    total = lax.dynamic_slice_in_dim(value, place * count, count, 0)
    for turn in range(1, chips):
        sent = lax.dynamic_slice_in_dim(value, (place ^ turn) * count, count, 0)
        total = total + exchange(sent, "col", 2 * turn)
    return total


def joined(terms, place):
    if len(terms) == 1:
        return terms[0]
    half = len(terms) // 2
    low, high = joined(terms[:half], place), joined(terms[half:], place)
    side = (place // half) % 2
    return jnp.where(side == 0, jnp.concatenate([low, high]), jnp.concatenate([high, low]))


def gather_plane(value):
    col = lax.axis_index("col")
    turns = range(1, lax.axis_size("col") // 2)
    terms = [value] + [exchange(value, "col", 2 * turn) for turn in turns]
    value = joined(terms, col // 2)
    return joined([value, exchange(value, "col", 1)], col)


def cut_list(nvir, row_count):
    return [(part, 0, nvir) for part in range(row_count)]


def on_device(three_index, occ_energy, vir_energy, block_mask, pair_list):
    row = lax.axis_index("row")
    col = lax.axis_index("col")
    row_count = lax.axis_size("row")
    col_count = lax.axis_size("col")
    position = col % NPANEL
    group = col // NPANEL
    groups = col_count // NPANEL
    nvir = three_index.shape[1]
    cuts = cut_list(nvir, row_count)

    own_orbital = col * row_count + row
    panels = [position ^ turn for turn in range(NPANEL)]
    orbitals = jnp.stack([own_orbital] + [at * row_count + row for at in panels])
    kept = block_mask[orbitals].reshape(NPANEL + 1, block_mask.shape[1], row_count, -1)
    kept = kept[:, :, row ^ jnp.arange(row_count), :].reshape(NPANEL + 1, kept.shape[1], -1)
    masks = jnp.repeat(kept.astype(jnp.float32), BLOCK, axis=-1)
    lists = pair_list[row]
    scalars = []
    for turn in range(NPANEL):
        live = jnp.any(lists == panels[turn]).astype(jnp.float32)
        scalars += [occ_energy[own_orbital] + occ_energy[orbitals[1 + turn]], live]
    small = masks[:3], masks[3:], jnp.stack(scalars[:4]), jnp.stack(scalars[4:])
    column = jnp.broadcast_to(vir_energy[:, None], (nvir, LANES))
    virtual = lax.optimization_barrier((column, vir_energy[None, :]))

    own, came, near, far = [], [], [], []

    def receive(at):
        part, first, count = cuts[at]
        rows = lax.dynamic_index_in_dim(three_index, row ^ part, 0, keepdims=False)
        rows = rows[first : first + count]
        if part == row_count - 1:
            rows = after(rows, near[0])
        own.append(exchange(rows, "row", part) if part else rows)

    for at in range(len(cuts)):
        while len(own) < min(at + 1 if at > 1 else row_count - 1, len(cuts)):
            receive(len(own))
        rows = own[at]
        if at:
            rows = after(rows, came[-1])
        reach = 1
        while reach < groups:
            span = min(reach, groups - reach) * NPANEL
            links = [(one, one + reach * NPANEL) for one in range(span)]
            got = lax.ppermute(rows, "col", links)
            rows = jnp.where((group >= reach) & (group < 2 * reach), got, rows)
            reach *= 2
        came.append(got)
        near.append(rows)
        sent = after(rows, far[-1]) if at else after(rows, *small, *virtual)
        far.append(exchange(sent, "col", 2))

    near_twin = [exchange(piece, "col", 1) for piece in near]
    halved, density, slices = early(
        cuts, small[2], virtual, small[0], own, near, near_twin
    )
    far_twin = [exchange(piece, "col", 1) for piece in far[:-1]]
    far_twin.append(exchange(after(far[-1], density), "col", 1))

    middle, edge, most = row_count // 2, row_count - 1, nvir // 4 * 3
    wanted = [(middle, 0, most), (middle, most, nvir - most), (edge, 0, nvir)]
    wanted += [(at, 0, nvir) for at in range(edge) if at != middle]
    scale = 1.0 / (row_count * col_count)
    total, pieces = late(
        cuts, wanted, scale, small[3], virtual, small[1], halved, far, far_twin,
        density, slices,
    )

    def leave(at, *others):
        return exchange(after(pieces[at], *others), "row", wanted[at][0])

    ends = [leave(0)]
    total = scatter_plane(scatter_chip(total))
    ends.append(leave(1, total))
    total = after(total, ends[0])
    for bit in bits("row")[:-1]:
        total = total + exchange(total, "row", bit)
    total = after(total, ends[1])
    ends += [leave(2, total), pieces[3]]
    ends += [leave(at, total) for at in range(4, len(wanted))]
    total = total + exchange(total, "row", bits("row")[-1])
    total = gather_plane(total)

    returned = jnp.zeros_like(three_index)
    for (part, first, _), piece in zip(wanted, ends):
        returned = lax.dynamic_update_slice(returned, piece[None], (row ^ part, first, 0))
    return returned, total


def solution(mesh):
    placed = (P("col", None, "row"), P(), P(), P(), P("col", None))
    return jax.shard_map(
        on_device,
        mesh=mesh,
        in_specs=placed,
        out_specs=(P("col", None, "row"), P()),
        check_vma=False,
    )
```
